128 devices in a mesh: dp: 32 (over x, z, core), rep: 4 (over y).
Axes of the slice: x: 4, y: 4, z: 4, core: 2. Of those that a mesh axis runs over, the one named last changes fastest.
Arguments:
- page_pool: bfloat16 [14336, 64, 576], P(('rep', 'dp')), parts along dimension 0, may hold values from -12 to 12
- move_source: int32 [3072, 1], P('rep'), parts along dimension 0, may hold values from 0 to 31; in each aligned block of 24 rows (0 to 23, 24 to 47, ...) at most 2 rows name the same one
- move_page: int32 [3072], P('rep'), parts along dimension 0, may hold values from 0 to 111
- move_slot: int32 [3072], P('rep'), parts along dimension 0, may hold values from 0 to 111, as said below
- row_count: int32 [128], P(('rep', 'dp')), parts along dimension 0, may hold values from 1 to 16, as said below
- lengths: int32 [2048], P(('rep', 'dp')), parts along dimension 0, may hold values from 1 to 2048, as said below
- page_table: int32 [2048, 32], P(('rep', 'dp')), parts along dimension 0, may hold values from 0 to 111
- queries: bfloat16 [2048, 64, 576], P(('rep', 'dp')), parts along dimension 0, may hold values from -32 to 32
- value_up: bfloat16 [64, 512, 128], P('dp'), may hold values from -0.25 to 0.25
- out_proj: bfloat16 [8192, 7168], P('dp'), may hold values from -0.375 to 0.375
- residual: bfloat16 [2048, 7168], P(('rep', 'dp')), parts along dimension 0, may hold values from -6 to 6
- norm_gain: float32 [7168], replicated, may hold values from 0.1 to 1.9
- gate_proj: bfloat16 [7168, 9216], P(None, 'dp'), may hold values from -0.0625 to 0.0625
- up_proj: bfloat16 [7168, 9216], P(None, 'dp'), may hold values from -0.0625 to 0.0625
- down_proj: bfloat16 [9216, 7168], P('dp'), may hold values from -0.0625 to 0.0625
Outputs:
- layer_out: bfloat16 [2048, 7168], P(('rep', 'dp')), parts along dimension 0
The draws below stay inside these ranges and needn't reach their ends.
There are 4 independent parts, one for each index of `rep`. The reference program is written for one: setup_inputs(seed, part) draws one part's arguments, and reference() takes and returns one part's arrays. A program takes and returns all parts, laid end to end along the dimension named above; an argument that names none is the same for every part. Nothing has to cross between parts.
Inputs may be any that keep to these rules, and one draw needn't show every extreme that they name: `move_source`: within the 24 moves of one destination rank, no source rank appears more than 2 times, and some source appears exactly 2 times. `move_slot`: the 24 slots of one destination rank are distinct. `row_count`: some rank has exactly 16 live rows. `lengths`: some row has exactly 2048 tokens.
All inputs are finite; a program needn't handle non-finite values.
Results may differ from the reference program's by a relative error of at most 0.02.
Values may be sent and summed in bfloat16 or wider, within the bound.
A program may use at most 128 MiB of HBM per device.

```python
import math
import jax
import jax.numpy as jnp
import numpy as np
from jax import lax

D = 7168
FF = 9216
HEADS = 64
LATENT = 512
ROPE = 64
VDIM = 128
PAGE = 64
POOL = 112
MAXP = 32
ROWS_MAX = 16
MOVES = 24
CAP = 2
ROWS = 512
N_DP = 32


def draw_page_pool(key, part):
    key = jax.random.fold_in(key, 1)
    shape = (N_DP * POOL, PAGE, LATENT + ROPE)
    values = jax.random.normal(key, shape, jnp.float32)
    return jnp.clip(values, -12.0, 12.0).astype(jnp.bfloat16)


def draw_queries(key, part):
    key = jax.random.fold_in(key, 2)
    shape = (N_DP * ROWS_MAX, HEADS, LATENT + ROPE)
    values = 0.5 * jax.random.normal(key, shape, jnp.float32)
    return jnp.clip(values, -32.0, 32.0).astype(jnp.bfloat16)


def draw_move_slot(key, part):
    key = jax.random.fold_in(key, 3)
    row_keys = jax.random.split(key, N_DP)
    slots = jax.vmap(lambda row_key: jax.random.permutation(row_key, POOL)[:MOVES])(row_keys)
    return slots.reshape(-1).astype(jnp.int32)


def draw_row_count(key, part):
    key = jax.random.fold_in(key, 4)
    counts = jax.random.randint(key, (N_DP,), 1, ROWS_MAX + 1)
    fullest = jax.random.randint(jax.random.fold_in(key, 1), (), 0, N_DP)
    return jnp.where(jnp.arange(N_DP) == fullest, ROWS_MAX, counts).astype(jnp.int32)


def draw_lengths(key, part):
    key = jax.random.fold_in(key, 6)
    values = jax.random.randint(key, (N_DP * ROWS_MAX,), 1, MAXP * PAGE + 1)
    longest = jax.random.randint(jax.random.fold_in(key, 1), (), 0, N_DP * ROWS_MAX)
    return jnp.where(jnp.arange(N_DP * ROWS_MAX) == longest, MAXP * PAGE, values).astype(jnp.int32)


def touch_ends(array, stream_key, low, largest):
    index_at = [jax.random.randint(jax.random.fold_in(stream_key, axis), (), 0, length) for axis, length in enumerate(array.shape)]
    widest = array.shape.index(max(array.shape))
    next_to = index_at[:widest] + [(index_at[widest] + 1) % array.shape[widest]] + index_at[widest + 1:]
    return array.at[tuple(index_at)].set(low).at[tuple(next_to)].set(largest)


def shard_levels(rng, extent, shards, least, high):
    factor_of = 1.0
    for axis_at, parts in shards:
        heights = jax.random.uniform(jax.random.fold_in(jax.random.fold_in(rng, 6), axis_at), (parts,), jnp.float32, least / len(shards), high / len(shards))
        factor_of = factor_of * jnp.repeat(jnp.exp(heights), extent[axis_at] // parts).reshape((-1,) + (1,) * (len(extent) - 1 - axis_at))
    return factor_of


def shared_out(own_key, own, number, rows, number_of, top, limit, lean):
    sequence = jax.random.permutation(own_key, number_of)
    heavy_load, common = portions_of(number_of, rows * top, limit, lean, True), portions_of(number_of, rows * top, limit, lean, False)
    places = jnp.arange(number_of)

    def named(tallies, offset_by):
        used = int((tallies > 0).sum())
        fixed = max(1, used // 4)
        passed = fixed + (places - fixed + offset_by * (used - fixed)) % max(1, number_of - fixed)
        return jnp.zeros((number_of,), jnp.int32).at[sequence[jnp.where(places < fixed, places, passed)]].set(jnp.asarray(tallies, jnp.int32))

    tallies = jnp.where(number % 4 == 0, named(heavy_load, number // 4), named(common, number - number // 4 - 1))
    mixed = jax.random.permutation(jax.random.fold_in(own, 3), number_of)
    source_of, sink = mixed[0:number_of // 2 * 2:2], mixed[1:number_of // 2 * 2:2]
    margin = jnp.minimum(tallies[source_of] - 1, limit - tallies[sink]) // 2
    margin = jnp.where((source_of == sequence[0]) | (sink == sequence[0]) | (tallies[sink] == 0), 0, jnp.maximum(margin, 0))
    passed = jax.random.randint(jax.random.fold_in(own, 4), (number_of // 2,), 0, 1 << 20) % (margin + 1)
    tallies = tallies.at[source_of].add(-passed).at[sink].add(passed)
    labels = jnp.searchsorted(jnp.cumsum(tallies), jnp.arange(rows * top), side="right").astype(jnp.int32)
    listing = labels.reshape(top, rows).T
    listing = listing[jax.random.permutation(jax.random.fold_in(own, 1), rows)]
    offset_by = jax.random.randint(jax.random.fold_in(own, 2), (rows, 1), 0, top)
    return jnp.take_along_axis(listing, (jnp.arange(top)[None, :] + offset_by) % top, axis=1)


def portions_of(count, total, most, slope, full):
    weights = [(1 << 20) // math.isqrt(grade ** slope) + 1 for grade in range(1, count + 1)]
    largest = most if full else min(most, max(-(-total // count), total * weights[0] // sum(weights)))
    least = 1 if total - largest >= count - 1 else 0
    holding, rest = [largest] + [least] * (count - 1), total - largest - least * (count - 1)
    while rest > 0:
        movable = [i for i in range(1, count) if holding[i] < largest] or [i for i in range(1, count) if holding[i] < most]
        pool, budget = sum([weights[i] for i in movable]), rest
        for i in movable:
            addition = min(most - holding[i], max(1, budget * weights[i] // pool), rest)
            holding[i] = holding[i] + addition
            rest = rest - addition
    return np.array(holding)


def centred(own_key, shape, spread, reach, cuts=(), dtype=jnp.bfloat16):
    gain = shard_levels(own_key, shape, cuts, -0.22, 0.18) if cuts else 1.0
    values = jax.random.normal(own_key, shape, jnp.float32) * spread * gain
    return jnp.minimum(jnp.maximum(values, -reach), reach).astype(dtype)


def setup_inputs(seed: int = 0, part: int = 0) -> dict:
    splits = jax.random.split(jax.random.key(seed), 16)
    own_keys = jax.random.split(jax.random.fold_in(splits[15], part), 16)
    page_pool = draw_page_pool(jax.random.fold_in(jax.random.fold_in(splits[15], part), 71), part)
    move_source_keys = jax.random.split(jax.random.fold_in(own_keys[1], 1), (N_DP * MOVES) // MOVES)
    move_source_turns = jax.random.permutation(jax.random.fold_in(own_keys[1], 3), (N_DP * MOVES) // MOVES)
    move_source = jax.vmap(lambda own, number: shared_out(jax.random.fold_in(own_keys[1], 2), own, number, MOVES, N_DP, 1, CAP, 2))(move_source_keys, move_source_turns).reshape((N_DP * MOVES, 1))
    move_page = touch_ends(jax.random.randint(own_keys[2], (N_DP * MOVES,), 0, POOL), jax.random.fold_in(own_keys[2], 1), 0, POOL - 1).astype(jnp.int32)
    move_slot = draw_move_slot(jax.random.fold_in(jax.random.fold_in(splits[15], part), 71), part)
    row_count = draw_row_count(jax.random.fold_in(jax.random.fold_in(splits[15], part), 71), part)
    lengths = draw_lengths(jax.random.fold_in(jax.random.fold_in(splits[15], part), 71), part)
    page_table = touch_ends(jax.random.randint(own_keys[6], (ROWS, MAXP), 0, POOL), jax.random.fold_in(own_keys[6], 1), 0, POOL - 1).astype(jnp.int32)
    queries = draw_queries(jax.random.fold_in(jax.random.fold_in(splits[15], part), 71), part)
    value_up = centred(splits[8], (HEADS, LATENT, VDIM), LATENT ** -0.5, 0.25, ((0, 32),))
    out_proj = centred(splits[9], (HEADS * VDIM, D), (HEADS * VDIM // 32) ** -0.5, 0.375, ((0, 32),))
    residual = centred(own_keys[10], (ROWS, D), 1.0, 6.0, ((0, 32),))
    norm_gain = jnp.clip(1.0 + 0.18 * jax.random.normal(splits[11], (D,), jnp.float32), 0.1, 1.9)
    gate_proj = centred(splits[12], (D, FF), D ** -0.5, 0.0625, ((1, 32),))
    up_proj = centred(splits[13], (D, FF), D ** -0.5, 0.0625, ((1, 32),))
    down_proj = centred(splits[14], (FF, D), FF ** -0.5, 0.0625, ((0, 32),))
    return dict(page_pool=page_pool, move_source=move_source, move_page=move_page, move_slot=move_slot, row_count=row_count, lengths=lengths, page_table=page_table, queries=queries, value_up=value_up, out_proj=out_proj, residual=residual, norm_gain=norm_gain, gate_proj=gate_proj, up_proj=up_proj, down_proj=down_proj)


SOFTMAX_SCALE = 192 ** (-0.5)

def rms_scale(values, gain_row):
    factor = lax.rsqrt(lax.optimization_barrier(jnp.mean(values * values, axis=-1, keepdims=True)) + 1e-06)
    return (values * factor * gain_row).astype(jnp.bfloat16)

def attend_rank(cache_pages, tables, row_lens, queries, row_limit):

    def one_row(inputs):
        table_row, row_len, query_row = inputs
        tokens = cache_pages[table_row].reshape(-1, cache_pages.shape[2])
        scores = jnp.einsum('hk,tk->ht', query_row.astype(jnp.float32), tokens.astype(jnp.float32)) * SOFTMAX_SCALE
        live_mask = jnp.arange(tokens.shape[0]) < row_len
        scores = jnp.where(live_mask[None, :], scores, -jnp.inf)
        top_score = lax.optimization_barrier(jnp.max(scores, axis=1, keepdims=True))
        exponent = jnp.exp(scores - top_score)
        weights = (exponent / lax.optimization_barrier(jnp.sum(exponent, axis=1, keepdims=True))).astype(jnp.bfloat16)
        latent_part = tokens[:, :LATENT].astype(jnp.float32)
        return jnp.einsum('ht,tl->hl', weights.astype(jnp.float32), latent_part).astype(jnp.bfloat16)
    outputs = lax.map(one_row, (tables, row_lens, queries))
    valid_rows = jnp.arange(tables.shape[0]) < row_limit
    return jnp.where(valid_rows[:, None, None], outputs, jnp.zeros_like(outputs))

def reference(page_pool, move_source, move_page, move_slot, row_count, lengths, page_table, queries, value_up, out_proj, residual, norm_gain, gate_proj, up_proj, down_proj):
    blocks = page_pool.reshape(N_DP, POOL, PAGE, LATENT + ROPE)
    sources = move_source.reshape(N_DP, MOVES).astype(jnp.int32)
    page_ids = move_page.reshape(N_DP, MOVES).astype(jnp.int32)
    slot_ids = move_slot.reshape(N_DP, MOVES).astype(jnp.int32)
    carried = blocks[sources, page_ids]
    moved_pool = jax.vmap(lambda pages_block, slot_list, fresh_pages: pages_block.at[slot_list].set(fresh_pages))(blocks, slot_ids, carried)

    def per_rank(packed):
        return attend_rank(*packed)
    latent_out = lax.map(per_rank, (moved_pool, page_table.reshape(N_DP, ROWS_MAX, MAXP), lengths.reshape(N_DP, ROWS_MAX), queries.reshape(N_DP, ROWS_MAX, HEADS, LATENT + ROPE), row_count))
    latent_out = latent_out.reshape(N_DP * ROWS_MAX, HEADS, LATENT)
    head_out = jnp.einsum('rhl,hlv->rhv', latent_out.astype(jnp.float32), value_up.astype(jnp.float32)).astype(jnp.bfloat16)
    head_out = head_out.reshape(N_DP * ROWS_MAX, HEADS * VDIM)
    middle = residual.astype(jnp.float32) + jnp.dot(head_out, out_proj, preferred_element_type=jnp.float32)
    normed = rms_scale(middle, norm_gain)
    gate_part = jnp.dot(normed, gate_proj, preferred_element_type=jnp.float32)
    up_part = jnp.dot(normed, up_proj, preferred_element_type=jnp.float32)
    hidden = (jax.nn.silu(gate_part) * up_part).astype(jnp.bfloat16)
    return (middle + jnp.dot(hidden, down_proj, preferred_element_type=jnp.float32)).astype(jnp.bfloat16)
```

```python
import functools

import jax
import jax.numpy as jnp
from jax import lax
from jax.experimental import pallas as pl
from jax.experimental.pallas import tpu as pltpu
from jax.sharding import PartitionSpec as P

LATENT = 512
SOFTMAX_SCALE = 192 ** (-0.5)
LOW = -1e30
MESH = pl.DeviceIdType.MESH
F32 = jnp.float32
BF16 = jnp.bfloat16
VMEM_LIMIT = 60 * 2**20
NX = 4
NZ = 4


def vspec():
    return pl.BlockSpec(memory_space=pltpu.VMEM)


def sspec():
    return pl.BlockSpec(memory_space=pltpu.SMEM)


def aspec():
    return pl.BlockSpec(memory_space=pl.ANY)


def pack_kernel(ids_ref, pool_ref, out_ref, sem):
    count = out_ref.shape[0]

    def start(i, carry):
        pltpu.make_async_copy(pool_ref.at[ids_ref[i]], out_ref.at[i], sem).start()
        return carry

    lax.fori_loop(0, count, start, 0)
    pltpu.make_async_copy(out_ref, out_ref, sem).wait()


def pack_pages(ids, pool):
    return pl.pallas_call(
        pack_kernel,
        out_shape=jax.ShapeDtypeStruct((ids.shape[0],) + pool.shape[1:], pool.dtype),
        in_specs=[sspec(), aspec()],
        out_specs=aspec(),
        scratch_shapes=[pltpu.SemaphoreType.DMA],
        name="pack_pages",
    )(ids, pool)


def flash_step(q, pages_ref, entries, carry):
    top, total, acc = carry
    group = len(entries)
    k = jnp.concatenate([pages_ref[e >> 7] for e in entries], axis=0)
    s = lax.dot_general(q, k, (((1,), (1,)), ((), ())), preferred_element_type=F32) * SOFTMAX_SCALE
    col = lax.broadcasted_iota(jnp.int32, (1, 64 * group), 1)
    limit = jnp.zeros((1, 64 * group), jnp.int32)
    for g, e in enumerate(entries):
        limit = jnp.where((col >> 6) == g, e & 127, limit)
    s = jnp.where((col & 63) < limit, s, LOW)
    new_top = jnp.maximum(top, jnp.max(s, axis=1, keepdims=True))
    shrink = jnp.exp(top - new_top)
    p = jnp.exp(s - new_top)
    total = total * shrink + jnp.sum(p, axis=1, keepdims=True)
    acc = acc * shrink + jnp.dot(p.astype(BF16), k[:, :LATENT], preferred_element_type=F32)
    return new_top, total, acc


GROUP_A = 8
GROUP_B = 4
LIST = 40


def local_kernel(table, lens, rc, slots, q_ref, pool_ref, acc_ref, top_ref, total_ref, list_ref, count_ref, slotmap, list_a):
    rows, heads = q_ref.shape[0], q_ref.shape[1]

    def clear(i, carry):
        slotmap[i] = -1
        return carry

    lax.fori_loop(0, pool_ref.shape[0], clear, 0)

    def mark(i, carry):
        slotmap[slots[i]] = i
        return carry

    lax.fori_loop(0, slots.shape[0], mark, 0)

    def row(r, carry):
        length = lens[r]
        pages = jnp.where(r < rc[0], (length + 63) // 64, 0)

        def place(p, c):
            a, b = c
            slot = table[r, p]
            valid = jnp.minimum(length - 64 * p, 64)
            moved = slotmap[slot]
            list_a[a] = slot * 128 + valid
            list_ref[r * LIST + b] = moved * 128 + valid
            is_moved = (moved >= 0).astype(jnp.int32)
            return a + 1 - is_moved, b + is_moved

        a, b = lax.fori_loop(0, pages, place, (0, 0))
        for g in range(GROUP_A):
            list_a[a + g] = 0
        for g in range(GROUP_B):
            list_ref[r * LIST + b + g] = 0
        count_ref[r] = b
        q = q_ref[r]

        def step(i, c):
            return flash_step(q, pool_ref, [list_a[i * GROUP_A + g] for g in range(GROUP_A)], c)

        init = (
            jnp.full((heads, 1), LOW, F32),
            jnp.zeros((heads, 1), F32),
            jnp.zeros((heads, LATENT), F32),
        )
        top, total, acc = lax.fori_loop(0, (a + GROUP_A - 1) // GROUP_A, step, init)
        acc_ref[r] = acc
        top_ref[r] = jnp.broadcast_to(top, (heads, 128))
        total_ref[r] = jnp.broadcast_to(total, (heads, 128))
        return carry

    lax.fori_loop(0, rows, row, 0)


def attend_local(table, lens, rc, slots, queries, pool):
    rows, heads, _ = queries.shape
    return pl.pallas_call(
        local_kernel,
        out_shape=(
            jax.ShapeDtypeStruct((rows, heads, LATENT), F32),
            jax.ShapeDtypeStruct((rows, heads, 128), F32),
            jax.ShapeDtypeStruct((rows, heads, 128), F32),
            jax.ShapeDtypeStruct((rows * LIST,), jnp.int32),
            jax.ShapeDtypeStruct((rows,), jnp.int32),
        ),
        in_specs=[sspec(), sspec(), sspec(), sspec(), vspec(), vspec()],
        out_specs=(vspec(), vspec(), vspec(), sspec(), sspec()),
        scratch_shapes=[pltpu.SMEM((pool.shape[0],), jnp.int32), pltpu.SMEM((LIST + 8,), jnp.int32)],
        compiler_params=pltpu.CompilerParams(vmem_limit_bytes=40 * 2**20),
        cost_estimate=pl.CostEstimate(flops=20_000_000_000, bytes_accessed=14_000_000, transcendentals=2_000_000),
        name="attend_local",
    )(table, lens, rc, slots, queries, pool)


def moved_kernel(list_ref, count_ref, index_ref, q_ref, acc_ref, top_ref, total_ref, in_ref, out_ref, pages, sem):
    rows = q_ref.shape[0]
    count = pages.shape[0]

    def start(i, carry):
        pltpu.make_async_copy(in_ref.at[index_ref[i]], pages.at[i], sem).start()
        return carry

    lax.fori_loop(0, count, start, 0)
    pltpu.make_async_copy(pages, pages, sem).wait()

    def row(r, carry):
        q = q_ref[r]

        def step(i, c):
            return flash_step(q, pages, [list_ref[r * LIST + i * GROUP_B + g] for g in range(GROUP_B)], c)

        init = (top_ref[r][:, :1], total_ref[r][:, :1], acc_ref[r])
        _, total, acc = lax.fori_loop(0, (count_ref[r] + GROUP_B - 1) // GROUP_B, step, init)
        total = jnp.where(total == 0.0, 1.0, total)
        out_ref[r] = (acc / total).astype(BF16)
        return carry

    lax.fori_loop(0, rows, row, 0)


def attend_moved(list_b, count_b, index, queries, acc, top, total, incoming):
    rows, heads, width = queries.shape
    return pl.pallas_call(
        moved_kernel,
        out_shape=jax.ShapeDtypeStruct((rows, heads, LATENT), BF16),
        in_specs=[sspec(), sspec(), sspec(), vspec(), vspec(), vspec(), vspec(), aspec()],
        out_specs=vspec(),
        scratch_shapes=[pltpu.VMEM((index.shape[0], incoming.shape[1], width), BF16), pltpu.SemaphoreType.DMA],
        compiler_params=pltpu.CompilerParams(vmem_limit_bytes=40 * 2**20),
        name="attend_moved",
    )(list_b, count_b, index, queries, acc, top, total, incoming)


SUBS = 2


def tail_kernel(
    lat, vu, wo, res, gain, gate, up, down, out_ref,
    rl, vus, wos, gus, ds, ho, part, nrm, mid, acc, hid,
    b1, b2, c1, c2, e1, e2, f1, f2,
    bar_sems, lat_ss, lat_rs, w_ls, w_ss, w_rs, rs_ss, rs_rs, ag_ss, ag_rs,
):
    me = lax.axis_index("dp")
    core = lax.rem(me, 2)
    chip = me // 2
    x = chip // NZ
    z = lax.rem(chip, NZ)
    cols_all = part.shape[3]
    half = cols_all // 2
    ff = gate.shape[0]

    def device(dx, dz):
        return {"dp": (lax.rem(x + dx + NX, NX) * NZ + lax.rem(z + dz + NZ, NZ)) * 2 + core}

    sibling = {"dp": me + 1 - 2 * core}

    barrier = pltpu.get_barrier_semaphore()
    peers = [(a, b) for a in range(NX) for b in range(NZ) if (a, b) != (0, 0)]
    for a, b in peers:
        pl.semaphore_signal(barrier, inc=1, device_id=device(a, b), device_id_type=MESH)
    pl.semaphore_signal(barrier, inc=1, device_id=sibling, device_id_type=MESH)
    pl.semaphore_wait(barrier, len(peers) + 1)

    sent = []

    def send(src, dst, ss, rs, to):
        copy = pltpu.make_async_remote_copy(
            src_ref=src, dst_ref=dst, send_sem=ss, recv_sem=rs, device_id=to, device_id_type=MESH
        )
        copy.start()
        sent.append(copy)
        return copy

    lat_copies = []
    for k, (a, b) in enumerate(peers):
        to_chip = lax.rem(x + a, NX) * NZ + lax.rem(z + b, NZ)
        lat_copies.append(send(lat.at[to_chip], rl.at[chip], lat_ss.at[k], lat_rs.at[k], device(a, b)))
    own_lat = pltpu.make_async_copy(lat.at[chip], rl.at[chip], bar_sems.at[0])
    own_lat.start()

    row0 = pl.multiple_of(core * ff, 16)
    row1 = pl.multiple_of(640 + core * ff, 16)
    places = [
        (vu, vus.at[core]),
        (wo, wos.at[core]),
        (gate, gus.at[pl.ds(row0, ff), :]),
        (up, gus.at[pl.ds(row1, ff), :]),
        (down, ds.at[pl.ds(row0, ff), :]),
    ]
    w_local, w_remote = [], []
    for k, (src, dst) in enumerate(places):
        copy = pltpu.make_async_copy(src, dst, w_ls.at[k])
        copy.start()
        w_local.append(copy)
        w_remote.append(send(src, dst, w_ss.at[k], w_rs.at[k], sibling))
    gus[pl.ds(2 * ff, 640 - 2 * ff), :] = jnp.zeros((640 - 2 * ff, cols_all), BF16)
    gus[pl.ds(640 + 2 * ff, 640 - 2 * ff), :] = jnp.zeros((640 - 2 * ff, cols_all), BF16)

    def weights_ready(*ks):
        for k in ks:
            w_local[k].wait()
            w_remote[k].wait_recv()

    own_lat.wait()
    for copy in lat_copies:
        copy.wait_recv()
    weights_ready(0)
    for h in range(4):
        l = rl[:, h * 16 : (h + 1) * 16, :].reshape(256, LATENT)
        ho[:, h * 128 : (h + 1) * 128] = jnp.dot(l, vus[h // 2, h % 2], preferred_element_type=F32).astype(BF16)

    width = half // SUBS
    wing = width // 2

    def reduce_scatter(turn, fill, bufs, finish):
        r1, r2, t1, t2 = bufs

        def chunk(h, phase, i, base, size):
            cs = pl.ds(base, size)
            xi, zi = lax.rem(x + i + NX, NX), lax.rem(z + i + NZ, NZ)
            along_x = (h == 0) == (phase == 0)
            if phase == 0:
                return part.at[xi, :, :, cs] if along_x else part.at[:, zi, :, cs]
            return part.at[xi, z, :, cs] if along_x else part.at[x, zi, :, cs]

        def to(h, phase, i):
            return device(i, 0) if (h == 0) == (phase == 0) else device(0, i)

        def sems(h, s, phase, k):
            at = (((turn * 2 + h) * SUBS + s) * 2 + phase) * 6 + k
            return rs_ss.at[at], rs_rs.at[at]

        def bufs_of(h, s, phase):
            first, second = (r1, r2) if phase == 0 else (t1, t2)
            return first.at[h, s], second.at[h, s]

        state = {}

        def start(h, s, phase):
            base = h * half + s * width
            first, second = bufs_of(h, s, phase)
            lo, hi = base, base + wing
            state[h, s, phase] = [
                send(chunk(h, phase, 2, lo, wing), first.at[0], *sems(h, s, phase, 0), to(h, phase, 1)),
                send(chunk(h, phase, 2, hi, wing), first.at[1], *sems(h, s, phase, 1), to(h, phase, -1)),
                send(chunk(h, phase, 1, hi, wing), second.at[0, ..., pl.ds(wing, wing)], *sems(h, s, phase, 2), to(h, phase, 1)),
                send(chunk(h, phase, -1, lo, wing), second.at[1, ..., pl.ds(0, wing)], *sems(h, s, phase, 3), to(h, phase, -1)),
            ]

        def middle(h, s, phase):
            base = h * half + s * width
            first, second = bufs_of(h, s, phase)
            copies = state[h, s, phase]
            for side, (i, at) in enumerate(((1, 0), (-1, wing))):
                copies[side].wait_recv()
                mine = chunk(h, phase, i, base + at, wing)
                mine[...] = (mine[...].astype(F32) + first[side].astype(F32)).astype(BF16)
                copies.append(
                    send(mine, second.at[side, ..., pl.ds(at, wing)], *sems(h, s, phase, 4 + side), to(h, phase, i))
                )

        def total(h, s, phase):
            base = h * half + s * width
            _, second = bufs_of(h, s, phase)
            for copy in state[h, s, phase][2:]:
                copy.wait_recv()
            mine = chunk(h, phase, 0, base, width)
            value = mine[...].astype(F32) + second[0].astype(F32) + second[1].astype(F32)
            if phase == 0:
                mine[...] = value.astype(BF16)
            else:
                finish(base, width, value)

        order = [(h, s) for s in range(SUBS) for h in range(2)]
        for h, s in order:
            fill(h * half + s * width, width)
            start(h, s, 0)
        for h, s in order:
            middle(h, s, 0)
        for h, s in order:
            total(h, s, 0)
            start(h, s, 1)
        for h, s in order:
            middle(h, s, 1)
        for h, s in order:
            total(h, s, 1)

    weights_ready(1)

    def fill_out(base, size):
        cs = pl.ds(base, size)
        v = jnp.dot(ho[:, :256], wos[0, :, cs], preferred_element_type=F32)
        v = v + jnp.dot(ho[:, 256:], wos[1, :, cs], preferred_element_type=F32)
        part[:, :, :, cs] = v.astype(BF16).reshape(NX, NZ, 16, size)

    squares = []

    def finish_out(base, size, value):
        cs = pl.ds(base, size)
        m = res[:, cs].astype(F32) + value
        mid[:, cs] = m
        squares.append(jnp.sum(m * m, axis=1, keepdims=True))

    reduce_scatter(0, fill_out, (b1, b2, c1, c2), finish_out)
    factor = lax.rsqrt(sum(squares) / cols_all + 1e-06)
    nrm[x, z] = (mid[...] * factor * gain[...]).astype(BF16)
    while sent:
        sent.pop().wait_send()

    quarter = half // 2

    def block(h, i, j, lo, size):
        cs = pl.ds(h * half + lo, size)
        dx, dz = (j, i) if h == 0 else (i, j)
        return nrm.at[lax.rem(x + dx + NX, NX), lax.rem(z + dz + NZ, NZ), :, cs]

    def ag_sems(h, k):
        return ag_ss.at[h * 20 + k], ag_rs.at[h * 20 + k]

    def along(h, first, i):
        return device(0, i) if (h == 0) == first else device(i, 0)

    def pass_on(ref, h, k, first, i):
        return send(ref, ref, *ag_sems(h, k), along(h, first, i))

    one, two = {}, {}
    for h in range(2):
        ref = block(h, 0, 0, 0, half)
        one[h] = [pass_on(ref, h, 0, True, 1), pass_on(ref, h, 1, True, -1)]

    def spread(h, n, i):
        ref = block(h, i, 0, 0, half)
        two[h, n] = [pass_on(ref, h, 4 + 4 * n, False, 1), pass_on(ref, h, 5 + 4 * n, False, -1)]

    def forward(h, n, i):
        two[h, n][0].wait_recv()
        two[h, n].append(pass_on(block(h, i, -1, 0, quarter), h, 6 + 4 * n, False, 1))
        two[h, n][1].wait_recv()
        two[h, n].append(pass_on(block(h, i, 1, quarter, quarter), h, 7 + 4 * n, False, -1))

    for h in range(2):
        spread(h, 0, 0)
    for h in range(2):
        one[h][0].wait_recv()
        one[h].append(pass_on(block(h, -1, 0, 0, quarter), h, 2, True, 1))
        one[h][1].wait_recv()
        one[h].append(pass_on(block(h, 1, 0, quarter, quarter), h, 3, True, -1))
        spread(h, 1, -1)
        spread(h, 2, 1)
    for h in range(2):
        forward(h, 0, 0)
    for h in range(2):
        one[h][2].wait_recv()
        one[h][3].wait_recv()
        spread(h, 3, 2)
    for n, i in ((1, -1), (2, 1), (3, 2)):
        for h in range(2):
            forward(h, n, i)
    for h in range(2):
        for n in range(4):
            two[h, n][2].wait_recv()
            two[h, n][3].wait_recv()

    weights_ready(2, 3)
    depth = cols_all // 4

    def up_step(k, carry):
        cs = pl.ds(pl.multiple_of(k * depth, 128), depth)
        v = lax.dot_general(
            nrm[:, :, :, cs].reshape(256, depth), gus[:, cs], (((1,), (1,)), ((), ())), preferred_element_type=F32
        )

        @pl.when(k == 0)
        def _():
            acc[...] = v

        @pl.when(k > 0)
        def _():
            acc[...] += v

        return carry

    lax.fori_loop(0, 4, up_step, 0)
    g = acc[:, :640]
    hid[...] = (g / (1.0 + jnp.exp(-g)) * acc[:, 640:]).astype(BF16)
    weights_ready(4)

    def fill_down(base, size):
        cs = pl.ds(base, size)
        v = jnp.dot(hid[:, : 2 * ff], ds[:, cs], preferred_element_type=F32)
        part[:, :, :, cs] = v.astype(BF16).reshape(NX, NZ, 16, size)

    def finish_down(base, size, value):
        cs = pl.ds(base, size)
        out_ref[:, cs] = (mid[:, cs] + value).astype(BF16)

    reduce_scatter(1, fill_down, (e1, e2, f1, f2), finish_down)
    while sent:
        sent.pop().wait_send()


def tail(lat, value_up, out_proj, residual, norm_gain, gate_t, up_t, down):
    cols = residual.shape[1]
    ff = gate_t.shape[0]
    width = cols // 2 // SUBS
    rs_bufs = [
        pltpu.VMEM((2, SUBS, 2, 4, 16, width // 2), BF16),
        pltpu.VMEM((2, SUBS, 2, 4, 16, width), BF16),
        pltpu.VMEM((2, SUBS, 2, 16, width // 2), BF16),
        pltpu.VMEM((2, SUBS, 2, 16, width), BF16),
    ]
    n_rs = 2 * 2 * SUBS * 2 * 6
    dma = pltpu.SemaphoreType.DMA
    return pl.pallas_call(
        tail_kernel,
        out_shape=jax.ShapeDtypeStruct(residual.shape, BF16),
        in_specs=[aspec(), aspec(), aspec(), vspec(), vspec(), aspec(), aspec(), aspec()],
        out_specs=vspec(),
        scratch_shapes=[
            pltpu.VMEM((16, 64, LATENT), BF16),
            pltpu.VMEM((2, 2, LATENT, 128), BF16),
            pltpu.VMEM((2, 256, cols), BF16),
            pltpu.VMEM((1280, cols), BF16),
            pltpu.VMEM((2 * ff, cols), BF16),
            pltpu.VMEM((256, 512), BF16),
            pltpu.VMEM((NX, NZ, 16, cols), BF16),
            pltpu.VMEM((NX, NZ, 16, cols), BF16),
            pltpu.VMEM((16, cols), F32),
            pltpu.VMEM((256, 1280), F32),
            pltpu.VMEM((256, 640), BF16),
            *rs_bufs,
            *rs_bufs,
            dma((1,)),
            dma((15,)),
            dma((15,)),
            dma((5,)),
            dma((5,)),
            dma((5,)),
            dma((n_rs,)),
            dma((n_rs,)),
            dma((40,)),
            dma((40,)),
        ],
        compiler_params=pltpu.CompilerParams(collective_id=0, has_side_effects=True, vmem_limit_bytes=VMEM_LIMIT),
        cost_estimate=pl.CostEstimate(flops=12_000_000_000, bytes_accessed=40_000_000, transcendentals=200_000),
        name="tail",
    )(lat, value_up, out_proj, residual, norm_gain.reshape(1, cols), gate_t, up_t, down)


def body(
    page_pool,
    move_source,
    move_page,
    move_slot,
    row_count,
    lengths,
    page_table,
    queries,
    value_up,
    out_proj,
    residual,
    norm_gain,
    gate_proj,
    up_proj,
    down_proj,
):
    rank_count = lax.axis_size("dp")
    own_rank = lax.axis_index("dp")
    move_count = move_page.shape[0] // rank_count
    capacity = 2
    sources = move_source.reshape(rank_count, move_count)
    page_ids = move_page.reshape(rank_count, move_count)
    slot_ids = move_slot.reshape(rank_count, move_count)
    move_order = jnp.arange(move_count)
    earlier = (sources[:, :, None] == sources[:, None, :]) & (
        move_order[None, None, :] < move_order[None, :, None]
    )
    arrival = jnp.sum(earlier.astype(jnp.int32), axis=2)
    chosen = (sources == own_rank)[:, :, None] & (
        arrival[:, :, None] == jnp.arange(capacity)[None, None, :]
    )
    send_ids = jnp.sum(jnp.where(chosen, page_ids[:, :, None], 0), axis=1).reshape(-1)
    page_shape = page_pool.shape[1:]
    outgoing = pack_pages(send_ids, page_pool).reshape((rank_count, capacity) + page_shape)
    incoming = lax.all_to_all(outgoing, "dp", split_axis=0, concat_axis=0, tiled=True)
    own_sources = lax.dynamic_index_in_dim(sources, own_rank, 0, keepdims=False)
    own_arrival = lax.dynamic_index_in_dim(arrival, own_rank, 0, keepdims=False)
    own_slots = lax.dynamic_index_in_dim(slot_ids, own_rank, 0, keepdims=False)
    acc, top, total, list_b, count_b = attend_local(
        page_table, lengths, row_count, own_slots, queries, page_pool
    )
    latent = attend_moved(
        list_b, count_b, own_sources * capacity + own_arrival, queries, acc, top, total,
        incoming.reshape((rank_count * capacity,) + page_shape),
    )
    rows, heads, _ = latent.shape
    lat = latent.reshape(rows, NX * NZ, heads // (NX * NZ), LATENT).transpose(1, 2, 0, 3)
    lat = lat.reshape(NX * NZ, -1, LATENT)
    return tail(lat, value_up, out_proj, residual, norm_gain, gate_proj.T, up_proj.T, down_proj)


def solution(mesh):
    in_specs = (
        P(("rep", "dp"), None, None),
        P("rep", None),
        P("rep"),
        P("rep"),
        P(("rep", "dp")),
        P(("rep", "dp")),
        P(("rep", "dp"), None),
        P(("rep", "dp"), None, None),
        P("dp", None, None),
        P("dp", None),
        P(("rep", "dp"), None),
        P(),
        P(None, "dp"),
        P(None, "dp"),
        P("dp", None),
    )
    out_specs = P(("rep", "dp"), None)
    return jax.shard_map(body, mesh=mesh, in_specs=in_specs, out_specs=out_specs, check_vma=False)
```

```python
import functools

import jax
import jax.numpy as jnp
from jax import lax
from jax.experimental import pallas as pl
from jax.experimental.pallas import tpu as pltpu
from jax.sharding import PartitionSpec as P

LATENT = 512
SOFTMAX_SCALE = 192 ** (-0.5)
LOW = -1e30
MESH = pl.DeviceIdType.MESH
F32 = jnp.float32
BF16 = jnp.bfloat16
VMEM_LIMIT = 60 * 2**20
NX = 4
NZ = 4


def vspec():
    return pl.BlockSpec(memory_space=pltpu.VMEM)


def sspec():
    return pl.BlockSpec(memory_space=pltpu.SMEM)


def aspec():
    return pl.BlockSpec(memory_space=pl.ANY)


def pack_kernel(ids_ref, pool_ref, out_ref):
    def pair(i, carry):
        one, two = pool_ref[ids_ref[2 * i]], pool_ref[ids_ref[2 * i + 1]]
        out_ref[i, :, :LATENT] = one[:, :LATENT]
        out_ref[i, :, LATENT : 2 * LATENT] = two[:, :LATENT]
        out_ref[i, :, 2 * LATENT :] = jnp.concatenate([one[:, LATENT:], two[:, LATENT:]], axis=1)
        return carry

    lax.fori_loop(0, out_ref.shape[0], pair, 0)


def pack_pages(ids, pool):
    _, page, width = pool.shape
    return pl.pallas_call(
        pack_kernel,
        out_shape=jax.ShapeDtypeStruct((ids.shape[0] // 2, page, 2 * width), pool.dtype),
        in_specs=[sspec(), vspec()],
        out_specs=vspec(),
        compiler_params=pltpu.CompilerParams(vmem_limit_bytes=40 * 2**20),
        name="pack_pages",
    )(ids, pool)


def flash_step(q, pages_ref, entries, carry):
    top, total, acc = carry
    group = len(entries)
    k = jnp.concatenate([pages_ref[e >> 7] for e in entries], axis=0)
    s = lax.dot_general(q, k, (((1,), (1,)), ((), ())), preferred_element_type=F32) * SOFTMAX_SCALE
    col = lax.broadcasted_iota(jnp.int32, (1, 64 * group), 1)
    limit = jnp.zeros((1, 64 * group), jnp.int32)
    for g, e in enumerate(entries):
        limit = jnp.where((col >> 6) == g, e & 127, limit)
    s = jnp.where((col & 63) < limit, s, LOW)
    new_top = jnp.maximum(top, jnp.max(s, axis=1, keepdims=True))
    shrink = jnp.exp(top - new_top)
    p = jnp.exp(s - new_top)
    total = total * shrink + jnp.sum(p, axis=1, keepdims=True)
    acc = acc * shrink + jnp.dot(p.astype(BF16), k[:, :LATENT], preferred_element_type=F32)
    return new_top, total, acc


GROUP_A = 8
GROUP_B = 4
LIST = 40


def local_kernel(table, lens, rc, slots, q_ref, pool_ref, acc_ref, top_ref, total_ref, list_ref, count_ref, slotmap, list_a):
    rows, heads = q_ref.shape[0], q_ref.shape[1]

    def clear(i, carry):
        slotmap[i] = -1
        return carry

    lax.fori_loop(0, pool_ref.shape[0], clear, 0)

    def mark(i, carry):
        slotmap[slots[i]] = i
        return carry

    lax.fori_loop(0, slots.shape[0], mark, 0)

    def row(r, carry):
        length = lens[r]
        pages = jnp.where(r < rc[0], (length + 63) // 64, 0)

        def place(p, c):
            a, b = c
            slot = table[r, p]
            valid = jnp.minimum(length - 64 * p, 64)
            moved = slotmap[slot]
            list_a[a] = slot * 128 + valid
            list_ref[r * LIST + b] = moved * 128 + valid
            is_moved = (moved >= 0).astype(jnp.int32)
            return a + 1 - is_moved, b + is_moved

        a, b = lax.fori_loop(0, pages, place, (0, 0))
        for g in range(GROUP_A):
            list_a[a + g] = 0
        for g in range(GROUP_B):
            list_ref[r * LIST + b + g] = 0
        count_ref[r] = b
        q = q_ref[r]

        def step(i, c):
            return flash_step(q, pool_ref, [list_a[i * GROUP_A + g] for g in range(GROUP_A)], c)

        init = (
            jnp.full((heads, 1), LOW, F32),
            jnp.zeros((heads, 1), F32),
            jnp.zeros((heads, LATENT), F32),
        )
        top, total, acc = lax.fori_loop(0, (a + GROUP_A - 1) // GROUP_A, step, init)
        acc_ref[r] = acc
        top_ref[r] = jnp.broadcast_to(top, (heads, 128))
        total_ref[r] = jnp.broadcast_to(total, (heads, 128))
        return carry

    lax.fori_loop(0, rows, row, 0)


def attend_local(table, lens, rc, slots, queries, pool):
    rows, heads, _ = queries.shape
    return pl.pallas_call(
        local_kernel,
        out_shape=(
            jax.ShapeDtypeStruct((rows, heads, LATENT), F32),
            jax.ShapeDtypeStruct((rows, heads, 128), F32),
            jax.ShapeDtypeStruct((rows, heads, 128), F32),
            jax.ShapeDtypeStruct((rows * LIST,), jnp.int32),
            jax.ShapeDtypeStruct((rows,), jnp.int32),
        ),
        in_specs=[sspec(), sspec(), sspec(), sspec(), vspec(), vspec()],
        out_specs=(vspec(), vspec(), vspec(), sspec(), sspec()),
        scratch_shapes=[pltpu.SMEM((pool.shape[0],), jnp.int32), pltpu.SMEM((LIST + 8,), jnp.int32)],
        compiler_params=pltpu.CompilerParams(vmem_limit_bytes=40 * 2**20),
        cost_estimate=pl.CostEstimate(flops=20_000_000_000, bytes_accessed=14_000_000, transcendentals=2_000_000),
        name="attend_local",
    )(table, lens, rc, slots, queries, pool)


def moved_kernel(list_ref, count_ref, index_ref, q_ref, acc_ref, top_ref, total_ref, in_ref, out_ref, pairs, pages, sem):
    rows = q_ref.shape[0]
    count = pages.shape[0]

    def start(i, carry):
        pltpu.make_async_copy(in_ref.at[index_ref[i] >> 1], pairs.at[i], sem).start()
        return carry

    lax.fori_loop(0, count, start, 0)
    pltpu.make_async_copy(pairs, pairs, sem).wait()

    def unpack(i, carry):
        first = (index_ref[i] & 1) == 0
        pages[i, :, :LATENT] = jnp.where(first, pairs[i, :, :LATENT], pairs[i, :, LATENT : 2 * LATENT])
        turned = pairs[i, :, 2 * LATENT :]
        pages[i, :, LATENT:] = jnp.where(first, turned[:, : pages.shape[2] - LATENT], turned[:, pages.shape[2] - LATENT :])
        return carry

    lax.fori_loop(0, count, unpack, 0)

    def row(r, carry):
        q = q_ref[r]

        def step(i, c):
            return flash_step(q, pages, [list_ref[r * LIST + i * GROUP_B + g] for g in range(GROUP_B)], c)

        init = (top_ref[r][:, :1], total_ref[r][:, :1], acc_ref[r])
        _, total, acc = lax.fori_loop(0, (count_ref[r] + GROUP_B - 1) // GROUP_B, step, init)
        total = jnp.where(total == 0.0, 1.0, total)
        out_ref[r] = (acc / total).astype(BF16)
        return carry

    lax.fori_loop(0, rows, row, 0)


def attend_moved(list_b, count_b, index, queries, acc, top, total, incoming):
    rows, heads, width = queries.shape
    return pl.pallas_call(
        moved_kernel,
        out_shape=jax.ShapeDtypeStruct((rows, heads, LATENT), BF16),
        in_specs=[sspec(), sspec(), sspec(), vspec(), vspec(), vspec(), vspec(), aspec()],
        out_specs=vspec(),
        scratch_shapes=[
            pltpu.VMEM((index.shape[0],) + incoming.shape[1:], BF16),
            pltpu.VMEM((index.shape[0], incoming.shape[1], width), BF16),
            pltpu.SemaphoreType.DMA,
        ],
        compiler_params=pltpu.CompilerParams(vmem_limit_bytes=40 * 2**20),
        name="attend_moved",
    )(list_b, count_b, index, queries, acc, top, total, incoming)


SUBS = 2


def tail_kernel(
    lat, vu, wo, res, gain, gate, up, down, out_ref,
    rl, vus, wos, gus, ds, ho, part, nrm, mid, acc, hid,
    b1, b2, c1, c2, e1, e2, f1, f2,
    bar_sems, lat_ss, lat_rs, w_ls, w_ss, w_rs, rs_ss, rs_rs, ag_ss, ag_rs,
):
    me = lax.axis_index("dp")
    core = lax.rem(me, 2)
    chip = me // 2
    x = chip // NZ
    z = lax.rem(chip, NZ)
    cols_all = part.shape[3]
    half = cols_all // 2
    ff = gate.shape[0]

    def device(dx, dz):
        return {"dp": (lax.rem(x + dx + NX, NX) * NZ + lax.rem(z + dz + NZ, NZ)) * 2 + core}

    sibling = {"dp": me + 1 - 2 * core}

    barrier = pltpu.get_barrier_semaphore()
    peers = [(a, b) for a in range(NX) for b in range(NZ) if (a, b) != (0, 0)]
    for a, b in peers:
        pl.semaphore_signal(barrier, inc=1, device_id=device(a, b), device_id_type=MESH)
    pl.semaphore_signal(barrier, inc=1, device_id=sibling, device_id_type=MESH)
    pl.semaphore_wait(barrier, len(peers) + 1)

    sent = []

    def send(src, dst, ss, rs, to):
        copy = pltpu.make_async_remote_copy(
            src_ref=src, dst_ref=dst, send_sem=ss, recv_sem=rs, device_id=to, device_id_type=MESH
        )
        copy.start()
        sent.append(copy)
        return copy

    lat_copies = []
    for k, (a, b) in enumerate(peers):
        to_chip = lax.rem(x + a, NX) * NZ + lax.rem(z + b, NZ)
        lat_copies.append(send(lat.at[to_chip], rl.at[chip], lat_ss.at[k], lat_rs.at[k], device(a, b)))
    own_lat = pltpu.make_async_copy(lat.at[chip], rl.at[chip], bar_sems.at[0])
    own_lat.start()

    row0 = pl.multiple_of(core * ff, 16)
    row1 = pl.multiple_of(640 + core * ff, 16)
    places = [
        (vu, vus.at[core]),
        (wo, wos.at[core]),
        (gate, gus.at[pl.ds(row0, ff), :]),
        (up, gus.at[pl.ds(row1, ff), :]),
        (down, ds.at[pl.ds(row0, ff), :]),
    ]
    w_local, w_remote = [], []
    for k, (src, dst) in enumerate(places):
        copy = pltpu.make_async_copy(src, dst, w_ls.at[k])
        copy.start()
        w_local.append(copy)
        w_remote.append(send(src, dst, w_ss.at[k], w_rs.at[k], sibling))
    gus[pl.ds(2 * ff, 640 - 2 * ff), :] = jnp.zeros((640 - 2 * ff, cols_all), BF16)
    gus[pl.ds(640 + 2 * ff, 640 - 2 * ff), :] = jnp.zeros((640 - 2 * ff, cols_all), BF16)

    def weights_ready(*ks):
        for k in ks:
            w_local[k].wait()
            w_remote[k].wait_recv()

    own_lat.wait()
    for copy in lat_copies:
        copy.wait_recv()
    weights_ready(0)
    for h in range(4):
        l = rl[:, h * 16 : (h + 1) * 16, :].reshape(256, LATENT)
        ho[:, h * 128 : (h + 1) * 128] = jnp.dot(l, vus[h // 2, h % 2], preferred_element_type=F32).astype(BF16)

    width = half // SUBS
    wing = width // 2

    def reduce_scatter(turn, fill, bufs, finish):
        r1, r2, t1, t2 = bufs

        def chunk(h, phase, i, base, size):
            cs = pl.ds(base, size)
            xi, zi = lax.rem(x + i + NX, NX), lax.rem(z + i + NZ, NZ)
            along_x = (h == 0) == (phase == 0)
            if phase == 0:
                return part.at[xi, :, :, cs] if along_x else part.at[:, zi, :, cs]
            return part.at[xi, z, :, cs] if along_x else part.at[x, zi, :, cs]

        def to(h, phase, i):
            return device(i, 0) if (h == 0) == (phase == 0) else device(0, i)

        def sems(h, s, phase, k):
            at = (((turn * 2 + h) * SUBS + s) * 2 + phase) * 6 + k
            return rs_ss.at[at], rs_rs.at[at]

        def bufs_of(h, s, phase):
            first, second = (r1, r2) if phase == 0 else (t1, t2)
            return first.at[h, s], second.at[h, s]

        state = {}

        def start(h, s, phase):
            base = h * half + s * width
            first, second = bufs_of(h, s, phase)
            lo, hi = base, base + wing
            state[h, s, phase] = [
                send(chunk(h, phase, 2, lo, wing), first.at[0], *sems(h, s, phase, 0), to(h, phase, 1)),
                send(chunk(h, phase, 2, hi, wing), first.at[1], *sems(h, s, phase, 1), to(h, phase, -1)),
                send(chunk(h, phase, 1, hi, wing), second.at[0, ..., pl.ds(wing, wing)], *sems(h, s, phase, 2), to(h, phase, 1)),
                send(chunk(h, phase, -1, lo, wing), second.at[1, ..., pl.ds(0, wing)], *sems(h, s, phase, 3), to(h, phase, -1)),
            ]

        def middle(h, s, phase):
            base = h * half + s * width
            first, second = bufs_of(h, s, phase)
            copies = state[h, s, phase]
            for side, (i, at) in enumerate(((1, 0), (-1, wing))):
                copies[side].wait_recv()
                mine = chunk(h, phase, i, base + at, wing)
                mine[...] = (mine[...].astype(F32) + first[side].astype(F32)).astype(BF16)
                copies.append(
                    send(mine, second.at[side, ..., pl.ds(at, wing)], *sems(h, s, phase, 4 + side), to(h, phase, i))
                )

        def total(h, s, phase):
            base = h * half + s * width
            _, second = bufs_of(h, s, phase)
            for copy in state[h, s, phase][2:]:
                copy.wait_recv()
            mine = chunk(h, phase, 0, base, width)
            value = mine[...].astype(F32) + second[0].astype(F32) + second[1].astype(F32)
            if phase == 0:
                mine[...] = value.astype(BF16)
            else:
                finish(base, width, value)

        order = [(h, s) for s in range(SUBS) for h in range(2)]
        for h, s in order:
            fill(h * half + s * width, width)
            start(h, s, 0)
        for h, s in order:
            middle(h, s, 0)
        for h, s in order:
            total(h, s, 0)
            start(h, s, 1)
        for h, s in order:
            middle(h, s, 1)
        for h, s in order:
            total(h, s, 1)

    weights_ready(1)

    def fill_out(base, size):
        cs = pl.ds(base, size)
        v = jnp.dot(ho[:, :256], wos[0, :, cs], preferred_element_type=F32)
        v = v + jnp.dot(ho[:, 256:], wos[1, :, cs], preferred_element_type=F32)
        part[:, :, :, cs] = v.astype(BF16).reshape(NX, NZ, 16, size)

    squares = []

    def finish_out(base, size, value):
        cs = pl.ds(base, size)
        m = res[:, cs].astype(F32) + value
        mid[:, cs] = m
        squares.append(jnp.sum(m * m, axis=1, keepdims=True))

    reduce_scatter(0, fill_out, (b1, b2, c1, c2), finish_out)
    factor = lax.rsqrt(sum(squares) / cols_all + 1e-06)
    nrm[x, z] = (mid[...] * factor * gain[...]).astype(BF16)
    while sent:
        sent.pop().wait_send()

    quarter = half // 2

    def block(h, i, j, lo, size):
        cs = pl.ds(h * half + lo, size)
        dx, dz = (j, i) if h == 0 else (i, j)
        return nrm.at[lax.rem(x + dx + NX, NX), lax.rem(z + dz + NZ, NZ), :, cs]

    def ag_sems(h, k):
        return ag_ss.at[h * 20 + k], ag_rs.at[h * 20 + k]

    def along(h, first, i):
        return device(0, i) if (h == 0) == first else device(i, 0)

    def pass_on(ref, h, k, first, i):
        return send(ref, ref, *ag_sems(h, k), along(h, first, i))

    one, two = {}, {}
    for h in range(2):
        ref = block(h, 0, 0, 0, half)
        one[h] = [pass_on(ref, h, 0, True, 1), pass_on(ref, h, 1, True, -1)]

    def spread(h, n, i):
        ref = block(h, i, 0, 0, half)
        two[h, n] = [pass_on(ref, h, 4 + 4 * n, False, 1), pass_on(ref, h, 5 + 4 * n, False, -1)]

    def forward(h, n, i):
        two[h, n][0].wait_recv()
        two[h, n].append(pass_on(block(h, i, -1, 0, quarter), h, 6 + 4 * n, False, 1))
        two[h, n][1].wait_recv()
        two[h, n].append(pass_on(block(h, i, 1, quarter, quarter), h, 7 + 4 * n, False, -1))

    for h in range(2):
        spread(h, 0, 0)
    for h in range(2):
        one[h][0].wait_recv()
        one[h].append(pass_on(block(h, -1, 0, 0, quarter), h, 2, True, 1))
        one[h][1].wait_recv()
        one[h].append(pass_on(block(h, 1, 0, quarter, quarter), h, 3, True, -1))
        spread(h, 1, -1)
        spread(h, 2, 1)
    for h in range(2):
        forward(h, 0, 0)
    for h in range(2):
        one[h][2].wait_recv()
        one[h][3].wait_recv()
        spread(h, 3, 2)
    for n, i in ((1, -1), (2, 1), (3, 2)):
        for h in range(2):
            forward(h, n, i)
    for h in range(2):
        for n in range(4):
            two[h, n][2].wait_recv()
            two[h, n][3].wait_recv()

    weights_ready(2, 3)
    depth = cols_all // 4

    def up_step(k, carry):
        cs = pl.ds(pl.multiple_of(k * depth, 128), depth)
        v = lax.dot_general(
            nrm[:, :, :, cs].reshape(256, depth), gus[:, cs], (((1,), (1,)), ((), ())), preferred_element_type=F32
        )

        @pl.when(k == 0)
        def _():
            acc[...] = v

        @pl.when(k > 0)
        def _():
            acc[...] += v

        return carry

    lax.fori_loop(0, 4, up_step, 0)
    g = acc[:, :640]
    hid[...] = (g / (1.0 + jnp.exp(-g)) * acc[:, 640:]).astype(BF16)
    weights_ready(4)

    def fill_down(base, size):
        cs = pl.ds(base, size)
        v = jnp.dot(hid[:, : 2 * ff], ds[:, cs], preferred_element_type=F32)
        part[:, :, :, cs] = v.astype(BF16).reshape(NX, NZ, 16, size)

    def finish_down(base, size, value):
        cs = pl.ds(base, size)
        out_ref[:, cs] = (mid[:, cs] + value).astype(BF16)

    reduce_scatter(1, fill_down, (e1, e2, f1, f2), finish_down)
    while sent:
        sent.pop().wait_send()


def tail(lat, value_up, out_proj, residual, norm_gain, gate_t, up_t, down):
    cols = residual.shape[1]
    ff = gate_t.shape[0]
    width = cols // 2 // SUBS
    rs_bufs = [
        pltpu.VMEM((2, SUBS, 2, 4, 16, width // 2), BF16),
        pltpu.VMEM((2, SUBS, 2, 4, 16, width), BF16),
        pltpu.VMEM((2, SUBS, 2, 16, width // 2), BF16),
        pltpu.VMEM((2, SUBS, 2, 16, width), BF16),
    ]
    n_rs = 2 * 2 * SUBS * 2 * 6
    dma = pltpu.SemaphoreType.DMA
    return pl.pallas_call(
        tail_kernel,
        out_shape=jax.ShapeDtypeStruct(residual.shape, BF16),
        in_specs=[aspec(), aspec(), aspec(), vspec(), vspec(), aspec(), aspec(), aspec()],
        out_specs=vspec(),
        scratch_shapes=[
            pltpu.VMEM((16, 64, LATENT), BF16),
            pltpu.VMEM((2, 2, LATENT, 128), BF16),
            pltpu.VMEM((2, 256, cols), BF16),
            pltpu.VMEM((1280, cols), BF16),
            pltpu.VMEM((2 * ff, cols), BF16),
            pltpu.VMEM((256, 512), BF16),
            pltpu.VMEM((NX, NZ, 16, cols), BF16),
            pltpu.VMEM((NX, NZ, 16, cols), BF16),
            pltpu.VMEM((16, cols), F32),
            pltpu.VMEM((256, 1280), F32),
            pltpu.VMEM((256, 640), BF16),
            *rs_bufs,
            *rs_bufs,
            dma((1,)),
            dma((15,)),
            dma((15,)),
            dma((5,)),
            dma((5,)),
            dma((5,)),
            dma((n_rs,)),
            dma((n_rs,)),
            dma((40,)),
            dma((40,)),
        ],
        compiler_params=pltpu.CompilerParams(collective_id=0, has_side_effects=True, vmem_limit_bytes=VMEM_LIMIT),
        cost_estimate=pl.CostEstimate(flops=12_000_000_000, bytes_accessed=40_000_000, transcendentals=200_000),
        name="tail",
    )(lat, value_up, out_proj, residual, norm_gain.reshape(1, cols), gate_t, up_t, down)


def body(
    page_pool,
    move_source,
    move_page,
    move_slot,
    row_count,
    lengths,
    page_table,
    queries,
    value_up,
    out_proj,
    residual,
    norm_gain,
    gate_proj,
    up_proj,
    down_proj,
):
    rank_count = lax.axis_size("dp")
    own_rank = lax.axis_index("dp")
    move_count = move_page.shape[0] // rank_count
    capacity = 2
    sources = move_source.reshape(rank_count, move_count)
    page_ids = move_page.reshape(rank_count, move_count)
    slot_ids = move_slot.reshape(rank_count, move_count)
    move_order = jnp.arange(move_count)
    earlier = (sources[:, :, None] == sources[:, None, :]) & (
        move_order[None, None, :] < move_order[None, :, None]
    )
    arrival = jnp.sum(earlier.astype(jnp.int32), axis=2)
    chosen = (sources == own_rank)[:, :, None] & (
        arrival[:, :, None] == jnp.arange(capacity)[None, None, :]
    )
    send_ids = jnp.sum(jnp.where(chosen, page_ids[:, :, None], 0), axis=1).reshape(-1)
    outgoing = pack_pages(send_ids, page_pool)
    incoming = lax.all_to_all(outgoing, "dp", split_axis=0, concat_axis=0, tiled=True)
    own_sources = lax.dynamic_index_in_dim(sources, own_rank, 0, keepdims=False)
    own_arrival = lax.dynamic_index_in_dim(arrival, own_rank, 0, keepdims=False)
    own_slots = lax.dynamic_index_in_dim(slot_ids, own_rank, 0, keepdims=False)
    acc, top, total, list_b, count_b = attend_local(
        page_table, lengths, row_count, own_slots, queries, page_pool
    )
    latent = attend_moved(
        list_b, count_b, own_sources * capacity + own_arrival, queries, acc, top, total, incoming
    )
    rows, heads, _ = latent.shape
    lat = latent.reshape(rows, NX * NZ, heads // (NX * NZ), LATENT).transpose(1, 2, 0, 3)
    lat = lat.reshape(NX * NZ, -1, LATENT)
    return tail(lat, value_up, out_proj, residual, norm_gain, gate_proj.T, up_proj.T, down_proj)


def solution(mesh):
    in_specs = (
        P(("rep", "dp"), None, None),
        P("rep", None),
        P("rep"),
        P("rep"),
        P(("rep", "dp")),
        P(("rep", "dp")),
        P(("rep", "dp"), None),
        P(("rep", "dp"), None, None),
        P("dp", None, None),
        P("dp", None),
        P(("rep", "dp"), None),
        P(),
        P(None, "dp"),
        P(None, "dp"),
        P("dp", None),
    )
    out_specs = P(("rep", "dp"), None)
    return jax.shard_map(body, mesh=mesh, in_specs=in_specs, out_specs=out_specs, check_vma=False)
```

```python
import functools

import jax
import jax.numpy as jnp
from jax import lax
from jax.experimental import pallas as pl
from jax.experimental.pallas import tpu as pltpu
from jax.sharding import PartitionSpec as P

LATENT = 512
SOFTMAX_SCALE = 192 ** (-0.5)
LOW = -1e30
MESH = pl.DeviceIdType.MESH
F32 = jnp.float32
BF16 = jnp.bfloat16
VMEM_LIMIT = 60 * 2**20
NX = 4
NZ = 4


def vspec():
    return pl.BlockSpec(memory_space=pltpu.VMEM)


def sspec():
    return pl.BlockSpec(memory_space=pltpu.SMEM)


def aspec():
    return pl.BlockSpec(memory_space=pl.ANY)


def attend_kernel(
    ids, entries, index, slots, rc, table, lens, q_ref, pool_hbm, out_ref,
    pool, outbox, via, inbox, pages, mult, acc, top, total,
    pool_sems, copy_sems, one_ss, one_rs, two_ss, two_rs,
):
    me = lax.axis_index("dp")
    core = lax.rem(me, 2)
    chip = me // 2
    x = chip // NZ
    z = lax.rem(chip, NZ)
    rows, heads, width = q_ref.shape
    page = pool.shape[1]
    part = page // 2
    refs = table.shape[1]
    moves = slots.shape[0]

    loads = []
    for k in range(4):
        span = pl.ds(k * (pool.shape[0] // 4), pool.shape[0] // 4)
        loads.append(pltpu.make_async_copy(pool_hbm.at[span], pool.at[span], pool_sems.at[k]))
        loads[-1].start()

    def device(a, b, e):
        return (lax.rem(x + a, NX) * NZ + lax.rem(z + b, NZ)) * 2 + lax.rem(core + e, 2)

    def on(a, b, e):
        return {"dp": device(a, b, e)}

    near = [(0, 0, 1)] + [(a, 0, e) for a in (1, 2, 3) for e in (0, 1)] + [(0, b, e) for b in (1, 2, 3) for e in (0, 1)]
    barrier = pltpu.get_barrier_semaphore()
    for at in near:
        pl.semaphore_signal(barrier, inc=1, device_id=on(*at), device_id_type=MESH)
    pl.semaphore_wait(barrier, len(near))
    for copy in loads:
        copy.wait()

    sent = []

    def send(src, dst, ss, rs, to):
        copy = pltpu.make_async_remote_copy(
            src_ref=src, dst_ref=dst, send_sem=ss, recv_sem=rs, device_id=to, device_id_type=MESH
        )
        copy.start()
        sent.append(copy)
        return copy

    def pack(i, first):
        d = first + i
        one, two = pool[ids[2 * d]], pool[ids[2 * d + 1]]
        rope = jnp.concatenate([one[:, LATENT:], two[:, LATENT:]], axis=1)
        for h in range(2):
            rs = slice(h * part, (h + 1) * part)
            outbox[h, d, :, :LATENT] = one[rs, :LATENT]
            outbox[h, d, :, LATENT : 2 * LATENT] = two[rs, :LATENT]
            outbox[h, d, :, 2 * LATENT :] = rope[rs]
        return first

    one_copies = {}
    final = {}
    local = []

    def deliver(h, a, b, e, src):
        origin = (lax.rem(x + (NX - a if h == 0 else 0), NX) * NZ + lax.rem(z + (0 if h == 0 else NZ - b), NZ)) * 2 + core
        dst = inbox.at[origin, pl.ds(h * part, part), :]
        at = ((a * NZ + b) * 2 + e) * 2 + h
        da, db = (0, b) if h == 0 else (a, 0)
        if (da, db, e) == (0, 0, 0):
            copy = pltpu.make_async_copy(src, dst, copy_sems.at[len(local)])
            copy.start()
            local.append(copy)
        else:
            final[at] = send(src, dst, two_ss.at[at], two_rs.at[at], on(da, db, e))

    for n, a in enumerate((2, 1, 3, 0)):
        xa = lax.rem(x + a, NX)
        lax.fori_loop(0, 8, pack, xa * 8)
        if a:
            one_copies[0, a] = send(
                outbox.at[0, pl.ds(xa * 8, 8)], via.at[0, a - 1], one_ss.at[a - 1], one_rs.at[a - 1], on(a, 0, 0)
            )
        for b in (2, 1, 3):
            zb = lax.rem(z + b, NZ)
            at = 3 + (b - 1) * 4 + n
            one_copies[1, b, n] = send(
                outbox.at[1, pl.ds(xa * 8 + zb * 2, 2)],
                via.at[1, b - 1, pl.ds(xa * 2, 2)],
                one_ss.at[at],
                one_rs.at[at],
                on(0, b, 0),
            )

    def second_hop(k):
        if k:
            one_copies[0, k].wait_recv()
            for n in range(4):
                one_copies[1, k, n].wait_recv()
        for o in (2, 1, 3, 0):
            for e in range(2):
                ce = lax.rem(core + e, 2)
                zo, xo = lax.rem(z + o, NZ), lax.rem(x + o, NX)
                deliver(0, k, o, e, via.at[0, k - 1, zo * 2 + ce] if k else outbox.at[0, x * 8 + zo * 2 + ce])
                deliver(1, o, k, e, via.at[1, k - 1, xo * 2 + ce] if k else outbox.at[1, xo * 8 + z * 2 + ce])

    def attend_row(r, carry):
        q = q_ref[r]
        group = 8
        col = lax.broadcasted_iota(jnp.int32, (1, page * group), 1)
        keys, scores = [], []
        for g in range(refs // group):
            es = [entries[r * refs + g * group + i] for i in range(group)]
            k = jnp.concatenate([pool[e >> 7] for e in es], axis=0)
            limit = jnp.zeros((1, page * group), jnp.int32)
            for i, e in enumerate(es):
                limit = jnp.where((col >> 6) == i, e & 127, limit)
            s = lax.dot_general(q, k, (((1,), (1,)), ((), ())), preferred_element_type=F32) * SOFTMAX_SCALE
            scores.append(jnp.where((col & 63) < limit, s, LOW))
            keys.append(k)
        m = functools.reduce(jnp.maximum, [jnp.max(s, axis=1, keepdims=True) for s in scores])
        t = jnp.zeros((heads, 1), F32)
        o = jnp.zeros((heads, LATENT), F32)
        for s, k in zip(scores, keys):
            p = jnp.exp(s - m)
            t = t + jnp.sum(p, axis=1, keepdims=True)
            o = o + jnp.dot(p.astype(BF16), k[:, :LATENT], preferred_element_type=F32)
        some = m > 0.5 * LOW
        acc[r] = jnp.where(some, o, 0.0)
        top[r] = jnp.broadcast_to(m, (heads, 128))
        total[r] = jnp.broadcast_to(jnp.where(some, t, 0.0), (heads, 128))
        return carry

    second_hop(0)
    lax.fori_loop(0, 5, attend_row, 0)
    second_hop(1)
    second_hop(3)
    lax.fori_loop(5, 9, attend_row, 0)
    second_hop(2)
    lax.fori_loop(9, rows, attend_row, 0)

    row = lax.broadcasted_iota(jnp.int32, (rows, refs), 0)
    pos = lax.broadcasted_iota(jnp.int32, (rows, refs), 1)
    valid = jnp.where(row < rc[0], jnp.clip(lens[...] - page * pos, 0, page), 0)
    whole = (valid == page).astype(F32)
    some = ((valid > 0) & (valid < page)).astype(F32)
    last = jnp.sum(some * valid.astype(F32), axis=1, keepdims=True)
    off = lax.broadcasted_iota(jnp.int32, (rows, page), 1).astype(F32)
    inside = (off < last).astype(F32)
    for i in range(0, moves, 2):
        pair = []
        for j in (i, i + 1):
            hit = (table[...] == slots[j]).astype(F32)
            pair.append(
                jnp.sum(hit * whole, axis=1, keepdims=True) + jnp.sum(hit * some, axis=1, keepdims=True) * inside
            )
        mult[:, i * page : (i + 2) * page] = jnp.concatenate(pair, axis=1)

    for copy in local:
        copy.wait()
    for copy in final.values():
        copy.wait_recv()

    def unpack(i, carry):
        at = index[i]
        pair = inbox[at >> 1]
        first = (at & 1) == 0
        here = pl.ds(pl.multiple_of(i * page, page), page)
        rope = width - LATENT
        pages[here, :LATENT] = jnp.where(first, pair[:, :LATENT], pair[:, LATENT : 2 * LATENT])
        pages[here, LATENT:] = jnp.where(
            first, pair[:, 2 * LATENT : 2 * LATENT + rope], pair[:, 2 * LATENT + rope :]
        )
        return carry

    lax.fori_loop(0, moves, unpack, 0)

    step = 4

    def moved_rows(n, carry):
        rs = pl.ds(n * step, step)
        q = q_ref[rs].reshape(step * heads, width)
        s = lax.dot_general(q, pages[...], (((1,), (1,)), ((), ())), preferred_element_type=F32) * SOFTMAX_SCALE
        times = jnp.concatenate(
            [jnp.broadcast_to(mult[pl.ds(n * step + i, 1), :], (heads, moves * page)) for i in range(step)], axis=0
        )
        s = jnp.where(times > 0.0, s, LOW)
        old = top[rs].reshape(step * heads, 128)[:, :1]
        m = jnp.maximum(old, jnp.max(s, axis=1, keepdims=True))
        shrink = jnp.exp(old - m)
        p = jnp.exp(s - m) * times
        t = total[rs].reshape(step * heads, 128)[:, :1] * shrink + jnp.sum(p, axis=1, keepdims=True)
        o = acc[rs].reshape(step * heads, LATENT) * shrink
        o = o + jnp.dot(p.astype(BF16), pages[:, :LATENT], preferred_element_type=F32)
        o = o / jnp.where(t == 0.0, 1.0, t)
        out_ref[rs] = o.astype(BF16).reshape(step, heads, LATENT)
        return carry

    lax.fori_loop(0, rows // step, moved_rows, 0)
    while sent:
        sent.pop().wait_send()


def attend(ids, entries, index, slots, rc, table, lens, queries, pool):
    rows, heads, width = queries.shape
    count, page, _ = pool.shape
    moves = slots.shape[0]
    ranks = NX * NZ * 2
    dma = pltpu.SemaphoreType.DMA
    return pl.pallas_call(
        attend_kernel,
        out_shape=jax.ShapeDtypeStruct((rows, heads, LATENT), BF16),
        in_specs=[sspec()] * 5 + [vspec()] * 3 + [aspec()],
        out_specs=vspec(),
        scratch_shapes=[
            pltpu.VMEM(pool.shape, BF16),
            pltpu.VMEM((2, ranks, page // 2, 2 * width), BF16),
            pltpu.VMEM((2, 3, 8, page // 2, 2 * width), BF16),
            pltpu.VMEM((ranks, page, 2 * width), BF16),
            pltpu.VMEM((moves * page, width), BF16),
            pltpu.VMEM((rows, moves * page), F32),
            pltpu.VMEM((rows, heads, LATENT), F32),
            pltpu.VMEM((rows, heads, 128), F32),
            pltpu.VMEM((rows, heads, 128), F32),
            dma((4,)),
            dma((8,)),
            dma((15,)),
            dma((15,)),
            dma((64,)),
            dma((64,)),
        ],
        compiler_params=pltpu.CompilerParams(collective_id=1, has_side_effects=True, vmem_limit_bytes=VMEM_LIMIT),
        name="attend",
    )(ids, entries, index, slots, rc, table, lens.reshape(rows, 1), queries, pool)


SUBS = 2


def tail_kernel(
    lat, vu, wo, res, gain, gate, up, down, out_ref,
    rl, vus, wos, gus, ds, ho, part, nrm, mid, acc, hid,
    b1, b2, c1, c2, e1, e2, f1, f2,
    bar_sems, lat_ss, lat_rs, w_ls, w_ss, w_rs, rs_ss, rs_rs, ag_ss, ag_rs,
):
    me = lax.axis_index("dp")
    core = lax.rem(me, 2)
    chip = me // 2
    x = chip // NZ
    z = lax.rem(chip, NZ)
    cols_all = part.shape[3]
    half = cols_all // 2
    ff = gate.shape[0]

    def device(dx, dz):
        return {"dp": (lax.rem(x + dx + NX, NX) * NZ + lax.rem(z + dz + NZ, NZ)) * 2 + core}

    sibling = {"dp": me + 1 - 2 * core}

    barrier = pltpu.get_barrier_semaphore()
    peers = [(a, b) for a in range(NX) for b in range(NZ) if (a, b) != (0, 0)]
    for a, b in peers:
        pl.semaphore_signal(barrier, inc=1, device_id=device(a, b), device_id_type=MESH)
    pl.semaphore_signal(barrier, inc=1, device_id=sibling, device_id_type=MESH)
    pl.semaphore_wait(barrier, len(peers) + 1)

    sent = []

    def send(src, dst, ss, rs, to):
        copy = pltpu.make_async_remote_copy(
            src_ref=src, dst_ref=dst, send_sem=ss, recv_sem=rs, device_id=to, device_id_type=MESH
        )
        copy.start()
        sent.append(copy)
        return copy

    lat_copies = []
    for k, (a, b) in enumerate(peers):
        to_chip = lax.rem(x + a, NX) * NZ + lax.rem(z + b, NZ)
        lat_copies.append(send(lat.at[to_chip], rl.at[chip], lat_ss.at[k], lat_rs.at[k], device(a, b)))
    own_lat = pltpu.make_async_copy(lat.at[chip], rl.at[chip], bar_sems.at[0])
    own_lat.start()

    row0 = pl.multiple_of(core * ff, 16)
    row1 = pl.multiple_of(640 + core * ff, 16)
    places = [
        (vu, vus.at[core]),
        (wo, wos.at[core]),
        (gate, gus.at[pl.ds(row0, ff), :]),
        (up, gus.at[pl.ds(row1, ff), :]),
        (down, ds.at[pl.ds(row0, ff), :]),
    ]
    w_local, w_remote = [], []
    for k, (src, dst) in enumerate(places):
        copy = pltpu.make_async_copy(src, dst, w_ls.at[k])
        copy.start()
        w_local.append(copy)
        w_remote.append(send(src, dst, w_ss.at[k], w_rs.at[k], sibling))
    gus[pl.ds(2 * ff, 640 - 2 * ff), :] = jnp.zeros((640 - 2 * ff, cols_all), BF16)
    gus[pl.ds(640 + 2 * ff, 640 - 2 * ff), :] = jnp.zeros((640 - 2 * ff, cols_all), BF16)

    def weights_ready(*ks):
        for k in ks:
            w_local[k].wait()
            w_remote[k].wait_recv()

    own_lat.wait()
    for copy in lat_copies:
        copy.wait_recv()
    weights_ready(0)
    for h in range(4):
        l = rl[:, h * 16 : (h + 1) * 16, :].reshape(256, LATENT)
        ho[:, h * 128 : (h + 1) * 128] = jnp.dot(l, vus[h // 2, h % 2], preferred_element_type=F32).astype(BF16)

    width = half // SUBS
    wing = width // 2

    def reduce_scatter(turn, fill, bufs, finish):
        r1, r2, t1, t2 = bufs

        def chunk(h, phase, i, base, size):
            cs = pl.ds(base, size)
            xi, zi = lax.rem(x + i + NX, NX), lax.rem(z + i + NZ, NZ)
            along_x = (h == 0) == (phase == 0)
            if phase == 0:
                return part.at[xi, :, :, cs] if along_x else part.at[:, zi, :, cs]
            return part.at[xi, z, :, cs] if along_x else part.at[x, zi, :, cs]

        def to(h, phase, i):
            return device(i, 0) if (h == 0) == (phase == 0) else device(0, i)

        def sems(h, s, phase, k):
            at = (((turn * 2 + h) * SUBS + s) * 2 + phase) * 6 + k
            return rs_ss.at[at], rs_rs.at[at]

        def bufs_of(h, s, phase):
            first, second = (r1, r2) if phase == 0 else (t1, t2)
            return first.at[h, s], second.at[h, s]

        state = {}

        def start(h, s, phase):
            base = h * half + s * width
            first, second = bufs_of(h, s, phase)
            lo, hi = base, base + wing
            state[h, s, phase] = [
                send(chunk(h, phase, 2, lo, wing), first.at[0], *sems(h, s, phase, 0), to(h, phase, 1)),
                send(chunk(h, phase, 2, hi, wing), first.at[1], *sems(h, s, phase, 1), to(h, phase, -1)),
                send(chunk(h, phase, 1, hi, wing), second.at[0, ..., pl.ds(wing, wing)], *sems(h, s, phase, 2), to(h, phase, 1)),
                send(chunk(h, phase, -1, lo, wing), second.at[1, ..., pl.ds(0, wing)], *sems(h, s, phase, 3), to(h, phase, -1)),
            ]

        def middle(h, s, phase):
            base = h * half + s * width
            first, second = bufs_of(h, s, phase)
            copies = state[h, s, phase]
            for side, (i, at) in enumerate(((1, 0), (-1, wing))):
                copies[side].wait_recv()
                mine = chunk(h, phase, i, base + at, wing)
                mine[...] = (mine[...].astype(F32) + first[side].astype(F32)).astype(BF16)
                copies.append(
                    send(mine, second.at[side, ..., pl.ds(at, wing)], *sems(h, s, phase, 4 + side), to(h, phase, i))
                )

        def total(h, s, phase):
            base = h * half + s * width
            _, second = bufs_of(h, s, phase)
            for copy in state[h, s, phase][2:]:
                copy.wait_recv()
            mine = chunk(h, phase, 0, base, width)
            value = mine[...].astype(F32) + second[0].astype(F32) + second[1].astype(F32)
            if phase == 0:
                mine[...] = value.astype(BF16)
            else:
                finish(base, width, value)

        order = [(h, s) for s in range(SUBS) for h in range(2)]
        for h, s in order:
            fill(h * half + s * width, width)
            start(h, s, 0)
        for h, s in order:
            middle(h, s, 0)
        for h, s in order:
            total(h, s, 0)
            start(h, s, 1)
        for h, s in order:
            middle(h, s, 1)
        for h, s in order:
            total(h, s, 1)

    weights_ready(1)

    def fill_out(base, size):
        cs = pl.ds(base, size)
        v = jnp.dot(ho[:, :256], wos[0, :, cs], preferred_element_type=F32)
        v = v + jnp.dot(ho[:, 256:], wos[1, :, cs], preferred_element_type=F32)
        part[:, :, :, cs] = v.astype(BF16).reshape(NX, NZ, 16, size)

    squares = []

    def finish_out(base, size, value):
        cs = pl.ds(base, size)
        m = res[:, cs].astype(F32) + value
        mid[:, cs] = m
        squares.append(jnp.sum(m * m, axis=1, keepdims=True))

    reduce_scatter(0, fill_out, (b1, b2, c1, c2), finish_out)
    factor = lax.rsqrt(sum(squares) / cols_all + 1e-06)
    nrm[x, z] = (mid[...] * factor * gain[...]).astype(BF16)
    while sent:
        sent.pop().wait_send()

    quarter = half // 2

    def block(h, i, j, lo, size):
        cs = pl.ds(h * half + lo, size)
        dx, dz = (j, i) if h == 0 else (i, j)
        return nrm.at[lax.rem(x + dx + NX, NX), lax.rem(z + dz + NZ, NZ), :, cs]

    def ag_sems(h, k):
        return ag_ss.at[h * 20 + k], ag_rs.at[h * 20 + k]

    def along(h, first, i):
        return device(0, i) if (h == 0) == first else device(i, 0)

    def pass_on(ref, h, k, first, i):
        return send(ref, ref, *ag_sems(h, k), along(h, first, i))

    one, two = {}, {}
    for h in range(2):
        ref = block(h, 0, 0, 0, half)
        one[h] = [pass_on(ref, h, 0, True, 1), pass_on(ref, h, 1, True, -1)]

    def spread(h, n, i):
        ref = block(h, i, 0, 0, half)
        two[h, n] = [pass_on(ref, h, 4 + 4 * n, False, 1), pass_on(ref, h, 5 + 4 * n, False, -1)]

    def forward(h, n, i):
        two[h, n][0].wait_recv()
        two[h, n].append(pass_on(block(h, i, -1, 0, quarter), h, 6 + 4 * n, False, 1))
        two[h, n][1].wait_recv()
        two[h, n].append(pass_on(block(h, i, 1, quarter, quarter), h, 7 + 4 * n, False, -1))

    for h in range(2):
        spread(h, 0, 0)
    for h in range(2):
        one[h][0].wait_recv()
        one[h].append(pass_on(block(h, -1, 0, 0, quarter), h, 2, True, 1))
        one[h][1].wait_recv()
        one[h].append(pass_on(block(h, 1, 0, quarter, quarter), h, 3, True, -1))
        spread(h, 1, -1)
        spread(h, 2, 1)
    for h in range(2):
        forward(h, 0, 0)
    for h in range(2):
        one[h][2].wait_recv()
        one[h][3].wait_recv()
        spread(h, 3, 2)
    for n, i in ((1, -1), (2, 1), (3, 2)):
        for h in range(2):
            forward(h, n, i)
    for h in range(2):
        for n in range(4):
            two[h, n][2].wait_recv()
            two[h, n][3].wait_recv()

    weights_ready(2, 3)
    depth = cols_all // 4

    def up_step(k, carry):
        cs = pl.ds(pl.multiple_of(k * depth, 128), depth)
        v = lax.dot_general(
            nrm[:, :, :, cs].reshape(256, depth), gus[:, cs], (((1,), (1,)), ((), ())), preferred_element_type=F32
        )

        @pl.when(k == 0)
        def _():
            acc[...] = v

        @pl.when(k > 0)
        def _():
            acc[...] += v

        return carry

    lax.fori_loop(0, 4, up_step, 0)
    g = acc[:, :640]
    hid[...] = (g / (1.0 + jnp.exp(-g)) * acc[:, 640:]).astype(BF16)
    weights_ready(4)

    def fill_down(base, size):
        cs = pl.ds(base, size)
        v = jnp.dot(hid[:, : 2 * ff], ds[:, cs], preferred_element_type=F32)
        part[:, :, :, cs] = v.astype(BF16).reshape(NX, NZ, 16, size)

    def finish_down(base, size, value):
        cs = pl.ds(base, size)
        out_ref[:, cs] = (mid[:, cs] + value).astype(BF16)

    reduce_scatter(1, fill_down, (e1, e2, f1, f2), finish_down)
    while sent:
        sent.pop().wait_send()


def tail(lat, value_up, out_proj, residual, norm_gain, gate_t, up_t, down):
    cols = residual.shape[1]
    ff = gate_t.shape[0]
    width = cols // 2 // SUBS
    rs_bufs = [
        pltpu.VMEM((2, SUBS, 2, 4, 16, width // 2), BF16),
        pltpu.VMEM((2, SUBS, 2, 4, 16, width), BF16),
        pltpu.VMEM((2, SUBS, 2, 16, width // 2), BF16),
        pltpu.VMEM((2, SUBS, 2, 16, width), BF16),
    ]
    n_rs = 2 * 2 * SUBS * 2 * 6
    dma = pltpu.SemaphoreType.DMA
    return pl.pallas_call(
        tail_kernel,
        out_shape=jax.ShapeDtypeStruct(residual.shape, BF16),
        in_specs=[aspec(), aspec(), aspec(), vspec(), vspec(), aspec(), aspec(), aspec()],
        out_specs=vspec(),
        scratch_shapes=[
            pltpu.VMEM((16, 64, LATENT), BF16),
            pltpu.VMEM((2, 2, LATENT, 128), BF16),
            pltpu.VMEM((2, 256, cols), BF16),
            pltpu.VMEM((1280, cols), BF16),
            pltpu.VMEM((2 * ff, cols), BF16),
            pltpu.VMEM((256, 512), BF16),
            pltpu.VMEM((NX, NZ, 16, cols), BF16),
            pltpu.VMEM((NX, NZ, 16, cols), BF16),
            pltpu.VMEM((16, cols), F32),
            pltpu.VMEM((256, 1280), F32),
            pltpu.VMEM((256, 640), BF16),
            *rs_bufs,
            *rs_bufs,
            dma((1,)),
            dma((15,)),
            dma((15,)),
            dma((5,)),
            dma((5,)),
            dma((5,)),
            dma((n_rs,)),
            dma((n_rs,)),
            dma((40,)),
            dma((40,)),
        ],
        compiler_params=pltpu.CompilerParams(collective_id=0, has_side_effects=True, vmem_limit_bytes=VMEM_LIMIT),
        cost_estimate=pl.CostEstimate(flops=12_000_000_000, bytes_accessed=40_000_000, transcendentals=200_000),
        name="tail",
    )(lat, value_up, out_proj, residual, norm_gain.reshape(1, cols), gate_t, up_t, down)


def body(
    page_pool,
    move_source,
    move_page,
    move_slot,
    row_count,
    lengths,
    page_table,
    queries,
    value_up,
    out_proj,
    residual,
    norm_gain,
    gate_proj,
    up_proj,
    down_proj,
):
    rank_count = lax.axis_size("dp")
    own_rank = lax.axis_index("dp")
    move_count = move_page.shape[0] // rank_count
    capacity = 2
    sources = move_source.reshape(rank_count, move_count)
    page_ids = move_page.reshape(rank_count, move_count)
    slot_ids = move_slot.reshape(rank_count, move_count)
    move_order = jnp.arange(move_count)
    earlier = (sources[:, :, None] == sources[:, None, :]) & (
        move_order[None, None, :] < move_order[None, :, None]
    )
    arrival = jnp.sum(earlier.astype(jnp.int32), axis=2)
    chosen = (sources == own_rank)[:, :, None] & (
        arrival[:, :, None] == jnp.arange(capacity)[None, None, :]
    )
    send_ids = jnp.sum(jnp.where(chosen, page_ids[:, :, None], 0), axis=1).reshape(-1)
    own_sources = lax.dynamic_index_in_dim(sources, own_rank, 0, keepdims=False)
    own_arrival = lax.dynamic_index_in_dim(arrival, own_rank, 0, keepdims=False)
    own_slots = lax.dynamic_index_in_dim(slot_ids, own_rank, 0, keepdims=False)
    rows, refs = page_table.shape
    page = page_pool.shape[1]
    valid = jnp.clip(lengths[:, None] - page * jnp.arange(refs)[None, :], 0, page)
    valid = jnp.where((jnp.arange(rows) < row_count[0])[:, None], valid, 0)
    is_moved = jnp.any(page_table[:, :, None] == own_slots[None, None, :], axis=2)
    entries = jnp.where(is_moved, 0, page_table * 128 + valid).reshape(-1)
    latent = attend(
        send_ids, entries, own_sources * capacity + own_arrival, own_slots, row_count, page_table, lengths,
        queries, page_pool,
    )
    rows, heads, _ = latent.shape
    lat = latent.reshape(rows, NX * NZ, heads // (NX * NZ), LATENT).transpose(1, 2, 0, 3)
    lat = lat.reshape(NX * NZ, -1, LATENT)
    return tail(lat, value_up, out_proj, residual, norm_gain, gate_proj.T, up_proj.T, down_proj)


def solution(mesh):
    in_specs = (
        P(("rep", "dp"), None, None),
        P("rep", None),
        P("rep"),
        P("rep"),
        P(("rep", "dp")),
        P(("rep", "dp")),
        P(("rep", "dp"), None),
        P(("rep", "dp"), None, None),
        P("dp", None, None),
        P("dp", None),
        P(("rep", "dp"), None),
        P(),
        P(None, "dp"),
        P(None, "dp"),
        P("dp", None),
    )
    out_specs = P(("rep", "dp"), None)
    return jax.shard_map(body, mesh=mesh, in_specs=in_specs, out_specs=out_specs, check_vma=False)
```

```python
import functools

import jax
import jax.numpy as jnp
from jax import lax
from jax.experimental import pallas as pl
from jax.experimental.pallas import tpu as pltpu
from jax.sharding import PartitionSpec as P

LATENT = 512
SOFTMAX_SCALE = 192 ** (-0.5)
LOW = -1e30
MESH = pl.DeviceIdType.MESH
F32 = jnp.float32
BF16 = jnp.bfloat16
VMEM_LIMIT = 60 * 2**20
NX = 4
NZ = 4


def vspec():
    return pl.BlockSpec(memory_space=pltpu.VMEM)


def sspec():
    return pl.BlockSpec(memory_space=pltpu.SMEM)


def aspec():
    return pl.BlockSpec(memory_space=pl.ANY)


def attend_kernel(
    src, page_of, slot_of, rc, lens, table, q_ref, pool_hbm, vu, wo, out_ref, vu_out, wo_out,
    pool, outbox, via, inbox, pages, mult, acc, top, total, packed, vu_box, wo_box, entries_v, entries,
    pool_sems, copy_sems, one_ss, one_rs, two_ss, two_rs, w_ss, w_rs, lat_ss, lat_rs,
):
    me = lax.axis_index("dp")
    core = lax.rem(me, 2)
    chip = me // 2
    x = chip // NZ
    z = lax.rem(chip, NZ)
    rows, heads, width = q_ref.shape
    page = pool.shape[1]
    part = page // 2
    refs = table.shape[1]
    moves = pages.shape[0] // page
    mine = me * moves

    loads = []
    for k in range(4):
        span = pl.ds(k * (pool.shape[0] // 4), pool.shape[0] // 4)
        loads.append(pltpu.make_async_copy(pool_hbm.at[span], pool.at[span], pool_sems.at[k]))
        loads[-1].start()

    def device(a, b, e):
        return (lax.rem(x + a, NX) * NZ + lax.rem(z + b, NZ)) * 2 + lax.rem(core + e, 2)

    def on(a, b, e):
        return {"dp": device(a, b, e)}

    near = [(0, 0, 1)] + [(a, 0, e) for a in (1, 2, 3) for e in (0, 1)] + [(0, b, e) for b in (1, 2, 3) for e in (0, 1)]
    far = [(a, b, 0) for a in (1, 2, 3) for b in (1, 2, 3)]
    barrier = pltpu.get_barrier_semaphore()
    for at in near + far:
        pl.semaphore_signal(barrier, inc=1, device_id=on(*at), device_id_type=MESH)

    row = lax.broadcasted_iota(jnp.int32, (rows, refs), 0)
    pos = lax.broadcasted_iota(jnp.int32, (rows, refs), 1)
    length = jnp.zeros((rows, refs), jnp.int32)
    for r in range(rows):
        length = jnp.where(row == r, jnp.where(r < rc[0], lens[r], 0), length)
    valid = jnp.clip(length - page * pos, 0, page)
    entry = table[...] * 128 + valid
    for i in range(moves):
        entry = jnp.where(table[...] == slot_of[mine + i], 0, entry)
    entries_v[:, :refs] = entry
    to_scalar = pltpu.make_async_copy(entries_v, entries, pool_sems.at[4])
    to_scalar.start()
    pl.semaphore_wait(barrier, len(near + far))
    for copy in loads:
        copy.wait()

    sent = []

    def send(src, dst, ss, rs, to):
        copy = pltpu.make_async_remote_copy(
            src_ref=src, dst_ref=dst, send_sem=ss, recv_sem=rs, device_id=to, device_id_type=MESH
        )
        copy.start()
        sent.append(copy)
        return copy

    def pack(i, first):
        d = first + i
        hits = [src[0, d * moves + j] == me for j in range(moves)]
        named = [page_of[d * moves + j] for j in range(moves)]
        early, late = 0, 0
        for j in range(moves):
            late = jnp.where(hits[j], named[j], late)
            early = jnp.where(hits[moves - 1 - j], named[moves - 1 - j], early)
        one, two = pool[early], pool[late]
        rope = jnp.concatenate([one[:, LATENT:], two[:, LATENT:]], axis=1)
        for h in range(2):
            rs = slice(h * part, (h + 1) * part)
            outbox[h, d, :, :LATENT] = one[rs, :LATENT]
            outbox[h, d, :, LATENT : 2 * LATENT] = two[rs, :LATENT]
            outbox[h, d, :, 2 * LATENT :] = rope[rs]
        return first

    one_copies = {}
    final = {}
    local = []

    def deliver(h, a, b, e, src):
        origin = (lax.rem(x + (NX - a if h == 0 else 0), NX) * NZ + lax.rem(z + (0 if h == 0 else NZ - b), NZ)) * 2 + core
        dst = inbox.at[origin, pl.ds(h * part, part), :]
        at = ((a * NZ + b) * 2 + e) * 2 + h
        da, db = (0, b) if h == 0 else (a, 0)
        if (da, db, e) == (0, 0, 0):
            copy = pltpu.make_async_copy(src, dst, copy_sems.at[len(local)])
            copy.start()
            local.append(copy)
        else:
            final[at] = send(src, dst, two_ss.at[at], two_rs.at[at], on(da, db, e))

    for n, a in enumerate((2, 1, 3, 0)):
        xa = lax.rem(x + a, NX)
        lax.fori_loop(0, 8, pack, xa * 8)
        if a:
            one_copies[0, a] = send(
                outbox.at[0, pl.ds(xa * 8, 8)], via.at[0, a - 1], one_ss.at[a - 1], one_rs.at[a - 1], on(a, 0, 0)
            )
        for b in (2, 1, 3):
            zb = lax.rem(z + b, NZ)
            at = 3 + (b - 1) * 4 + n
            one_copies[1, b, n] = send(
                outbox.at[1, pl.ds(xa * 8 + zb * 2, 2)],
                via.at[1, b - 1, pl.ds(xa * 2, 2)],
                one_ss.at[at],
                one_rs.at[at],
                on(0, b, 0),
            )

    def second_hop(k):
        if k:
            one_copies[0, k].wait_recv()
            for n in range(4):
                one_copies[1, k, n].wait_recv()
        for o in (2, 1, 3, 0):
            for e in range(2):
                ce = lax.rem(core + e, 2)
                zo, xo = lax.rem(z + o, NZ), lax.rem(x + o, NX)
                deliver(0, k, o, e, via.at[0, k - 1, zo * 2 + ce] if k else outbox.at[0, x * 8 + zo * 2 + ce])
                deliver(1, o, k, e, via.at[1, k - 1, xo * 2 + ce] if k else outbox.at[1, xo * 8 + z * 2 + ce])

    def attend_row(r, carry):
        q = q_ref[r]
        group = 8
        col = lax.broadcasted_iota(jnp.int32, (1, page * group), 1)
        keys, scores = [], []
        for g in range(refs // group):
            es = [entries[r, g * group + i] for i in range(group)]
            k = jnp.concatenate([pool[e >> 7] for e in es], axis=0)
            limit = jnp.zeros((1, page * group), jnp.int32)
            for i, e in enumerate(es):
                limit = jnp.where((col >> 6) == i, e & 127, limit)
            s = lax.dot_general(q, k, (((1,), (1,)), ((), ())), preferred_element_type=F32) * SOFTMAX_SCALE
            scores.append(jnp.where((col & 63) < limit, s, LOW))
            keys.append(k)
        m = functools.reduce(jnp.maximum, [jnp.max(s, axis=1, keepdims=True) for s in scores])
        t = jnp.zeros((heads, 1), F32)
        o = jnp.zeros((heads, LATENT), F32)
        for s, k in zip(scores, keys):
            p = jnp.exp(s - m)
            t = t + jnp.sum(p, axis=1, keepdims=True)
            o = o + jnp.dot(p.astype(BF16), k[:, :LATENT], preferred_element_type=F32)
        some = m > 0.5 * LOW
        acc[r] = jnp.where(some, o, 0.0)
        top[r] = jnp.broadcast_to(m, (heads, 128))
        total[r] = jnp.broadcast_to(jnp.where(some, t, 0.0), (heads, 128))
        return carry

    w_copies = [
        send(vu, vu_box, w_ss.at[0], w_rs.at[0], on(0, 0, 1)),
        send(wo, wo_box, w_ss.at[1], w_rs.at[1], on(0, 0, 1)),
    ]
    second_hop(0)
    to_scalar.wait()
    lax.fori_loop(0, 5, attend_row, 0)
    second_hop(1)
    second_hop(3)
    lax.fori_loop(5, 9, attend_row, 0)
    second_hop(2)
    lax.fori_loop(9, rows, attend_row, 0)

    for k, (box, out) in enumerate(((vu_box, vu_out), (wo_box, wo_out))):
        w_copies[k].wait_recv()
        w_copies[k] = pltpu.make_async_copy(box, out, pool_sems.at[k])
        w_copies[k].start()

    block = 16
    whole = (valid == page).astype(F32)
    some = ((valid > 0) & (valid < page)).astype(F32)
    last = jnp.sum(some * valid.astype(F32), axis=1, keepdims=True)
    off = lax.broadcasted_iota(jnp.int32, (rows, page), 1).astype(F32)
    inside = (off < last).astype(F32)
    for i in range(0, moves, 2):
        pair = []
        for j in (i, i + 1):
            hit = (table[...] == slot_of[mine + j]).astype(F32)
            pair.append(
                jnp.sum(hit * whole, axis=1, keepdims=True) + jnp.sum(hit * some, axis=1, keepdims=True) * inside
            )
        pair = jnp.concatenate(pair, axis=1)
        for r in range(rows):
            mult[r * block : (r + 1) * block, i * page : (i + 2) * page] = jnp.broadcast_to(
                pair[r : r + 1], (block, 2 * page)
            )

    places = []
    for i in range(moves):
        again = 0
        for j in range(i):
            again = again + (src[0, mine + i] == src[0, mine + j]).astype(jnp.int32)
        places.append((src[0, mine + i], again))

    for copy in local:
        copy.wait()
    for copy in final.values():
        copy.wait_recv()

    rope = width - LATENT
    for i, (rank, again) in enumerate(places):
        pair = inbox[rank]
        first = again == 0
        here = slice(i * page, (i + 1) * page)
        pages[here, :LATENT] = jnp.where(first, pair[:, :LATENT], pair[:, LATENT : 2 * LATENT])
        pages[here, LATENT:] = jnp.where(
            first, pair[:, 2 * LATENT : 2 * LATENT + rope], pair[:, 2 * LATENT + rope :]
        )

    size = rows * block
    to = lax.broadcasted_iota(jnp.int32, (size, size), 0)
    frm = lax.broadcasted_iota(jnp.int32, (size, size), 1)
    turn = (frm == (to % rows) * block + to // rows).astype(BF16)
    lat_copies = []
    for n, a in enumerate((2, 1, 3, 0)):
        xa = lax.rem(x + a, NX)
        hs = pl.ds(pl.multiple_of(xa * block, block), block)
        q = q_ref[:, hs, :].reshape(size, width)
        s = lax.dot_general(q, pages[...], (((1,), (1,)), ((), ())), preferred_element_type=F32) * SOFTMAX_SCALE
        times = mult[...]
        s = jnp.where(times > 0.0, s, LOW)
        old = top[:, hs, :].reshape(size, 128)[:, :1]
        m = jnp.maximum(old, jnp.max(s, axis=1, keepdims=True))
        shrink = jnp.exp(old - m)
        p = jnp.exp(s - m) * times
        t = total[:, hs, :].reshape(size, 128)[:, :1] * shrink + jnp.sum(p, axis=1, keepdims=True)
        o = acc[:, hs, :].reshape(size, LATENT) * shrink
        o = o + jnp.dot(p.astype(BF16), pages[:, :LATENT], preferred_element_type=F32)
        o = (o / jnp.where(t == 0.0, 1.0, t)).astype(BF16)
        o = jnp.dot(turn, o, preferred_element_type=F32).astype(BF16)
        packed[n] = o.reshape(NZ, -1, LATENT)
        for b in (2, 1, 3, 0):
            one, dst = packed.at[n, lax.rem(z + b, NZ)], out_ref.at[chip]
            if (a, b) == (0, 0):
                own_lat = pltpu.make_async_copy(one, dst, pool_sems.at[2])
                own_lat.start()
            else:
                lat_copies.append(send(one, dst, lat_ss.at[n * 4 + b], lat_rs.at[n * 4 + b], on(a, b, 0)))
    own_lat.wait()
    for copy in lat_copies:
        copy.wait_recv()
    for copy in w_copies:
        copy.wait()
    while sent:
        sent.pop().wait_send()


def attend(src, page_of, slot_of, rc, lens, table, queries, pool, value_up, out_proj):
    rows, heads, width = queries.shape
    count, page, _ = pool.shape
    ranks = NX * NZ * 2
    moves = page_of.shape[0] // ranks
    dma = pltpu.SemaphoreType.DMA
    return pl.pallas_call(
        attend_kernel,
        out_shape=(
            jax.ShapeDtypeStruct((NX * NZ, rows * heads // (NX * NZ), LATENT), BF16),
            jax.ShapeDtypeStruct(value_up.shape, BF16),
            jax.ShapeDtypeStruct(out_proj.shape, BF16),
        ),
        in_specs=[sspec()] * 5 + [vspec()] * 2 + [aspec()] * 3,
        out_specs=(aspec(), aspec(), aspec()),
        scratch_shapes=[
            pltpu.VMEM(pool.shape, BF16),
            pltpu.VMEM((2, ranks, page // 2, 2 * width), BF16),
            pltpu.VMEM((2, 3, 8, page // 2, 2 * width), BF16),
            pltpu.VMEM((ranks, page, 2 * width), BF16),
            pltpu.VMEM((moves * page, width), BF16),
            pltpu.VMEM((rows * 16, moves * page), F32),
            pltpu.VMEM((rows, heads, LATENT), F32),
            pltpu.VMEM((rows, heads, 128), F32),
            pltpu.VMEM((rows, heads, 128), F32),
            pltpu.VMEM((4, NZ, rows * heads // (NX * NZ), LATENT), BF16),
            pltpu.VMEM(value_up.shape, BF16),
            pltpu.VMEM(out_proj.shape, BF16),
            pltpu.VMEM((rows, 128), jnp.int32),
            pltpu.SMEM((rows, 128), jnp.int32),
            dma((5,)),
            dma((8,)),
            dma((15,)),
            dma((15,)),
            dma((64,)),
            dma((64,)),
            dma((2,)),
            dma((2,)),
            dma((16,)),
            dma((16,)),
        ],
        compiler_params=pltpu.CompilerParams(collective_id=1, has_side_effects=True, vmem_limit_bytes=VMEM_LIMIT),
        name="attend",
    )(src, page_of, slot_of, rc, lens, table, queries, pool, value_up, out_proj)


SUBS = 2


def tail_kernel(
    lat, vu, vu2, wo, wo2, res, gain, gate, up, down, out_ref,
    rl, vus, wos, gus, ds, ho, part, nrm, mid, acc, hid,
    b1, b2, c1, c2, e1, e2, f1, f2,
    in_sems, w_ls, w_ss, w_rs, rs_ss, rs_rs, ag_ss, ag_rs,
):
    me = lax.axis_index("dp")
    core = lax.rem(me, 2)
    chip = me // 2
    x = chip // NZ
    z = lax.rem(chip, NZ)
    cols_all = part.shape[3]
    half = cols_all // 2
    ff = gate.shape[0]

    def device(dx, dz):
        return {"dp": (lax.rem(x + dx + NX, NX) * NZ + lax.rem(z + dz + NZ, NZ)) * 2 + core}

    sibling = {"dp": me + 1 - 2 * core}

    loads = [
        pltpu.make_async_copy(src, dst, in_sems.at[k])
        for k, (src, dst) in enumerate(
            (
                (lat, rl),
                (vu, vus.at[core]),
                (vu2, vus.at[1 - core]),
                (wo, wos.at[core]),
                (wo2, wos.at[1 - core]),
            )
        )
    ]
    for copy in loads:
        copy.start()
    barrier = pltpu.get_barrier_semaphore()
    peers = [(1, 0), (-1, 0), (0, 1), (0, -1)]
    for a, b in peers:
        pl.semaphore_signal(barrier, inc=1, device_id=device(a, b), device_id_type=MESH)
    pl.semaphore_signal(barrier, inc=1, device_id=sibling, device_id_type=MESH)
    pl.semaphore_wait(barrier, len(peers) + 1)

    sent = []

    def send(src, dst, ss, rs, to):
        copy = pltpu.make_async_remote_copy(
            src_ref=src, dst_ref=dst, send_sem=ss, recv_sem=rs, device_id=to, device_id_type=MESH
        )
        copy.start()
        sent.append(copy)
        return copy

    row0 = pl.multiple_of(core * ff, 16)
    row1 = pl.multiple_of(640 + core * ff, 16)
    places = [
        (gate, gus.at[pl.ds(row0, ff), :]),
        (up, gus.at[pl.ds(row1, ff), :]),
        (down, ds.at[pl.ds(row0, ff), :]),
    ]
    w_local, w_remote = [], []

    def start_weights():
        for k, (src, dst) in enumerate(places):
            copy = pltpu.make_async_copy(src, dst, w_ls.at[k])
            copy.start()
            w_local.append(copy)
            w_remote.append(send(src, dst, w_ss.at[k], w_rs.at[k], sibling))

    def weights_ready(*ks):
        for k in ks:
            w_local[k].wait()
            w_remote[k].wait_recv()

    loads[0].wait()
    loads[1].wait()
    loads[2].wait()
    for h in range(4):
        l = rl[:, h * 16 : (h + 1) * 16, :].reshape(256, LATENT)
        ho[:, h * 128 : (h + 1) * 128] = jnp.dot(l, vus[h // 2, h % 2], preferred_element_type=F32).astype(BF16)

    width = half // SUBS
    wing = width // 2

    def reduce_scatter(turn, fill, bufs, finish):
        r1, r2, t1, t2 = bufs

        def chunk(h, phase, i, base, size):
            cs = pl.ds(base, size)
            xi, zi = lax.rem(x + i + NX, NX), lax.rem(z + i + NZ, NZ)
            along_x = (h == 0) == (phase == 0)
            if phase == 0:
                return part.at[xi, :, :, cs] if along_x else part.at[:, zi, :, cs]
            return part.at[xi, z, :, cs] if along_x else part.at[x, zi, :, cs]

        def to(h, phase, i):
            return device(i, 0) if (h == 0) == (phase == 0) else device(0, i)

        def sems(h, s, phase, k):
            at = (((turn * 2 + h) * SUBS + s) * 2 + phase) * 6 + k
            return rs_ss.at[at], rs_rs.at[at]

        def bufs_of(h, s, phase):
            first, second = (r1, r2) if phase == 0 else (t1, t2)
            return first.at[h, s], second.at[h, s]

        state = {}

        def start(h, s, phase):
            base = h * half + s * width
            first, second = bufs_of(h, s, phase)
            lo, hi = base, base + wing
            state[h, s, phase] = [
                send(chunk(h, phase, 2, lo, wing), first.at[0], *sems(h, s, phase, 0), to(h, phase, 1)),
                send(chunk(h, phase, 2, hi, wing), first.at[1], *sems(h, s, phase, 1), to(h, phase, -1)),
                send(chunk(h, phase, 1, hi, wing), second.at[0, ..., pl.ds(wing, wing)], *sems(h, s, phase, 2), to(h, phase, 1)),
                send(chunk(h, phase, -1, lo, wing), second.at[1, ..., pl.ds(0, wing)], *sems(h, s, phase, 3), to(h, phase, -1)),
            ]

        def middle(h, s, phase):
            base = h * half + s * width
            first, second = bufs_of(h, s, phase)
            copies = state[h, s, phase]
            for side, (i, at) in enumerate(((1, 0), (-1, wing))):
                copies[side].wait_recv()
                mine = chunk(h, phase, i, base + at, wing)
                mine[...] = (mine[...].astype(F32) + first[side].astype(F32)).astype(BF16)
                copies.append(
                    send(mine, second.at[side, ..., pl.ds(at, wing)], *sems(h, s, phase, 4 + side), to(h, phase, i))
                )

        def total(h, s, phase):
            base = h * half + s * width
            _, second = bufs_of(h, s, phase)
            for copy in state[h, s, phase][2:]:
                copy.wait_recv()
            mine = chunk(h, phase, 0, base, width)
            value = mine[...].astype(F32) + second[0].astype(F32) + second[1].astype(F32)
            if phase == 0:
                mine[...] = value.astype(BF16)
            else:
                finish(base, width, value)

        order = [(h, s) for s in range(SUBS) for h in range(2)]
        for h, s in order:
            fill(h * half + s * width, width)
            start(h, s, 0)
        if turn == 0:
            start_weights()
            gus[pl.ds(2 * ff, 640 - 2 * ff), :] = jnp.zeros((640 - 2 * ff, cols_all), BF16)
            gus[pl.ds(640 + 2 * ff, 640 - 2 * ff), :] = jnp.zeros((640 - 2 * ff, cols_all), BF16)
        for h, s in order:
            middle(h, s, 0)
        for h, s in order:
            total(h, s, 0)
            start(h, s, 1)
        for h, s in order:
            middle(h, s, 1)
        for h, s in order:
            total(h, s, 1)

    loads[3].wait()
    loads[4].wait()

    def fill_out(base, size):
        cs = pl.ds(base, size)
        v = jnp.dot(ho[:, :256], wos[0, :, cs], preferred_element_type=F32)
        v = v + jnp.dot(ho[:, 256:], wos[1, :, cs], preferred_element_type=F32)
        part[:, :, :, cs] = v.astype(BF16).reshape(NX, NZ, 16, size)

    squares = []

    def finish_out(base, size, value):
        cs = pl.ds(base, size)
        m = res[:, cs].astype(F32) + value
        mid[:, cs] = m
        squares.append(jnp.sum(m * m, axis=1, keepdims=True))

    reduce_scatter(0, fill_out, (b1, b2, c1, c2), finish_out)
    factor = lax.rsqrt(sum(squares) / cols_all + 1e-06)
    nrm[x, z] = (mid[...] * factor * gain[...]).astype(BF16)
    while sent:
        sent.pop().wait_send()

    quarter = half // 2

    def block(h, i, j, lo, size):
        cs = pl.ds(h * half + lo, size)
        dx, dz = (j, i) if h == 0 else (i, j)
        return nrm.at[lax.rem(x + dx + NX, NX), lax.rem(z + dz + NZ, NZ), :, cs]

    def ag_sems(h, k):
        return ag_ss.at[h * 20 + k], ag_rs.at[h * 20 + k]

    def along(h, first, i):
        return device(0, i) if (h == 0) == first else device(i, 0)

    def pass_on(ref, h, k, first, i):
        return send(ref, ref, *ag_sems(h, k), along(h, first, i))

    one, two = {}, {}
    for h in range(2):
        ref = block(h, 0, 0, 0, half)
        one[h] = [pass_on(ref, h, 0, True, 1), pass_on(ref, h, 1, True, -1)]

    def spread(h, n, i):
        ref = block(h, i, 0, 0, half)
        two[h, n] = [pass_on(ref, h, 4 + 4 * n, False, 1), pass_on(ref, h, 5 + 4 * n, False, -1)]

    def forward(h, n, i):
        two[h, n][0].wait_recv()
        two[h, n].append(pass_on(block(h, i, -1, 0, quarter), h, 6 + 4 * n, False, 1))
        two[h, n][1].wait_recv()
        two[h, n].append(pass_on(block(h, i, 1, quarter, quarter), h, 7 + 4 * n, False, -1))

    for h in range(2):
        spread(h, 0, 0)
    for h in range(2):
        one[h][0].wait_recv()
        one[h].append(pass_on(block(h, -1, 0, 0, quarter), h, 2, True, 1))
        one[h][1].wait_recv()
        one[h].append(pass_on(block(h, 1, 0, quarter, quarter), h, 3, True, -1))
        spread(h, 1, -1)
        spread(h, 2, 1)
    for h in range(2):
        forward(h, 0, 0)
    for h in range(2):
        one[h][2].wait_recv()
        one[h][3].wait_recv()
        spread(h, 3, 2)
    for n, i in ((1, -1), (2, 1), (3, 2)):
        for h in range(2):
            forward(h, n, i)
    for h in range(2):
        for n in range(4):
            two[h, n][2].wait_recv()
            two[h, n][3].wait_recv()

    weights_ready(0, 1)
    depth = cols_all // 4

    def up_step(k, carry):
        cs = pl.ds(pl.multiple_of(k * depth, 128), depth)
        v = lax.dot_general(
            nrm[:, :, :, cs].reshape(256, depth), gus[:, cs], (((1,), (1,)), ((), ())), preferred_element_type=F32
        )

        @pl.when(k == 0)
        def _():
            acc[...] = v

        @pl.when(k > 0)
        def _():
            acc[...] += v

        return carry

    lax.fori_loop(0, 4, up_step, 0)
    g = acc[:, :640]
    hid[...] = (g / (1.0 + jnp.exp(-g)) * acc[:, 640:]).astype(BF16)
    weights_ready(2)

    def fill_down(base, size):
        cs = pl.ds(base, size)
        v = jnp.dot(hid[:, : 2 * ff], ds[:, cs], preferred_element_type=F32)
        part[:, :, :, cs] = v.astype(BF16).reshape(NX, NZ, 16, size)

    def finish_down(base, size, value):
        cs = pl.ds(base, size)
        out_ref[:, cs] = (mid[:, cs] + value).astype(BF16)

    reduce_scatter(1, fill_down, (e1, e2, f1, f2), finish_down)
    while sent:
        sent.pop().wait_send()


def tail(lat, value_up, value_up_2, out_proj, out_proj_2, residual, norm_gain, gate_t, up_t, down):
    cols = residual.shape[1]
    ff = gate_t.shape[0]
    width = cols // 2 // SUBS
    rs_bufs = [
        pltpu.VMEM((2, SUBS, 2, 4, 16, width // 2), BF16),
        pltpu.VMEM((2, SUBS, 2, 4, 16, width), BF16),
        pltpu.VMEM((2, SUBS, 2, 16, width // 2), BF16),
        pltpu.VMEM((2, SUBS, 2, 16, width), BF16),
    ]
    n_rs = 2 * 2 * SUBS * 2 * 6
    dma = pltpu.SemaphoreType.DMA
    return pl.pallas_call(
        tail_kernel,
        out_shape=jax.ShapeDtypeStruct(residual.shape, BF16),
        in_specs=[aspec()] * 5 + [vspec()] * 2 + [aspec()] * 3,
        out_specs=vspec(),
        scratch_shapes=[
            pltpu.VMEM((16, 64, LATENT), BF16),
            pltpu.VMEM((2, 2, LATENT, 128), BF16),
            pltpu.VMEM((2, 256, cols), BF16),
            pltpu.VMEM((1280, cols), BF16),
            pltpu.VMEM((2 * ff, cols), BF16),
            pltpu.VMEM((256, 512), BF16),
            pltpu.VMEM((NX, NZ, 16, cols), BF16),
            pltpu.VMEM((NX, NZ, 16, cols), BF16),
            pltpu.VMEM((16, cols), F32),
            pltpu.VMEM((256, 1280), F32),
            pltpu.VMEM((256, 640), BF16),
            *rs_bufs,
            *rs_bufs,
            dma((5,)),
            dma((3,)),
            dma((3,)),
            dma((3,)),
            dma((n_rs,)),
            dma((n_rs,)),
            dma((40,)),
            dma((40,)),
        ],
        compiler_params=pltpu.CompilerParams(collective_id=0, has_side_effects=True, vmem_limit_bytes=VMEM_LIMIT),
        cost_estimate=pl.CostEstimate(flops=12_000_000_000, bytes_accessed=40_000_000, transcendentals=200_000),
        name="tail",
    )(lat, value_up, value_up_2, out_proj, out_proj_2, residual, norm_gain.reshape(1, cols), gate_t, up_t, down)


def body(
    page_pool,
    move_source,
    move_page,
    move_slot,
    row_count,
    lengths,
    page_table,
    queries,
    value_up,
    out_proj,
    residual,
    norm_gain,
    gate_proj,
    up_proj,
    down_proj,
):
    lat, value_up_2, out_proj_2 = attend(
        move_source.reshape(1, -1), move_page, move_slot, row_count, lengths, page_table, queries, page_pool,
        value_up, out_proj,
    )
    return tail(
        lat, value_up, value_up_2, out_proj, out_proj_2, residual, norm_gain, gate_proj.T, up_proj.T, down_proj
    )


def solution(mesh):
    in_specs = (
        P(("rep", "dp"), None, None),
        P("rep", None),
        P("rep"),
        P("rep"),
        P(("rep", "dp")),
        P(("rep", "dp")),
        P(("rep", "dp"), None),
        P(("rep", "dp"), None, None),
        P("dp", None, None),
        P("dp", None),
        P(("rep", "dp"), None),
        P(),
        P(None, "dp"),
        P(None, "dp"),
        P("dp", None),
    )
    out_specs = P(("rep", "dp"), None)
    return jax.shard_map(body, mesh=mesh, in_specs=in_specs, out_specs=out_specs, check_vma=False)
```

```python
import functools

import jax
import jax.numpy as jnp
from jax import lax
from jax.experimental import pallas as pl
from jax.experimental.pallas import tpu as pltpu
from jax.sharding import PartitionSpec as P

LATENT = 512
SOFTMAX_SCALE = 192 ** (-0.5)
LOW = -1e30
MESH = pl.DeviceIdType.MESH
F32 = jnp.float32
BF16 = jnp.bfloat16
VMEM_LIMIT = 60 * 2**20
NX = 4
NZ = 4


def vspec():
    return pl.BlockSpec(memory_space=pltpu.VMEM)


def sspec():
    return pl.BlockSpec(memory_space=pltpu.SMEM)


def aspec():
    return pl.BlockSpec(memory_space=pl.ANY)


def attend_kernel(
    src, page_of, slot_of, rc, lens, table, q_ref, pool_hbm, vu, wo, out_ref, vu_out, wo_out,
    pool, outbox, via, inbox, pages, mult, acc, top, total, packed, vu_box, wo_box, entries_v, entries,
    pool_sems, copy_sems, one_ss, one_rs, two_ss, two_rs, w_ss, w_rs, lat_ss, lat_rs,
):
    me = lax.axis_index("dp")
    core = lax.rem(me, 2)
    chip = me // 2
    x = chip // NZ
    z = lax.rem(chip, NZ)
    rows, heads, width = q_ref.shape
    page = pool.shape[1]
    part = page // 2
    refs = table.shape[1]
    moves = pages.shape[0] // page
    mine = me * moves

    loads = []
    for k in range(8):
        span = pl.ds(k * (pool.shape[0] // 8), pool.shape[0] // 8)
        loads.append(pltpu.make_async_copy(pool_hbm.at[span], pool.at[span], pool_sems.at[k]))
        loads[-1].start()

    def device(a, b, e):
        return (lax.rem(x + a, NX) * NZ + lax.rem(z + b, NZ)) * 2 + lax.rem(core + e, 2)

    def on(a, b, e):
        return {"dp": device(a, b, e)}

    near = [(0, 0, 1)] + [(a, 0, e) for a in (1, 2, 3) for e in (0, 1)] + [(0, b, e) for b in (1, 2, 3) for e in (0, 1)]
    far = [(a, b, 0) for a in (1, 2, 3) for b in (1, 2, 3)]
    barrier = pltpu.get_barrier_semaphore()
    for at in near + far:
        pl.semaphore_signal(barrier, inc=1, device_id=on(*at), device_id_type=MESH)

    row = lax.broadcasted_iota(jnp.int32, (rows, refs), 0)
    pos = lax.broadcasted_iota(jnp.int32, (rows, refs), 1)
    length = jnp.zeros((rows, refs), jnp.int32)
    for r in range(rows):
        length = jnp.where(row == r, jnp.where(r < rc[0], lens[r], 0), length)
    valid = jnp.clip(length - page * pos, 0, page)
    entry = table[...] * 128 + valid
    for i in range(moves):
        entry = jnp.where(table[...] == slot_of[mine + i], 0, entry)
    entries_v[:, :refs] = entry
    to_scalar = pltpu.make_async_copy(entries_v, entries, pool_sems.at[8])
    to_scalar.start()
    pl.semaphore_wait(barrier, len(near + far))
    for copy in loads:
        copy.wait()

    sent = []

    def send(src, dst, ss, rs, to):
        copy = pltpu.make_async_remote_copy(
            src_ref=src, dst_ref=dst, send_sem=ss, recv_sem=rs, device_id=to, device_id_type=MESH
        )
        copy.start()
        sent.append(copy)
        return copy

    def pack(i, first):
        d = first + i
        hits = [src[0, d * moves + j] == me for j in range(moves)]
        named = [page_of[d * moves + j] for j in range(moves)]
        early, late = 0, 0
        for j in range(moves):
            late = jnp.where(hits[j], named[j], late)
            early = jnp.where(hits[moves - 1 - j], named[moves - 1 - j], early)
        one, two = pool[early], pool[late]
        rope = jnp.concatenate([one[:, LATENT:], two[:, LATENT:]], axis=1)
        for h in range(2):
            rs = slice(h * part, (h + 1) * part)
            outbox[h, d, :, :LATENT] = one[rs, :LATENT]
            outbox[h, d, :, LATENT : 2 * LATENT] = two[rs, :LATENT]
            outbox[h, d, :, 2 * LATENT :] = rope[rs]
        return first

    one_copies = {}
    final = {}
    local = []

    def deliver(h, a, b, e, src):
        origin = (lax.rem(x + (NX - a if h == 0 else 0), NX) * NZ + lax.rem(z + (0 if h == 0 else NZ - b), NZ)) * 2 + core
        dst = inbox.at[origin, pl.ds(h * part, part), :]
        at = ((a * NZ + b) * 2 + e) * 2 + h
        da, db = (0, b) if h == 0 else (a, 0)
        if (da, db, e) == (0, 0, 0):
            copy = pltpu.make_async_copy(src, dst, copy_sems.at[len(local)])
            copy.start()
            local.append(copy)
        else:
            final[at] = send(src, dst, two_ss.at[at], two_rs.at[at], on(da, db, e))

    for n, a in enumerate((2, 1, 3, 0)):
        xa = lax.rem(x + a, NX)
        lax.fori_loop(0, 8, pack, xa * 8)
        if a:
            one_copies[0, a] = send(
                outbox.at[0, pl.ds(xa * 8, 8)], via.at[0, a - 1], one_ss.at[a - 1], one_rs.at[a - 1], on(a, 0, 0)
            )
        for b in (2, 1, 3):
            zb = lax.rem(z + b, NZ)
            at = 3 + (b - 1) * 4 + n
            one_copies[1, b, n] = send(
                outbox.at[1, pl.ds(xa * 8 + zb * 2, 2)],
                via.at[1, b - 1, pl.ds(xa * 2, 2)],
                one_ss.at[at],
                one_rs.at[at],
                on(0, b, 0),
            )

    def second_hop(k):
        if k:
            one_copies[0, k].wait_recv()
            for n in range(4):
                one_copies[1, k, n].wait_recv()
        for o in (2, 1, 3, 0):
            for e in range(2):
                ce = lax.rem(core + e, 2)
                zo, xo = lax.rem(z + o, NZ), lax.rem(x + o, NX)
                deliver(0, k, o, e, via.at[0, k - 1, zo * 2 + ce] if k else outbox.at[0, x * 8 + zo * 2 + ce])
                deliver(1, o, k, e, via.at[1, k - 1, xo * 2 + ce] if k else outbox.at[1, xo * 8 + z * 2 + ce])

    def attend_row(r, carry):
        q = q_ref[r]
        group = 8
        col = lax.broadcasted_iota(jnp.int32, (1, page * group), 1)
        keys, scores = [], []
        for g in range(refs // group):
            es = [entries[r, g * group + i] for i in range(group)]
            k = jnp.concatenate([pool[e >> 7] for e in es], axis=0)
            limit = jnp.zeros((1, page * group), jnp.int32)
            for i, e in enumerate(es):
                limit = jnp.where((col >> 6) == i, e & 127, limit)
            s = lax.dot_general(q, k, (((1,), (1,)), ((), ())), preferred_element_type=F32) * SOFTMAX_SCALE
            scores.append(jnp.where((col & 63) < limit, s, LOW))
            keys.append(k)
        m = functools.reduce(jnp.maximum, [jnp.max(s, axis=1, keepdims=True) for s in scores])
        t = jnp.zeros((heads, 1), F32)
        o = jnp.zeros((heads, LATENT), F32)
        for s, k in zip(scores, keys):
            p = jnp.exp(s - m)
            t = t + jnp.sum(p, axis=1, keepdims=True)
            o = o + jnp.dot(p.astype(BF16), k[:, :LATENT], preferred_element_type=F32)
        some = m > 0.5 * LOW
        acc[r] = jnp.where(some, o, 0.0)
        top[r] = jnp.broadcast_to(m, (heads, 128))
        total[r] = jnp.broadcast_to(jnp.where(some, t, 0.0), (heads, 128))
        return carry

    w_copies = [
        send(vu, vu_box, w_ss.at[0], w_rs.at[0], on(0, 0, 1)),
        send(wo, wo_box, w_ss.at[1], w_rs.at[1], on(0, 0, 1)),
    ]
    second_hop(0)
    to_scalar.wait()
    lax.fori_loop(0, 5, attend_row, 0)
    second_hop(1)
    second_hop(3)
    lax.fori_loop(5, 9, attend_row, 0)
    second_hop(2)
    lax.fori_loop(9, rows, attend_row, 0)

    for k, (box, out) in enumerate(((vu_box, vu_out), (wo_box, wo_out))):
        w_copies[k].wait_recv()
        w_copies[k] = pltpu.make_async_copy(box, out, pool_sems.at[k])
        w_copies[k].start()

    block = 16
    whole = (valid == page).astype(F32)
    some = ((valid > 0) & (valid < page)).astype(F32)
    last = jnp.sum(some * valid.astype(F32), axis=1, keepdims=True)
    off = lax.broadcasted_iota(jnp.int32, (rows, page), 1).astype(F32)
    inside = (off < last).astype(F32)
    for i in range(0, moves, 2):
        pair = []
        for j in (i, i + 1):
            hit = (table[...] == slot_of[mine + j]).astype(F32)
            pair.append(
                jnp.sum(hit * whole, axis=1, keepdims=True) + jnp.sum(hit * some, axis=1, keepdims=True) * inside
            )
        pair = jnp.concatenate(pair, axis=1)
        for r in range(rows):
            mult[r * block : (r + 1) * block, i * page : (i + 2) * page] = jnp.broadcast_to(
                pair[r : r + 1], (block, 2 * page)
            )

    places = []
    for i in range(moves):
        again = 0
        for j in range(i):
            again = again + (src[0, mine + i] == src[0, mine + j]).astype(jnp.int32)
        places.append((src[0, mine + i], again))

    for copy in local:
        copy.wait()
    for copy in final.values():
        copy.wait_recv()

    rope = width - LATENT
    for i, (rank, again) in enumerate(places):
        pair = inbox[rank]
        first = again == 0
        here = slice(i * page, (i + 1) * page)
        pages[here, :LATENT] = jnp.where(first, pair[:, :LATENT], pair[:, LATENT : 2 * LATENT])
        pages[here, LATENT:] = jnp.where(
            first, pair[:, 2 * LATENT : 2 * LATENT + rope], pair[:, 2 * LATENT + rope :]
        )

    size = rows * block
    to = lax.broadcasted_iota(jnp.int32, (size, size), 0)
    frm = lax.broadcasted_iota(jnp.int32, (size, size), 1)
    turn = (frm == (to % rows) * block + to // rows).astype(BF16)
    lat_copies = []
    for n, a in enumerate((2, 0, 1, 3)):
        xa = lax.rem(x + a, NX)
        hs = pl.ds(pl.multiple_of(xa * block, block), block)
        q = q_ref[:, hs, :].reshape(size, width)
        s = lax.dot_general(q, pages[...], (((1,), (1,)), ((), ())), preferred_element_type=F32) * SOFTMAX_SCALE
        times = mult[...]
        s = jnp.where(times > 0.0, s, LOW)
        old = top[:, hs, :].reshape(size, 128)[:, :1]
        m = jnp.maximum(old, jnp.max(s, axis=1, keepdims=True))
        shrink = jnp.exp(old - m)
        p = jnp.exp(s - m) * times
        t = total[:, hs, :].reshape(size, 128)[:, :1] * shrink + jnp.sum(p, axis=1, keepdims=True)
        o = acc[:, hs, :].reshape(size, LATENT) * shrink
        o = o + jnp.dot(p.astype(BF16), pages[:, :LATENT], preferred_element_type=F32)
        o = (o / jnp.where(t == 0.0, 1.0, t)).astype(BF16)
        o = jnp.dot(turn, o, preferred_element_type=F32).astype(BF16)
        packed[n] = o.reshape(NZ, -1, LATENT)
        for b in (2, 1, 3, 0):
            one, dst = packed.at[n, lax.rem(z + b, NZ)], out_ref.at[chip]
            if (a, b) == (0, 0):
                own_lat = pltpu.make_async_copy(one, dst, pool_sems.at[2])
                own_lat.start()
            else:
                lat_copies.append(send(one, dst, lat_ss.at[n * 4 + b], lat_rs.at[n * 4 + b], on(a, b, 0)))
    own_lat.wait()
    for copy in lat_copies:
        copy.wait_recv()
    for copy in w_copies:
        copy.wait()
    while sent:
        sent.pop().wait_send()


def attend(src, page_of, slot_of, rc, lens, table, queries, pool, value_up, out_proj):
    rows, heads, width = queries.shape
    count, page, _ = pool.shape
    ranks = NX * NZ * 2
    moves = page_of.shape[0] // ranks
    dma = pltpu.SemaphoreType.DMA
    return pl.pallas_call(
        attend_kernel,
        out_shape=(
            jax.ShapeDtypeStruct((NX * NZ, rows * heads // (NX * NZ), LATENT), BF16),
            jax.ShapeDtypeStruct(value_up.shape, BF16),
            jax.ShapeDtypeStruct(out_proj.shape, BF16),
        ),
        in_specs=[sspec()] * 5 + [vspec()] * 2 + [aspec()] * 3,
        out_specs=(aspec(), aspec(), aspec()),
        scratch_shapes=[
            pltpu.VMEM(pool.shape, BF16),
            pltpu.VMEM((2, ranks, page // 2, 2 * width), BF16),
            pltpu.VMEM((2, 3, 8, page // 2, 2 * width), BF16),
            pltpu.VMEM((ranks, page, 2 * width), BF16),
            pltpu.VMEM((moves * page, width), BF16),
            pltpu.VMEM((rows * 16, moves * page), F32),
            pltpu.VMEM((rows, heads, LATENT), F32),
            pltpu.VMEM((rows, heads, 128), F32),
            pltpu.VMEM((rows, heads, 128), F32),
            pltpu.VMEM((4, NZ, rows * heads // (NX * NZ), LATENT), BF16),
            pltpu.VMEM(value_up.shape, BF16),
            pltpu.VMEM(out_proj.shape, BF16),
            pltpu.VMEM((rows, 128), jnp.int32),
            pltpu.SMEM((rows, 128), jnp.int32),
            dma((9,)),
            dma((8,)),
            dma((15,)),
            dma((15,)),
            dma((64,)),
            dma((64,)),
            dma((2,)),
            dma((2,)),
            dma((16,)),
            dma((16,)),
        ],
        compiler_params=pltpu.CompilerParams(collective_id=1, has_side_effects=True, vmem_limit_bytes=VMEM_LIMIT),
        name="attend",
    )(src, page_of, slot_of, rc, lens, table, queries, pool, value_up, out_proj)


SUBS = 2


def tail_kernel(
    lat, vu, vu2, wo, wo2, res, gain, gate, up, down, out_ref,
    rl, vus, wos, gus, ds, ho, part, nrm, mid, acc, hid,
    b1, b2, c1, c2, e1, e2, f1, f2,
    in_sems, w_ls, w_ss, w_rs, rs_ss, rs_rs, ag_ss, ag_rs,
):
    me = lax.axis_index("dp")
    core = lax.rem(me, 2)
    chip = me // 2
    x = chip // NZ
    z = lax.rem(chip, NZ)
    cols_all = part.shape[3]
    half = cols_all // 2
    ff = gate.shape[0]

    def device(dx, dz):
        return {"dp": (lax.rem(x + dx + NX, NX) * NZ + lax.rem(z + dz + NZ, NZ)) * 2 + core}

    sibling = {"dp": me + 1 - 2 * core}

    width = half // SUBS
    wing = width // 2
    order = [(h, s) for s in range(SUBS) for h in range(2)]

    barrier = pltpu.get_barrier_semaphore()
    peers = [(1, 0), (-1, 0), (0, 1), (0, -1)]
    for a, b in peers:
        pl.semaphore_signal(barrier, inc=1, device_id=device(a, b), device_id_type=MESH)
    pl.semaphore_signal(barrier, inc=1, device_id=sibling, device_id_type=MESH)
    pairs = [(lat, rl), (vu, vus.at[core]), (vu2, vus.at[1 - core])]
    for h, s in order:
        cs = pl.ds(h * half + s * width, width)
        pairs += [(wo.at[:, cs], wos.at[core, :, cs]), (wo2.at[:, cs], wos.at[1 - core, :, cs])]
    loads = [pltpu.make_async_copy(src, dst, in_sems.at[k]) for k, (src, dst) in enumerate(pairs)]
    for copy in loads:
        copy.start()

    sent = []

    def send(src, dst, ss, rs, to):
        copy = pltpu.make_async_remote_copy(
            src_ref=src, dst_ref=dst, send_sem=ss, recv_sem=rs, device_id=to, device_id_type=MESH
        )
        copy.start()
        sent.append(copy)
        return copy

    row0 = pl.multiple_of(core * ff, 16)
    row1 = pl.multiple_of(640 + core * ff, 16)
    places = [
        (gate, gus.at[pl.ds(row0, ff), :]),
        (up, gus.at[pl.ds(row1, ff), :]),
        (down, ds.at[pl.ds(row0, ff), :]),
    ]
    w_local, w_remote = [], []

    def start_weights():
        for k, (src, dst) in enumerate(places):
            copy = pltpu.make_async_copy(src, dst, w_ls.at[k])
            copy.start()
            w_local.append(copy)
            w_remote.append(send(src, dst, w_ss.at[k], w_rs.at[k], sibling))

    def weights_ready(*ks):
        for k in ks:
            w_local[k].wait()
            w_remote[k].wait_recv()

    loads[0].wait()
    loads[1].wait()
    loads[2].wait()
    for h in range(4):
        l = rl[:, h * 16 : (h + 1) * 16, :].reshape(256, LATENT)
        ho[:, h * 128 : (h + 1) * 128] = jnp.dot(l, vus[h // 2, h % 2], preferred_element_type=F32).astype(BF16)

    def reduce_scatter(turn, fill, bufs, finish, after=None):
        r1, r2, t1, t2 = bufs

        def chunk(h, phase, i, base, size):
            cs = pl.ds(base, size)
            xi, zi = lax.rem(x + i + NX, NX), lax.rem(z + i + NZ, NZ)
            along_x = (h == 0) == (phase == 0)
            if phase == 0:
                return part.at[xi, :, :, cs] if along_x else part.at[:, zi, :, cs]
            return part.at[xi, z, :, cs] if along_x else part.at[x, zi, :, cs]

        def to(h, phase, i):
            return device(i, 0) if (h == 0) == (phase == 0) else device(0, i)

        def sems(h, s, phase, k):
            at = (((turn * 2 + h) * SUBS + s) * 2 + phase) * 6 + k
            return rs_ss.at[at], rs_rs.at[at]

        def bufs_of(h, s, phase):
            first, second = (r1, r2) if phase == 0 else (t1, t2)
            return first.at[h, s], second.at[h, s]

        state = {}

        def start(h, s, phase):
            base = h * half + s * width
            first, second = bufs_of(h, s, phase)
            lo, hi = base, base + wing
            state[h, s, phase] = [
                send(chunk(h, phase, 2, lo, wing), first.at[0], *sems(h, s, phase, 0), to(h, phase, 1)),
                send(chunk(h, phase, 2, hi, wing), first.at[1], *sems(h, s, phase, 1), to(h, phase, -1)),
                send(chunk(h, phase, 1, hi, wing), second.at[0, ..., pl.ds(wing, wing)], *sems(h, s, phase, 2), to(h, phase, 1)),
                send(chunk(h, phase, -1, lo, wing), second.at[1, ..., pl.ds(0, wing)], *sems(h, s, phase, 3), to(h, phase, -1)),
            ]

        def middle(h, s, phase):
            base = h * half + s * width
            first, second = bufs_of(h, s, phase)
            copies = state[h, s, phase]
            for side, (i, at) in enumerate(((1, 0), (-1, wing))):
                copies[side].wait_recv()
                mine = chunk(h, phase, i, base + at, wing)
                mine[...] = (mine[...].astype(F32) + first[side].astype(F32)).astype(BF16)
                copies.append(
                    send(mine, second.at[side, ..., pl.ds(at, wing)], *sems(h, s, phase, 4 + side), to(h, phase, i))
                )

        def total(h, s, phase):
            base = h * half + s * width
            _, second = bufs_of(h, s, phase)
            for copy in state[h, s, phase][2:]:
                copy.wait_recv()
            mine = chunk(h, phase, 0, base, width)
            value = mine[...].astype(F32) + second[0].astype(F32) + second[1].astype(F32)
            if phase == 0:
                mine[...] = value.astype(BF16)
            else:
                finish(base, width, value)

        for n, (h, s) in enumerate(order):
            fill(n, h * half + s * width, width)
            if turn == 0 and n == 0:
                pl.semaphore_wait(barrier, len(peers) + 1)
            start(h, s, 0)
        if turn == 0:
            start_weights()
            gus[pl.ds(2 * ff, 640 - 2 * ff), :] = jnp.zeros((640 - 2 * ff, cols_all), BF16)
            gus[pl.ds(640 + 2 * ff, 640 - 2 * ff), :] = jnp.zeros((640 - 2 * ff, cols_all), BF16)
        for h, s in order:
            middle(h, s, 0)
        for h, s in order:
            total(h, s, 0)
            start(h, s, 1)
        for h, s in order:
            middle(h, s, 1)
        for h, s in order:
            total(h, s, 1)
            if after is not None and h == 1:
                after(s)


    def fill_out(n, base, size):
        loads[3 + 2 * n].wait()
        loads[4 + 2 * n].wait()
        cs = pl.ds(base, size)
        v = jnp.dot(ho[:, :256], wos[0, :, cs], preferred_element_type=F32)
        v = v + jnp.dot(ho[:, 256:], wos[1, :, cs], preferred_element_type=F32)
        part[:, :, :, cs] = v.astype(BF16).reshape(NX, NZ, 16, size)

    squares = []

    def finish_out(base, size, value):
        cs = pl.ds(base, size)
        m = res[:, cs].astype(F32) + value
        mid[:, cs] = m
        squares.append(jnp.sum(m * m, axis=1, keepdims=True))
        nrm[x, z, :, cs] = (m * gain[:, cs]).astype(BF16)

    def block(h, s, i, j, piece):
        base = h * half + s * width
        rest = wing + (128 if (h, s) == (1, SUBS - 1) else 0)
        lo, size = {"all": (0, wing + rest), "low": (0, wing), "high": (wing, rest)}[piece]
        dx, dz = (j, i) if h == 0 else (i, j)
        return nrm.at[lax.rem(x + dx + NX, NX), lax.rem(z + dz + NZ, NZ), :, pl.ds(base + lo, size)]

    one, two = {}, {}

    def pass_on(h, s, i, j, piece, k, first, step):
        ref = block(h, s, i, j, piece)
        at = (h * SUBS + s) * 20 + k
        to = device(0, step) if (h == 0) == first else device(step, 0)
        return send(ref, ref, ag_ss.at[at], ag_rs.at[at], to)

    def spread(h, s, n, i):
        two[h, s, n] = [pass_on(h, s, i, 0, "all", 4 + 4 * n, False, 1), pass_on(h, s, i, 0, "all", 5 + 4 * n, False, -1)]

    def forward(s, n, i):
        for h in range(2):
            got = two[h, s, n]
            got[0].wait_recv()
            got.append(pass_on(h, s, i, -1, "low", 6 + 4 * n, False, 1))
            got[1].wait_recv()
            got.append(pass_on(h, s, i, 1, "high", 7 + 4 * n, False, -1))

    def gather_start(s):
        if s == SUBS - 1:
            scale = lax.rsqrt(sum(squares) / cols_all + 1e-06)
            rough = scale.astype(BF16).astype(F32)
            lane = lax.broadcasted_iota(jnp.int32, (16, 128), 1)
            nrm[x, z, :, cols_all:] = jnp.where(lane < 64, rough, scale - rough).astype(BF16)
        for h in range(2):
            one[h, s] = [pass_on(h, s, 0, 0, "all", 0, True, 1), pass_on(h, s, 0, 0, "all", 1, True, -1)]
        for h in range(2):
            spread(h, s, 0, 0)

    def gather_next(s):
        for h in range(2):
            got = one[h, s]
            got[0].wait_recv()
            got.append(pass_on(h, s, -1, 0, "low", 2, True, 1))
            got[1].wait_recv()
            got.append(pass_on(h, s, 1, 0, "high", 3, True, -1))
            spread(h, s, 1, -1)
            spread(h, s, 2, 1)

    def gather_last(s):
        for h in range(2):
            one[h, s][2].wait_recv()
            one[h, s][3].wait_recv()
            spread(h, s, 3, 2)

    def gathered(s):
        for h in range(2):
            for n in range(4):
                two[h, s, n][2].wait_recv()
                two[h, s, n][3].wait_recv()

    def up_step(h, s):
        cs = pl.ds(h * half + s * width, width)
        v = lax.dot_general(
            nrm[:, :, :, cs].reshape(256, width), gus[:, cs], (((1,), (1,)), ((), ())), preferred_element_type=F32
        )
        if (h, s) == (0, 0):
            acc[...] = v
        else:
            acc[...] += v

    reduce_scatter(0, fill_out, (b1, b2, c1, c2), finish_out, gather_start)
    gather_next(0)
    gather_next(1)
    forward(0, 0, 0)
    gather_last(0)
    forward(1, 0, 0)
    gather_last(1)
    forward(0, 1, -1)
    forward(0, 2, 1)
    forward(1, 1, -1)
    forward(0, 3, 2)
    forward(1, 2, 1)
    gathered(0)
    weights_ready(0, 1)
    up_step(0, 0)
    forward(1, 3, 2)
    up_step(1, 0)
    gathered(1)
    up_step(0, 1)
    up_step(1, 1)
    scales = nrm[:, :, :, cols_all:].reshape(256, 128).astype(F32)
    scale = scales[:, :1] + scales[:, 64:65]
    g = acc[:, :640] * scale
    hid[...] = (g / (1.0 + jnp.exp(-g)) * (acc[:, 640:] * scale)).astype(BF16)
    while sent:
        sent.pop().wait_send()
    weights_ready(2)

    def fill_down(n, base, size):
        cs = pl.ds(base, size)
        v = jnp.dot(hid[:, : 2 * ff], ds[:, cs], preferred_element_type=F32)
        part[:, :, :, cs] = v.astype(BF16).reshape(NX, NZ, 16, size)

    def finish_down(base, size, value):
        cs = pl.ds(base, size)
        out_ref[:, cs] = (mid[:, cs] + value).astype(BF16)

    reduce_scatter(1, fill_down, (e1, e2, f1, f2), finish_down)
    while sent:
        sent.pop().wait_send()


def tail(lat, value_up, value_up_2, out_proj, out_proj_2, residual, norm_gain, gate_t, up_t, down):
    cols = residual.shape[1]
    ff = gate_t.shape[0]
    width = cols // 2 // SUBS
    rs_bufs = [
        pltpu.VMEM((2, SUBS, 2, 4, 16, width // 2), BF16),
        pltpu.VMEM((2, SUBS, 2, 4, 16, width), BF16),
        pltpu.VMEM((2, SUBS, 2, 16, width // 2), BF16),
        pltpu.VMEM((2, SUBS, 2, 16, width), BF16),
    ]
    n_rs = 2 * 2 * SUBS * 2 * 6
    dma = pltpu.SemaphoreType.DMA
    return pl.pallas_call(
        tail_kernel,
        out_shape=jax.ShapeDtypeStruct(residual.shape, BF16),
        in_specs=[aspec()] * 5 + [vspec()] * 2 + [aspec()] * 3,
        out_specs=vspec(),
        scratch_shapes=[
            pltpu.VMEM((16, 64, LATENT), BF16),
            pltpu.VMEM((2, 2, LATENT, 128), BF16),
            pltpu.VMEM((2, 256, cols), BF16),
            pltpu.VMEM((1280, cols), BF16),
            pltpu.VMEM((2 * ff, cols), BF16),
            pltpu.VMEM((256, 512), BF16),
            pltpu.VMEM((NX, NZ, 16, cols), BF16),
            pltpu.VMEM((NX, NZ, 16, cols + 128), BF16),
            pltpu.VMEM((16, cols), F32),
            pltpu.VMEM((256, 1280), F32),
            pltpu.VMEM((256, 640), BF16),
            *rs_bufs,
            *rs_bufs,
            dma((3 + 4 * SUBS,)),
            dma((3,)),
            dma((3,)),
            dma((3,)),
            dma((n_rs,)),
            dma((n_rs,)),
            dma((40 * SUBS,)),
            dma((40 * SUBS,)),
        ],
        compiler_params=pltpu.CompilerParams(collective_id=0, has_side_effects=True, vmem_limit_bytes=VMEM_LIMIT),
        cost_estimate=pl.CostEstimate(flops=12_000_000_000, bytes_accessed=40_000_000, transcendentals=200_000),
        name="tail",
    )(lat, value_up, value_up_2, out_proj, out_proj_2, residual, norm_gain.reshape(1, cols), gate_t, up_t, down)


def body(
    page_pool,
    move_source,
    move_page,
    move_slot,
    row_count,
    lengths,
    page_table,
    queries,
    value_up,
    out_proj,
    residual,
    norm_gain,
    gate_proj,
    up_proj,
    down_proj,
):
    lat, value_up_2, out_proj_2 = attend(
        move_source.reshape(1, -1), move_page, move_slot, row_count, lengths, page_table, queries, page_pool,
        value_up, out_proj,
    )
    return tail(
        lat, value_up, value_up_2, out_proj, out_proj_2, residual, norm_gain, gate_proj.T, up_proj.T, down_proj
    )


def solution(mesh):
    in_specs = (
        P(("rep", "dp"), None, None),
        P("rep", None),
        P("rep"),
        P("rep"),
        P(("rep", "dp")),
        P(("rep", "dp")),
        P(("rep", "dp"), None),
        P(("rep", "dp"), None, None),
        P("dp", None, None),
        P("dp", None),
        P(("rep", "dp"), None),
        P(),
        P(None, "dp"),
        P(None, "dp"),
        P("dp", None),
    )
    out_specs = P(("rep", "dp"), None)
    return jax.shard_map(body, mesh=mesh, in_specs=in_specs, out_specs=out_specs, check_vma=False)
```

```python
import functools

import jax
import jax.numpy as jnp
from jax import lax
from jax.experimental import pallas as pl
from jax.experimental.pallas import tpu as pltpu
from jax.sharding import PartitionSpec as P

LATENT = 512
SOFTMAX_SCALE = 192 ** (-0.5)
LOW = -1e30
MESH = pl.DeviceIdType.MESH
F32 = jnp.float32
BF16 = jnp.bfloat16
VMEM_LIMIT = 60 * 2**20
NX = 4
NZ = 4


def vspec():
    return pl.BlockSpec(memory_space=pltpu.VMEM)


def sspec():
    return pl.BlockSpec(memory_space=pltpu.SMEM)


def aspec():
    return pl.BlockSpec(memory_space=pl.ANY)


SUBS = 2


def layer_kernel(
    src, page_of, slot_of, rc, lens, table, q_hbm, pool_hbm, vu, wo, res, gain, gate, up, down,
    out_ref, gate_2, up_2, down_2,
    via, inbox, rl, nrm, vus, wos, packed, entries_v, entries, b1, b2, c1, c2,
    pool_sems, copy_sems, one_ss, one_rs, two_ss, two_rs, w_ls, w_ss, w_rs, lat_ss, lat_rs, in_sems,
    rs_ss, rs_rs, ag_ss, ag_rs,
):
    me = lax.axis_index("dp")
    core = lax.rem(me, 2)
    chip = me // 2
    x = chip // NZ
    z = lax.rem(chip, NZ)
    rows, heads, width = q_hbm.shape
    count, page, _ = pool_hbm.shape
    part = page // 2
    refs = table.shape[1]
    moves = page_of.shape[0] // (NX * NZ * 2)
    mine = me * moves

    def device(a, b, e):
        return (lax.rem(x + a, NX) * NZ + lax.rem(z + b, NZ)) * 2 + lax.rem(core + e, 2)

    def on(a, b, e):
        return {"dp": device(a, b, e)}

    near = [(0, 0, 1)] + [(a, 0, e) for a in (1, 2, 3) for e in (0, 1)] + [(0, b, e) for b in (1, 2, 3) for e in (0, 1)]
    far = [(a, b, 0) for a in (1, 2, 3) for b in (1, 2, 3)]
    barrier = pltpu.get_barrier_semaphore()
    for at in near + far:
        pl.semaphore_signal(barrier, inc=1, device_id=on(*at), device_id_type=MESH)

    sent = []

    def remote(src, dst, ss, rs, to):
        return pltpu.make_async_remote_copy(
            src_ref=src, dst_ref=dst, send_sem=ss, recv_sem=rs, device_id=to, device_id_type=MESH
        )

    def send(src, dst, ss, rs, to):
        copy = remote(src, dst, ss, rs, to)
        copy.start()
        sent.append(copy)
        return copy

    head_groups = (2, 0, 1, 3)

    def weight_copies():
        refs_of = ((vu, vus.at[core]), (wo, wos.at[core]), (gate, gate_2), (up, up_2), (down, down_2))
        return [remote(one, to, w_ss.at[k], w_rs.at[k], on(0, 0, 1)) for k, (one, to) in enumerate(refs_of)]

    def weight_places():
        return [
            pltpu.make_async_copy(one, to, w_ls.at[k])
            for k, (one, to) in enumerate(((vu, vus.at[core]), (wo, wos.at[core])))
        ]

    def latent_copies(n):
        copies = []
        for b in (2, 1, 3, 0):
            one, to = packed.at[n, lax.rem(z + b, NZ)], rl.at[chip]
            if (head_groups[n], b) == (0, 0):
                copies.append(pltpu.make_async_copy(one, to, pool_sems.at[0]))
            else:
                at = n * 4 + b
                copies.append(remote(one, to, lat_ss.at[at], lat_rs.at[at], on(head_groups[n], b, 0)))
        return copies

    def attention(pool, outbox, pages, mult, acc, top, total, q_ref):
        loads = []
        for k in range(8):
            span = pl.ds(k * (count // 8), count // 8)
            loads.append(pltpu.make_async_copy(pool_hbm.at[span], pool.at[span], pool_sems.at[k]))
        loads.append(pltpu.make_async_copy(q_hbm, q_ref, pool_sems.at[9]))
        for copy in loads:
            copy.start()

        row = lax.broadcasted_iota(jnp.int32, (rows, refs), 0)
        pos = lax.broadcasted_iota(jnp.int32, (rows, refs), 1)
        length = jnp.zeros((rows, refs), jnp.int32)
        for r in range(rows):
            length = jnp.where(row == r, jnp.where(r < rc[0], lens[r], 0), length)
        valid = jnp.clip(length - page * pos, 0, page)
        entry = table[...] * 128 + valid
        for i in range(moves):
            entry = jnp.where(table[...] == slot_of[mine + i], 0, entry)
        entries_v[:, :refs] = entry
        to_scalar = pltpu.make_async_copy(entries_v, entries, pool_sems.at[8])
        to_scalar.start()

        pl.semaphore_wait(barrier, len(near + far))
        for copy in loads:
            copy.wait()

        def pack(i, first):
            d = first + i
            hits = [src[0, d * moves + j] == me for j in range(moves)]
            named = [page_of[d * moves + j] for j in range(moves)]
            early, late = 0, 0
            for j in range(moves):
                late = jnp.where(hits[j], named[j], late)
                early = jnp.where(hits[moves - 1 - j], named[moves - 1 - j], early)
            one, two = pool[early], pool[late]
            rope = jnp.concatenate([one[:, LATENT:], two[:, LATENT:]], axis=1)
            for h in range(2):
                rs = slice(h * part, (h + 1) * part)
                outbox[h, d, :, :LATENT] = one[rs, :LATENT]
                outbox[h, d, :, LATENT : 2 * LATENT] = two[rs, :LATENT]
                outbox[h, d, :, 2 * LATENT :] = rope[rs]
            return first

        one_copies = {}
        final = {}
        local = []

        def deliver(h, a, b, e, src):
            origin = (lax.rem(x + (NX - a if h == 0 else 0), NX) * NZ + lax.rem(z + (0 if h == 0 else NZ - b), NZ)) * 2 + core
            dst = inbox.at[origin, pl.ds(h * part, part), :]
            at = ((a * NZ + b) * 2 + e) * 2 + h
            da, db = (0, b) if h == 0 else (a, 0)
            if (da, db, e) == (0, 0, 0):
                copy = pltpu.make_async_copy(src, dst, copy_sems.at[len(local)])
                copy.start()
                local.append(copy)
            else:
                final[at] = send(src, dst, two_ss.at[at], two_rs.at[at], on(da, db, e))

        for n, a in enumerate((2, 1, 3, 0)):
            xa = lax.rem(x + a, NX)
            lax.fori_loop(0, 8, pack, xa * 8)
            if a:
                one_copies[0, a] = send(
                    outbox.at[0, pl.ds(xa * 8, 8)], via.at[0, a - 1], one_ss.at[a - 1], one_rs.at[a - 1], on(a, 0, 0)
                )
            for b in (2, 1, 3):
                zb = lax.rem(z + b, NZ)
                at = 3 + (b - 1) * 4 + n
                one_copies[1, b, n] = send(
                    outbox.at[1, pl.ds(xa * 8 + zb * 2, 2)],
                    via.at[1, b - 1, pl.ds(xa * 2, 2)],
                    one_ss.at[at],
                    one_rs.at[at],
                    on(0, b, 0),
                )

        def second_hop(k):
            if k:
                one_copies[0, k].wait_recv()
                for n in range(4):
                    one_copies[1, k, n].wait_recv()
            for o in (2, 1, 3, 0):
                for e in range(2):
                    ce = lax.rem(core + e, 2)
                    zo, xo = lax.rem(z + o, NZ), lax.rem(x + o, NX)
                    deliver(0, k, o, e, via.at[0, k - 1, zo * 2 + ce] if k else outbox.at[0, x * 8 + zo * 2 + ce])
                    deliver(1, o, k, e, via.at[1, k - 1, xo * 2 + ce] if k else outbox.at[1, xo * 8 + z * 2 + ce])

        def attend_row(r, carry):
            q = q_ref[r]
            group = 8
            col = lax.broadcasted_iota(jnp.int32, (1, page * group), 1)
            keys, scores = [], []
            for g in range(refs // group):
                es = [entries[r, g * group + i] for i in range(group)]
                k = jnp.concatenate([pool[e >> 7] for e in es], axis=0)
                limit = jnp.zeros((1, page * group), jnp.int32)
                for i, e in enumerate(es):
                    limit = jnp.where((col >> 6) == i, e & 127, limit)
                s = lax.dot_general(q, k, (((1,), (1,)), ((), ())), preferred_element_type=F32) * SOFTMAX_SCALE
                scores.append(jnp.where((col & 63) < limit, s, LOW))
                keys.append(k)
            m = functools.reduce(jnp.maximum, [jnp.max(s, axis=1, keepdims=True) for s in scores])
            t = jnp.zeros((heads, 1), F32)
            o = jnp.zeros((heads, LATENT), F32)
            for s, k in zip(scores, keys):
                p = jnp.exp(s - m)
                t = t + jnp.sum(p, axis=1, keepdims=True)
                o = o + jnp.dot(p.astype(BF16), k[:, :LATENT], preferred_element_type=F32)
            some = m > 0.5 * LOW
            acc[r] = jnp.where(some, o, 0.0)
            top[r] = jnp.broadcast_to(m, (heads, 128))
            total[r] = jnp.broadcast_to(jnp.where(some, t, 0.0), (heads, 128))
            return carry

        for copy in weight_copies() + weight_places():
            copy.start()
        second_hop(0)
        to_scalar.wait()
        lax.fori_loop(0, 5, attend_row, 0)
        second_hop(1)
        second_hop(3)
        lax.fori_loop(5, 9, attend_row, 0)
        second_hop(2)
        lax.fori_loop(9, rows, attend_row, 0)

        block = 16
        whole = (valid == page).astype(F32)
        some = ((valid > 0) & (valid < page)).astype(F32)
        last = jnp.sum(some * valid.astype(F32), axis=1, keepdims=True)
        off = lax.broadcasted_iota(jnp.int32, (rows, page), 1).astype(F32)
        inside = (off < last).astype(F32)
        for i in range(0, moves, 2):
            pair = []
            for j in (i, i + 1):
                hit = (table[...] == slot_of[mine + j]).astype(F32)
                pair.append(
                    jnp.sum(hit * whole, axis=1, keepdims=True) + jnp.sum(hit * some, axis=1, keepdims=True) * inside
                )
            pair = jnp.concatenate(pair, axis=1)
            for r in range(rows):
                mult[r * block : (r + 1) * block, i * page : (i + 2) * page] = jnp.broadcast_to(
                    pair[r : r + 1], (block, 2 * page)
                )

        places = []
        for i in range(moves):
            again = 0
            for j in range(i):
                again = again + (src[0, mine + i] == src[0, mine + j]).astype(jnp.int32)
            places.append((src[0, mine + i], again))

        for copy in local:
            copy.wait()
        for copy in final.values():
            copy.wait_recv()
        while sent:
            sent.pop().wait_send()

        rope = width - LATENT
        for i, (rank, again) in enumerate(places):
            pair = inbox[rank]
            first = again == 0
            here = slice(i * page, (i + 1) * page)
            pages[here, :LATENT] = jnp.where(first, pair[:, :LATENT], pair[:, LATENT : 2 * LATENT])
            pages[here, LATENT:] = jnp.where(
                first, pair[:, 2 * LATENT : 2 * LATENT + rope], pair[:, 2 * LATENT + rope :]
            )

        size = rows * block
        to = lax.broadcasted_iota(jnp.int32, (size, size), 0)
        frm = lax.broadcasted_iota(jnp.int32, (size, size), 1)
        turn = (frm == (to % rows) * block + to // rows).astype(BF16)
        for n, a in enumerate(head_groups):
            xa = lax.rem(x + a, NX)
            hs = pl.ds(pl.multiple_of(xa * block, block), block)
            q = q_ref[:, hs, :].reshape(size, width)
            s = lax.dot_general(q, pages[...], (((1,), (1,)), ((), ())), preferred_element_type=F32) * SOFTMAX_SCALE
            times = mult[...]
            s = jnp.where(times > 0.0, s, LOW)
            old = top[:, hs, :].reshape(size, 128)[:, :1]
            m = jnp.maximum(old, jnp.max(s, axis=1, keepdims=True))
            shrink = jnp.exp(old - m)
            p = jnp.exp(s - m) * times
            t = total[:, hs, :].reshape(size, 128)[:, :1] * shrink + jnp.sum(p, axis=1, keepdims=True)
            o = acc[:, hs, :].reshape(size, LATENT) * shrink
            o = o + jnp.dot(p.astype(BF16), pages[:, :LATENT], preferred_element_type=F32)
            o = (o / jnp.where(t == 0.0, 1.0, t)).astype(BF16)
            o = jnp.dot(turn, o, preferred_element_type=F32).astype(BF16)
            packed[n] = o.reshape(NZ, -1, LATENT)
            for copy in latent_copies(n):
                copy.start()

    def rest(gus, ds, ho, part, mid, acc, hid):
        cols_all = part.shape[3]
        half = cols_all // 2
        ff = gate.shape[0]

        def step_to(dx, dz):
            return on(dx % NX, dz % NZ, 0)

        width = half // SUBS
        wing = width // 2
        order = [(h, s) for s in range(SUBS) for h in range(2)]

        row0 = pl.multiple_of(core * ff, 16)
        row1 = pl.multiple_of(2 * ff - row0 - ff, 16)
        loads = []
        w_copies = weight_copies()
        for k, copy in enumerate(w_copies[2:]):
            copy.wait_recv()
            own, other = ((gate, gate_2), (up, up_2), (down, down_2))[k]
            base = 640 if k == 1 else 0
            into = ds if k == 2 else gus
            loads.append(pltpu.make_async_copy(own, into.at[pl.ds(base + row0, ff), :], in_sems.at[2 * k]))
            loads.append(pltpu.make_async_copy(other, into.at[pl.ds(base + row1, ff), :], in_sems.at[2 * k + 1]))
        for copy in loads:
            copy.start()

        def weights_ready(*ks):
            for k in ks:
                loads[2 * k].wait()
                loads[2 * k + 1].wait()

        for copy in weight_places():
            copy.wait()
        for copy in w_copies[:2]:
            copy.wait_recv()
        sent.extend(w_copies)
        for n in range(4):
            for b, copy in zip((2, 1, 3, 0), latent_copies(n)):
                if (head_groups[n], b) == (0, 0):
                    copy.wait()
                else:
                    copy.wait_recv()
                    sent.append(copy)
        for h in range(4):
            l = rl[:, h * 16 : (h + 1) * 16, :].reshape(256, LATENT)
            ho[:, h * 128 : (h + 1) * 128] = jnp.dot(l, vus[h // 2, h % 2], preferred_element_type=F32).astype(BF16)

        def reduce_scatter(turn, fill, bufs, finish, after=None):
            r1, r2, t1, t2 = bufs

            def chunk(h, phase, i, base, size):
                cs = pl.ds(base, size)
                xi, zi = lax.rem(x + i + NX, NX), lax.rem(z + i + NZ, NZ)
                along_x = (h == 0) == (phase == 0)
                if phase == 0:
                    return part.at[xi, :, :, cs] if along_x else part.at[:, zi, :, cs]
                return part.at[xi, z, :, cs] if along_x else part.at[x, zi, :, cs]

            def to(h, phase, i):
                return step_to(i, 0) if (h == 0) == (phase == 0) else step_to(0, i)

            def sems(h, s, phase, k):
                at = (((turn * 2 + h) * SUBS + s) * 2 + phase) * 6 + k
                return rs_ss.at[at], rs_rs.at[at]

            def bufs_of(h, s, phase):
                first, second = (r1, r2) if phase == 0 else (t1, t2)
                return first.at[h, s], second.at[h, s]

            state = {}

            def start(h, s, phase):
                base = h * half + s * width
                first, second = bufs_of(h, s, phase)
                lo, hi = base, base + wing
                state[h, s, phase] = [
                    send(chunk(h, phase, 2, lo, wing), first.at[0], *sems(h, s, phase, 0), to(h, phase, 1)),
                    send(chunk(h, phase, 2, hi, wing), first.at[1], *sems(h, s, phase, 1), to(h, phase, -1)),
                    send(chunk(h, phase, 1, hi, wing), second.at[0, ..., pl.ds(wing, wing)], *sems(h, s, phase, 2), to(h, phase, 1)),
                    send(chunk(h, phase, -1, lo, wing), second.at[1, ..., pl.ds(0, wing)], *sems(h, s, phase, 3), to(h, phase, -1)),
                ]

            def middle(h, s, phase):
                base = h * half + s * width
                first, second = bufs_of(h, s, phase)
                copies = state[h, s, phase]
                for side, (i, at) in enumerate(((1, 0), (-1, wing))):
                    copies[side].wait_recv()
                    mine = chunk(h, phase, i, base + at, wing)
                    mine[...] = (mine[...].astype(F32) + first[side].astype(F32)).astype(BF16)
                    copies.append(
                        send(mine, second.at[side, ..., pl.ds(at, wing)], *sems(h, s, phase, 4 + side), to(h, phase, i))
                    )

            def total(h, s, phase):
                base = h * half + s * width
                _, second = bufs_of(h, s, phase)
                for copy in state[h, s, phase][2:]:
                    copy.wait_recv()
                mine = chunk(h, phase, 0, base, width)
                value = mine[...].astype(F32) + second[0].astype(F32) + second[1].astype(F32)
                if phase == 0:
                    mine[...] = value.astype(BF16)
                else:
                    finish(base, width, value)

            for n, (h, s) in enumerate(order):
                fill(n, h * half + s * width, width)
                start(h, s, 0)
            if turn == 0:
                gus[pl.ds(2 * ff, 640 - 2 * ff), :] = jnp.zeros((640 - 2 * ff, cols_all), BF16)
                gus[pl.ds(640 + 2 * ff, 640 - 2 * ff), :] = jnp.zeros((640 - 2 * ff, cols_all), BF16)
            for h, s in order:
                middle(h, s, 0)
            for h, s in order:
                total(h, s, 0)
                start(h, s, 1)
            for h, s in order:
                middle(h, s, 1)
            for h, s in order:
                total(h, s, 1)
                if after is not None and h == 1:
                    after(s)


        def fill_out(n, base, size):
            cs = pl.ds(base, size)
            v = jnp.dot(ho[:, :256], wos[0, :, cs], preferred_element_type=F32)
            v = v + jnp.dot(ho[:, 256:], wos[1, :, cs], preferred_element_type=F32)
            part[:, :, :, cs] = v.astype(BF16).reshape(NX, NZ, 16, size)

        squares = []

        def finish_out(base, size, value):
            cs = pl.ds(base, size)
            m = res[:, cs].astype(F32) + value
            mid[:, cs] = m
            squares.append(jnp.sum(m * m, axis=1, keepdims=True))
            nrm[x, z, :, cs] = (m * gain[:, cs]).astype(BF16)

        def block(h, s, i, j, piece):
            base = h * half + s * width
            rest = wing + (128 if (h, s) == (1, SUBS - 1) else 0)
            lo, size = {"all": (0, wing + rest), "low": (0, wing), "high": (wing, rest)}[piece]
            dx, dz = (j, i) if h == 0 else (i, j)
            return nrm.at[lax.rem(x + dx + NX, NX), lax.rem(z + dz + NZ, NZ), :, pl.ds(base + lo, size)]

        one, two = {}, {}

        def pass_on(h, s, i, j, piece, k, first, step):
            ref = block(h, s, i, j, piece)
            at = (h * SUBS + s) * 20 + k
            to = step_to(0, step) if (h == 0) == first else step_to(step, 0)
            return send(ref, ref, ag_ss.at[at], ag_rs.at[at], to)

        def spread(h, s, n, i):
            two[h, s, n] = [pass_on(h, s, i, 0, "all", 4 + 4 * n, False, 1), pass_on(h, s, i, 0, "all", 5 + 4 * n, False, -1)]

        def forward(s, n, i):
            for h in range(2):
                got = two[h, s, n]
                got[0].wait_recv()
                got.append(pass_on(h, s, i, -1, "low", 6 + 4 * n, False, 1))
                got[1].wait_recv()
                got.append(pass_on(h, s, i, 1, "high", 7 + 4 * n, False, -1))

        def gather_start(s):
            if s == SUBS - 1:
                scale = lax.rsqrt(sum(squares) / cols_all + 1e-06)
                rough = scale.astype(BF16).astype(F32)
                lane = lax.broadcasted_iota(jnp.int32, (16, 128), 1)
                nrm[x, z, :, cols_all:] = jnp.where(lane < 64, rough, scale - rough).astype(BF16)
            for h in range(2):
                one[h, s] = [pass_on(h, s, 0, 0, "all", 0, True, 1), pass_on(h, s, 0, 0, "all", 1, True, -1)]
            for h in range(2):
                spread(h, s, 0, 0)

        def gather_next(s):
            for h in range(2):
                got = one[h, s]
                got[0].wait_recv()
                got.append(pass_on(h, s, -1, 0, "low", 2, True, 1))
                got[1].wait_recv()
                got.append(pass_on(h, s, 1, 0, "high", 3, True, -1))
                spread(h, s, 1, -1)
                spread(h, s, 2, 1)

        def gather_last(s):
            for h in range(2):
                one[h, s][2].wait_recv()
                one[h, s][3].wait_recv()
                spread(h, s, 3, 2)

        def gathered(s):
            for h in range(2):
                for n in range(4):
                    two[h, s, n][2].wait_recv()
                    two[h, s, n][3].wait_recv()

        def up_step(h, s):
            cs = pl.ds(h * half + s * width, width)
            v = lax.dot_general(
                nrm[:, :, :, cs].reshape(256, width), gus[:, cs], (((1,), (1,)), ((), ())), preferred_element_type=F32
            )
            if (h, s) == (0, 0):
                acc[...] = v
            else:
                acc[...] += v

        reduce_scatter(0, fill_out, (b1, b2, c1, c2), finish_out, gather_start)
        gather_next(0)
        gather_next(1)
        forward(0, 0, 0)
        gather_last(0)
        forward(1, 0, 0)
        gather_last(1)
        forward(0, 1, -1)
        forward(0, 2, 1)
        forward(1, 1, -1)
        forward(0, 3, 2)
        forward(1, 2, 1)
        gathered(0)
        weights_ready(0, 1)
        up_step(0, 0)
        forward(1, 3, 2)
        up_step(1, 0)
        gathered(1)
        up_step(0, 1)
        up_step(1, 1)
        scales = nrm[:, :, :, cols_all:].reshape(256, 128).astype(F32)
        scale = scales[:, :1] + scales[:, 64:65]
        g = acc[:, :640] * scale
        hid[...] = (g / (1.0 + jnp.exp(-g)) * (acc[:, 640:] * scale)).astype(BF16)
        while sent:
            sent.pop().wait_send()
        weights_ready(2)

        def fill_down(n, base, size):
            cs = pl.ds(base, size)
            v = jnp.dot(hid[:, : 2 * ff], ds[:, cs], preferred_element_type=F32)
            part[:, :, :, cs] = v.astype(BF16).reshape(NX, NZ, 16, size)

        def finish_down(base, size, value):
            cs = pl.ds(base, size)
            out_ref[:, cs] = (mid[:, cs] + value).astype(BF16)

        reduce_scatter(1, fill_down, (b1, b2, c1, c2), finish_down)
        while sent:
            sent.pop().wait_send()


    vmem = pltpu.VMEM
    cols, ff = res.shape[1], gate.shape[0]
    pl.run_scoped(
        attention,
        vmem(pool_hbm.shape, BF16),
        vmem((2, NX * NZ * 2, page // 2, 2 * width), BF16),
        vmem((moves * page, width), BF16),
        vmem((rows * 16, moves * page), F32),
        vmem((rows, heads, LATENT), F32),
        vmem((rows, heads, 128), F32),
        vmem((rows, heads, 128), F32),
        vmem(q_hbm.shape, BF16),
    )
    pl.run_scoped(
        rest,
        vmem((1280, cols), BF16),
        vmem((2 * ff, cols), BF16),
        vmem((256, 512), BF16),
        vmem((NX, NZ, 16, cols), BF16),
        vmem((16, cols), F32),
        vmem((256, 1280), F32),
        vmem((256, 640), BF16),
    )


def layer(src, page_of, slot_of, rc, lens, table, queries, pool, vu, wo, res, gain, gate, up, down):
    rows, heads, width = queries.shape
    page = pool.shape[1]
    ranks = NX * NZ * 2
    cols = res.shape[1]
    block = cols // 2 // SUBS
    n_rs = 2 * 2 * SUBS * 2 * 6
    dma, vmem = pltpu.SemaphoreType.DMA, pltpu.VMEM
    out, _, _, _ = pl.pallas_call(
        layer_kernel,
        out_shape=tuple(jax.ShapeDtypeStruct(a.shape, BF16) for a in (res, gate, up, down)),
        in_specs=[sspec()] * 5 + [vspec()] + [aspec()] * 4 + [vspec()] * 2 + [aspec()] * 3,
        out_specs=(vspec(), aspec(), aspec(), aspec()),
        scratch_shapes=[
            vmem((2, 3, 8, page // 2, 2 * width), BF16),
            vmem((ranks, page, 2 * width), BF16),
            vmem((NX * NZ, rows * heads // (NX * NZ), LATENT), BF16),
            vmem((NX, NZ, 16, cols + 128), BF16),
            vmem((2,) + vu.shape, BF16),
            vmem((2,) + wo.shape, BF16),
            vmem((4, NZ, rows * heads // (NX * NZ), LATENT), BF16),
            vmem((rows, 128), jnp.int32),
            pltpu.SMEM((rows, 128), jnp.int32),
            vmem((2, SUBS, 2, 4, 16, block // 2), BF16),
            vmem((2, SUBS, 2, 4, 16, block), BF16),
            vmem((2, SUBS, 2, 16, block // 2), BF16),
            vmem((2, SUBS, 2, 16, block), BF16),
            dma((10,)),
            dma((8,)),
            dma((15,)),
            dma((15,)),
            dma((64,)),
            dma((64,)),
            dma((2,)),
            dma((5,)),
            dma((5,)),
            dma((16,)),
            dma((16,)),
            dma((6,)),
            dma((n_rs,)),
            dma((n_rs,)),
            dma((40 * SUBS,)),
            dma((40 * SUBS,)),
        ],
        compiler_params=pltpu.CompilerParams(collective_id=0, has_side_effects=True, vmem_limit_bytes=VMEM_LIMIT),
        name="layer",
    )(src, page_of, slot_of, rc, lens, table, queries, pool, vu, wo, res, gain, gate, up, down)
    return out


def body(
    page_pool,
    move_source,
    move_page,
    move_slot,
    row_count,
    lengths,
    page_table,
    queries,
    value_up,
    out_proj,
    residual,
    norm_gain,
    gate_proj,
    up_proj,
    down_proj,
):
    return layer(
        move_source.reshape(1, -1), move_page, move_slot, row_count, lengths, page_table, queries, page_pool,
        value_up, out_proj, residual, norm_gain.reshape(1, -1), gate_proj.T, up_proj.T, down_proj,
    )


def solution(mesh):
    in_specs = (
        P(("rep", "dp"), None, None),
        P("rep", None),
        P("rep"),
        P("rep"),
        P(("rep", "dp")),
        P(("rep", "dp")),
        P(("rep", "dp"), None),
        P(("rep", "dp"), None, None),
        P("dp", None, None),
        P("dp", None),
        P(("rep", "dp"), None),
        P(),
        P(None, "dp"),
        P(None, "dp"),
        P("dp", None),
    )
    out_specs = P(("rep", "dp"), None)
    return jax.shard_map(body, mesh=mesh, in_specs=in_specs, out_specs=out_specs, check_vma=False)
```

```python
import functools

import jax
import jax.numpy as jnp
from jax import lax
from jax.experimental import pallas as pl
from jax.experimental.pallas import tpu as pltpu
from jax.sharding import PartitionSpec as P

LATENT = 512
SOFTMAX_SCALE = 192 ** (-0.5)
LOW = -1e30
MESH = pl.DeviceIdType.MESH
F32 = jnp.float32
BF16 = jnp.bfloat16
VMEM_LIMIT = 60 * 2**20
NX = 4
NZ = 4


def vspec():
    return pl.BlockSpec(memory_space=pltpu.VMEM)


def sspec():
    return pl.BlockSpec(memory_space=pltpu.SMEM)


def aspec():
    return pl.BlockSpec(memory_space=pl.ANY)


SUBS = 2


def layer_kernel(
    src, page_of, slot_of, rc, lens, table, q_hbm, pool_hbm, vu, wo, res, gain, gate, up, down,
    out_ref, gate_2, up_2, down_2,
    via, inbox, rl, nrm, vus, wos, packed, entries_v, entries, b1, b2, c1, c2,
    pool_sems, copy_sems, one_ss, one_rs, two_ss, two_rs, w_ls, w_ss, w_rs, lat_ss, lat_rs, in_sems,
    rs_ss, rs_rs, ag_ss, ag_rs,
):
    me = lax.axis_index("dp")
    core = lax.rem(me, 2)
    chip = me // 2
    x = chip // NZ
    z = lax.rem(chip, NZ)
    rows, heads, width = q_hbm.shape
    count, page, _ = pool_hbm.shape
    part = page // 2
    refs = table.shape[1]
    moves = page_of.shape[0] // (NX * NZ * 2)
    mine = me * moves

    def device(a, b, e):
        return (lax.rem(x + a, NX) * NZ + lax.rem(z + b, NZ)) * 2 + lax.rem(core + e, 2)

    def on(a, b, e):
        return {"dp": device(a, b, e)}

    near = [(0, 0, 1)] + [(a, 0, e) for a in (1, 2, 3) for e in (0, 1)] + [(0, b, e) for b in (1, 2, 3) for e in (0, 1)]
    far = [(a, b, 0) for a in (1, 2, 3) for b in (1, 2, 3)]
    barrier = pltpu.get_barrier_semaphore()
    for at in near + far:
        pl.semaphore_signal(barrier, inc=1, device_id=on(*at), device_id_type=MESH)

    sent = []

    def remote(src, dst, ss, rs, to):
        return pltpu.make_async_remote_copy(
            src_ref=src, dst_ref=dst, send_sem=ss, recv_sem=rs, device_id=to, device_id_type=MESH
        )

    def send(src, dst, ss, rs, to):
        copy = remote(src, dst, ss, rs, to)
        copy.start()
        sent.append(copy)
        return copy

    head_groups = (2, 0, 1, 3)

    def weight_copies():
        refs_of = ((vu, vus.at[core]), (wo, wos.at[core]), (gate, gate_2), (up, up_2), (down, down_2))
        return [remote(one, to, w_ss.at[k], w_rs.at[k], on(0, 0, 1)) for k, (one, to) in enumerate(refs_of)]

    def weight_places():
        return [
            pltpu.make_async_copy(one, to, w_ls.at[k])
            for k, (one, to) in enumerate(((vu, vus.at[core]), (wo, wos.at[core])))
        ]

    def latent_copies(n):
        copies = []
        for b in (2, 1, 3, 0):
            one, to = packed.at[n, lax.rem(z + b, NZ)], rl.at[chip]
            if (head_groups[n], b) == (0, 0):
                copies.append(pltpu.make_async_copy(one, to, pool_sems.at[0]))
            else:
                at = n * 4 + b
                copies.append(remote(one, to, lat_ss.at[at], lat_rs.at[at], on(head_groups[n], b, 0)))
        return copies

    def attention(pool, outbox, pages, mult, acc, top, total, q_ref):
        loads = []
        for k in range(8):
            span = pl.ds(k * (count // 8), count // 8)
            loads.append(pltpu.make_async_copy(pool_hbm.at[span], pool.at[span], pool_sems.at[k]))
        for copy in loads:
            copy.start()

        row = lax.broadcasted_iota(jnp.int32, (rows, refs), 0)
        pos = lax.broadcasted_iota(jnp.int32, (rows, refs), 1)
        length = jnp.zeros((rows, refs), jnp.int32)
        for r in range(rows):
            length = jnp.where(row == r, jnp.where(r < rc[0], lens[r], 0), length)
        valid = jnp.clip(length - page * pos, 0, page)
        entry = table[...] * 128 + valid
        for i in range(moves):
            entry = jnp.where(table[...] == slot_of[mine + i], 0, entry)
        entries_v[:, :refs] = entry
        to_scalar = pltpu.make_async_copy(entries_v, entries, pool_sems.at[8])
        to_scalar.start()

        pl.semaphore_wait(barrier, len(near + far))
        for copy in loads:
            copy.wait()

        def pack(i, first):
            d = first + i
            hits = [src[0, d * moves + j] == me for j in range(moves)]
            named = [page_of[d * moves + j] for j in range(moves)]
            early, late = 0, 0
            for j in range(moves):
                late = jnp.where(hits[j], named[j], late)
                early = jnp.where(hits[moves - 1 - j], named[moves - 1 - j], early)
            one, two = pool[early], pool[late]
            rope = jnp.concatenate([one[:, LATENT:], two[:, LATENT:]], axis=1)
            for h in range(2):
                rs = slice(h * part, (h + 1) * part)
                outbox[h, d, :, :LATENT] = one[rs, :LATENT]
                outbox[h, d, :, LATENT : 2 * LATENT] = two[rs, :LATENT]
                outbox[h, d, :, 2 * LATENT :] = rope[rs]
            return first

        one_copies = {}
        final = {}
        local = []

        def deliver(h, a, b, e, src):
            origin = (lax.rem(x + (NX - a if h == 0 else 0), NX) * NZ + lax.rem(z + (0 if h == 0 else NZ - b), NZ)) * 2 + core
            dst = inbox.at[origin, pl.ds(h * part, part), :]
            at = ((a * NZ + b) * 2 + e) * 2 + h
            da, db = (0, b) if h == 0 else (a, 0)
            if (da, db, e) == (0, 0, 0):
                copy = pltpu.make_async_copy(src, dst, copy_sems.at[len(local)])
                copy.start()
                local.append(copy)
            else:
                final[at] = send(src, dst, two_ss.at[at], two_rs.at[at], on(da, db, e))

        for n, a in enumerate((2, 1, 3, 0)):
            xa = lax.rem(x + a, NX)
            lax.fori_loop(0, 8, pack, xa * 8)
            if a:
                one_copies[0, a] = send(
                    outbox.at[0, pl.ds(xa * 8, 8)], via.at[0, a - 1], one_ss.at[a - 1], one_rs.at[a - 1], on(a, 0, 0)
                )
            for b in (2, 1, 3):
                zb = lax.rem(z + b, NZ)
                at = 3 + (b - 1) * 4 + n
                one_copies[1, b, n] = send(
                    outbox.at[1, pl.ds(xa * 8 + zb * 2, 2)],
                    via.at[1, b - 1, pl.ds(xa * 2, 2)],
                    one_ss.at[at],
                    one_rs.at[at],
                    on(0, b, 0),
                )

        def second_hop(k):
            if k:
                one_copies[0, k].wait_recv()
                for n in range(4):
                    one_copies[1, k, n].wait_recv()
            for o in (2, 1, 3, 0):
                for e in range(2):
                    ce = lax.rem(core + e, 2)
                    zo, xo = lax.rem(z + o, NZ), lax.rem(x + o, NX)
                    deliver(0, k, o, e, via.at[0, k - 1, zo * 2 + ce] if k else outbox.at[0, x * 8 + zo * 2 + ce])
                    deliver(1, o, k, e, via.at[1, k - 1, xo * 2 + ce] if k else outbox.at[1, xo * 8 + z * 2 + ce])

        def attend_row(r, carry):
            q = q_ref[r]
            group = 8
            col = lax.broadcasted_iota(jnp.int32, (1, page * group), 1)
            keys, scores = [], []
            for g in range(refs // group):
                es = [entries[r, g * group + i] for i in range(group)]
                k = jnp.concatenate([pool[e >> 7] for e in es], axis=0)
                limit = jnp.zeros((1, page * group), jnp.int32)
                for i, e in enumerate(es):
                    limit = jnp.where((col >> 6) == i, e & 127, limit)
                s = lax.dot_general(q, k, (((1,), (1,)), ((), ())), preferred_element_type=F32) * SOFTMAX_SCALE
                scores.append(jnp.where((col & 63) < limit, s, LOW))
                keys.append(k)
            m = functools.reduce(jnp.maximum, [jnp.max(s, axis=1, keepdims=True) for s in scores])
            t = jnp.zeros((heads, 1), F32)
            o = jnp.zeros((heads, LATENT), F32)
            for s, k in zip(scores, keys):
                p = jnp.exp(s - m)
                t = t + jnp.sum(p, axis=1, keepdims=True)
                o = o + jnp.dot(p.astype(BF16), k[:, :LATENT], preferred_element_type=F32)
            some = m > 0.5 * LOW
            acc[r] = jnp.where(some, o, 0.0)
            top[r] = jnp.broadcast_to(m, (heads, 128))
            total[r] = jnp.broadcast_to(jnp.where(some, t, 0.0), (heads, 128))
            return carry

        for copy in weight_copies() + weight_places():
            copy.start()
        load_q = pltpu.make_async_copy(q_hbm, q_ref, pool_sems.at[9])
        load_q.start()
        second_hop(0)
        to_scalar.wait()
        load_q.wait()
        lax.fori_loop(0, 5, attend_row, 0)
        second_hop(1)
        second_hop(3)
        lax.fori_loop(5, 9, attend_row, 0)
        second_hop(2)
        lax.fori_loop(9, rows, attend_row, 0)

        block = 16
        whole = (valid == page).astype(F32)
        some = ((valid > 0) & (valid < page)).astype(F32)
        last = jnp.sum(some * valid.astype(F32), axis=1, keepdims=True)
        off = lax.broadcasted_iota(jnp.int32, (rows, page), 1).astype(F32)
        inside = (off < last).astype(F32)
        for i in range(0, moves, 2):
            pair = []
            for j in (i, i + 1):
                hit = (table[...] == slot_of[mine + j]).astype(F32)
                pair.append(
                    jnp.sum(hit * whole, axis=1, keepdims=True) + jnp.sum(hit * some, axis=1, keepdims=True) * inside
                )
            pair = jnp.concatenate(pair, axis=1)
            for r in range(rows):
                mult[r * block : (r + 1) * block, i * page : (i + 2) * page] = jnp.broadcast_to(
                    pair[r : r + 1], (block, 2 * page)
                )

        places = []
        for i in range(moves):
            again = 0
            for j in range(i):
                again = again + (src[0, mine + i] == src[0, mine + j]).astype(jnp.int32)
            places.append((src[0, mine + i], again))

        for copy in local:
            copy.wait()
        for copy in final.values():
            copy.wait_recv()
        while sent:
            sent.pop().wait_send()

        rope = width - LATENT
        for i, (rank, again) in enumerate(places):
            pair = inbox[rank]
            first = again == 0
            here = slice(i * page, (i + 1) * page)
            pages[here, :LATENT] = jnp.where(first, pair[:, :LATENT], pair[:, LATENT : 2 * LATENT])
            pages[here, LATENT:] = jnp.where(
                first, pair[:, 2 * LATENT : 2 * LATENT + rope], pair[:, 2 * LATENT + rope :]
            )

        size = rows * block
        to = lax.broadcasted_iota(jnp.int32, (size, size), 0)
        frm = lax.broadcasted_iota(jnp.int32, (size, size), 1)
        turn = (frm == (to % rows) * block + to // rows).astype(BF16)
        for n, a in enumerate(head_groups):
            xa = lax.rem(x + a, NX)
            hs = pl.ds(pl.multiple_of(xa * block, block), block)
            q = q_ref[:, hs, :].reshape(size, width)
            s = lax.dot_general(q, pages[...], (((1,), (1,)), ((), ())), preferred_element_type=F32) * SOFTMAX_SCALE
            times = mult[...]
            s = jnp.where(times > 0.0, s, LOW)
            old = top[:, hs, :].reshape(size, 128)[:, :1]
            m = jnp.maximum(old, jnp.max(s, axis=1, keepdims=True))
            shrink = jnp.exp(old - m)
            p = jnp.exp(s - m) * times
            t = total[:, hs, :].reshape(size, 128)[:, :1] * shrink + jnp.sum(p, axis=1, keepdims=True)
            o = acc[:, hs, :].reshape(size, LATENT) * shrink
            o = o + jnp.dot(p.astype(BF16), pages[:, :LATENT], preferred_element_type=F32)
            o = (o / jnp.where(t == 0.0, 1.0, t)).astype(BF16)
            o = jnp.dot(turn, o, preferred_element_type=F32).astype(BF16)
            packed[n] = o.reshape(NZ, -1, LATENT)
            for copy in latent_copies(n):
                copy.start()

    def rest(gus, ds, ho, part, mid, acc, hid):
        cols_all = part.shape[3]
        half = cols_all // 2
        ff = gate.shape[0]

        def step_to(dx, dz):
            return on(dx % NX, dz % NZ, 0)

        width = half // SUBS
        wing = width // 2
        order = [(h, s) for s in range(SUBS) for h in range(2)]

        row0 = pl.multiple_of(core * ff, 16)
        row1 = pl.multiple_of(2 * ff - row0 - ff, 16)
        loads = []
        w_copies = weight_copies()
        for k, copy in enumerate(w_copies[2:]):
            copy.wait_recv()
            own, other = ((gate, gate_2), (up, up_2), (down, down_2))[k]
            base = 640 if k == 1 else 0
            into = ds if k == 2 else gus
            loads.append(pltpu.make_async_copy(own, into.at[pl.ds(base + row0, ff), :], in_sems.at[2 * k]))
            loads.append(pltpu.make_async_copy(other, into.at[pl.ds(base + row1, ff), :], in_sems.at[2 * k + 1]))
        def weights_ready(*ks):
            for k in ks:
                loads[2 * k].wait()
                loads[2 * k + 1].wait()

        for copy in weight_places():
            copy.wait()
        for copy in w_copies[:2]:
            copy.wait_recv()
        sent.extend(w_copies)
        for n in range(4):
            for b, copy in zip((2, 1, 3, 0), latent_copies(n)):
                if (head_groups[n], b) == (0, 0):
                    copy.wait()
                else:
                    copy.wait_recv()
                    sent.append(copy)
        for h in range(4):
            l = rl[:, h * 16 : (h + 1) * 16, :].reshape(256, LATENT)
            ho[:, h * 128 : (h + 1) * 128] = jnp.dot(l, vus[h // 2, h % 2], preferred_element_type=F32).astype(BF16)

        def reduce_scatter(turn, fill, bufs, finish, after=None):
            r1, r2, t1, t2 = bufs

            def chunk(h, phase, i, base, size):
                cs = pl.ds(base, size)
                xi, zi = lax.rem(x + i + NX, NX), lax.rem(z + i + NZ, NZ)
                along_x = (h == 0) == (phase == 0)
                if phase == 0:
                    return part.at[xi, :, :, cs] if along_x else part.at[:, zi, :, cs]
                return part.at[xi, z, :, cs] if along_x else part.at[x, zi, :, cs]

            def to(h, phase, i):
                return step_to(i, 0) if (h == 0) == (phase == 0) else step_to(0, i)

            def sems(h, s, phase, k):
                at = (((turn * 2 + h) * SUBS + s) * 2 + phase) * 6 + k
                return rs_ss.at[at], rs_rs.at[at]

            def bufs_of(h, s, phase):
                first, second = (r1, r2) if phase == 0 else (t1, t2)
                return first.at[h, s], second.at[h, s]

            state = {}

            def start(h, s, phase, side):
                base = h * half + s * width + side * wing
                first, second = bufs_of(h, s, phase)
                step = 1 - 2 * side
                copies = state.setdefault((h, s, phase), {})
                copies[side] = send(
                    chunk(h, phase, 2, base, wing), first.at[side], *sems(h, s, phase, side), to(h, phase, step)
                )
                copies[3 - side] = send(
                    chunk(h, phase, -step, base, wing),
                    second.at[1 - side, ..., pl.ds(side * wing, wing)],
                    *sems(h, s, phase, 3 - side),
                    to(h, phase, -step),
                )

            def middle(h, s, phase):
                base = h * half + s * width
                first, second = bufs_of(h, s, phase)
                copies = state[h, s, phase]
                for side, (i, at) in enumerate(((1, 0), (-1, wing))):
                    copies[side].wait_recv()
                    mine = chunk(h, phase, i, base + at, wing)
                    mine[...] = (mine[...].astype(F32) + first[side].astype(F32)).astype(BF16)
                    copies[4 + side] = send(
                        mine, second.at[side, ..., pl.ds(at, wing)], *sems(h, s, phase, 4 + side), to(h, phase, i)
                    )

            def total(h, s, phase):
                base = h * half + s * width
                _, second = bufs_of(h, s, phase)
                for k in range(2, 6):
                    state[h, s, phase][k].wait_recv()
                mine = chunk(h, phase, 0, base, width)
                value = mine[...].astype(F32) + second[0].astype(F32) + second[1].astype(F32)
                if phase == 0:
                    mine[...] = value.astype(BF16)
                else:
                    finish(base, width, value)

            for s in range(SUBS):
                for side in range(2):
                    for h in range(2):
                        fill(h * half + s * width + side * wing, wing)
                        start(h, s, 0, side)
            if turn == 0:
                gus[pl.ds(2 * ff, 640 - 2 * ff), :] = jnp.zeros((640 - 2 * ff, cols_all), BF16)
                gus[pl.ds(640 + 2 * ff, 640 - 2 * ff), :] = jnp.zeros((640 - 2 * ff, cols_all), BF16)
            for h, s in order:
                middle(h, s, 0)
            if turn == 0:
                for copy in loads[:4]:
                    copy.start()
            for h, s in order:
                total(h, s, 0)
                start(h, s, 1, 0)
                start(h, s, 1, 1)
            for h, s in order:
                middle(h, s, 1)
            for h, s in order:
                total(h, s, 1)
                if after is not None and h == 1:
                    after(s)


        def fill_out(base, size):
            cs = pl.ds(base, size)
            v = jnp.dot(ho[:, :256], wos[0, :, cs], preferred_element_type=F32)
            v = v + jnp.dot(ho[:, 256:], wos[1, :, cs], preferred_element_type=F32)
            part[:, :, :, cs] = v.astype(BF16).reshape(NX, NZ, 16, size)

        squares = []

        def finish_out(base, size, value):
            cs = pl.ds(base, size)
            m = res[:, cs].astype(F32) + value
            mid[:, cs] = m
            squares.append(jnp.sum(m * m, axis=1, keepdims=True))
            nrm[x, z, :, cs] = (m * gain[:, cs]).astype(BF16)

        def block(h, s, i, j, piece):
            base = h * half + s * width
            rest = wing + (128 if (h, s) == (1, SUBS - 1) else 0)
            lo, size = {"all": (0, wing + rest), "low": (0, wing), "high": (wing, rest)}[piece]
            dx, dz = (j, i) if h == 0 else (i, j)
            return nrm.at[lax.rem(x + dx + NX, NX), lax.rem(z + dz + NZ, NZ), :, pl.ds(base + lo, size)]

        one, two = {}, {}

        def pass_on(h, s, i, j, piece, k, first, step):
            ref = block(h, s, i, j, piece)
            at = (h * SUBS + s) * 20 + k
            to = step_to(0, step) if (h == 0) == first else step_to(step, 0)
            return send(ref, ref, ag_ss.at[at], ag_rs.at[at], to)

        def spread(h, s, n, i):
            two[h, s, n] = [pass_on(h, s, i, 0, "all", 4 + 4 * n, False, 1), pass_on(h, s, i, 0, "all", 5 + 4 * n, False, -1)]

        def forward(s, n, i):
            for h in range(2):
                got = two[h, s, n]
                got[0].wait_recv()
                got.append(pass_on(h, s, i, -1, "low", 6 + 4 * n, False, 1))
                got[1].wait_recv()
                got.append(pass_on(h, s, i, 1, "high", 7 + 4 * n, False, -1))

        def gather_start(s):
            if s == SUBS - 1:
                scale = lax.rsqrt(sum(squares) / cols_all + 1e-06)
                rough = scale.astype(BF16).astype(F32)
                lane = lax.broadcasted_iota(jnp.int32, (16, 128), 1)
                nrm[x, z, :, cols_all:] = jnp.where(lane < 64, rough, scale - rough).astype(BF16)
            for h in range(2):
                one[h, s] = [pass_on(h, s, 0, 0, "all", 0, True, 1), pass_on(h, s, 0, 0, "all", 1, True, -1)]
            for h in range(2):
                spread(h, s, 0, 0)

        def gather_next(s):
            for h in range(2):
                got = one[h, s]
                got[0].wait_recv()
                got.append(pass_on(h, s, -1, 0, "low", 2, True, 1))
                got[1].wait_recv()
                got.append(pass_on(h, s, 1, 0, "high", 3, True, -1))
                spread(h, s, 1, -1)
                spread(h, s, 2, 1)

        def gather_last(s):
            for h in range(2):
                one[h, s][2].wait_recv()
                one[h, s][3].wait_recv()
                spread(h, s, 3, 2)

        def gathered(s):
            for h in range(2):
                for n in range(4):
                    two[h, s, n][2].wait_recv()
                    two[h, s, n][3].wait_recv()

        def up_step(h, s):
            cs = pl.ds(h * half + s * width, width)
            v = lax.dot_general(
                nrm[:, :, :, cs].reshape(256, width), gus[:, cs], (((1,), (1,)), ((), ())), preferred_element_type=F32
            )
            if (h, s) == (0, 0):
                acc[...] = v
            else:
                acc[...] += v

        reduce_scatter(0, fill_out, (b1, b2, c1, c2), finish_out, gather_start)
        gather_next(0)
        gather_next(1)
        forward(0, 0, 0)
        gather_last(0)
        forward(1, 0, 0)
        gather_last(1)
        for copy in loads[4:]:
            copy.start()
        forward(0, 1, -1)
        forward(0, 2, 1)
        forward(1, 1, -1)
        forward(0, 3, 2)
        forward(1, 2, 1)
        forward(1, 3, 2)
        gathered(0)
        weights_ready(0, 1)
        up_step(0, 0)
        up_step(1, 0)
        gathered(1)
        up_step(0, 1)
        up_step(1, 1)
        scales = nrm[:, :, :, cols_all:].reshape(256, 128).astype(F32)
        scale = scales[:, :1] + scales[:, 64:65]
        g = acc[:, :640] * scale
        hid[...] = (g / (1.0 + jnp.exp(-g)) * (acc[:, 640:] * scale)).astype(BF16)
        while sent:
            sent.pop().wait_send()
        weights_ready(2)

        def fill_down(base, size):
            cs = pl.ds(base, size)
            v = jnp.dot(hid[:, : 2 * ff], ds[:, cs], preferred_element_type=F32)
            part[:, :, :, cs] = v.astype(BF16).reshape(NX, NZ, 16, size)

        def finish_down(base, size, value):
            cs = pl.ds(base, size)
            out_ref[:, cs] = (mid[:, cs] + value).astype(BF16)

        reduce_scatter(1, fill_down, (b1, b2, c1, c2), finish_down)
        while sent:
            sent.pop().wait_send()


    vmem = pltpu.VMEM
    cols, ff = res.shape[1], gate.shape[0]
    pl.run_scoped(
        attention,
        vmem(pool_hbm.shape, BF16),
        vmem((2, NX * NZ * 2, page // 2, 2 * width), BF16),
        vmem((moves * page, width), BF16),
        vmem((rows * 16, moves * page), F32),
        vmem((rows, heads, LATENT), F32),
        vmem((rows, heads, 128), F32),
        vmem((rows, heads, 128), F32),
        vmem(q_hbm.shape, BF16),
    )
    pl.run_scoped(
        rest,
        vmem((1280, cols), BF16),
        vmem((2 * ff, cols), BF16),
        vmem((256, 512), BF16),
        vmem((NX, NZ, 16, cols), BF16),
        vmem((16, cols), F32),
        vmem((256, 1280), F32),
        vmem((256, 640), BF16),
    )


def layer(src, page_of, slot_of, rc, lens, table, queries, pool, vu, wo, res, gain, gate, up, down):
    rows, heads, width = queries.shape
    page = pool.shape[1]
    ranks = NX * NZ * 2
    cols = res.shape[1]
    block = cols // 2 // SUBS
    n_rs = 2 * 2 * SUBS * 2 * 6
    dma, vmem = pltpu.SemaphoreType.DMA, pltpu.VMEM
    out, _, _, _ = pl.pallas_call(
        layer_kernel,
        out_shape=tuple(jax.ShapeDtypeStruct(a.shape, BF16) for a in (res, gate, up, down)),
        in_specs=[sspec()] * 5 + [vspec()] + [aspec()] * 4 + [vspec()] * 2 + [aspec()] * 3,
        out_specs=(vspec(), aspec(), aspec(), aspec()),
        scratch_shapes=[
            vmem((2, 3, 8, page // 2, 2 * width), BF16),
            vmem((ranks, page, 2 * width), BF16),
            vmem((NX * NZ, rows * heads // (NX * NZ), LATENT), BF16),
            vmem((NX, NZ, 16, cols + 128), BF16),
            vmem((2,) + vu.shape, BF16),
            vmem((2,) + wo.shape, BF16),
            vmem((4, NZ, rows * heads // (NX * NZ), LATENT), BF16),
            vmem((rows, 128), jnp.int32),
            pltpu.SMEM((rows, 128), jnp.int32),
            vmem((2, SUBS, 2, 4, 16, block // 2), BF16),
            vmem((2, SUBS, 2, 4, 16, block), BF16),
            vmem((2, SUBS, 2, 16, block // 2), BF16),
            vmem((2, SUBS, 2, 16, block), BF16),
            dma((10,)),
            dma((8,)),
            dma((15,)),
            dma((15,)),
            dma((64,)),
            dma((64,)),
            dma((2,)),
            dma((5,)),
            dma((5,)),
            dma((16,)),
            dma((16,)),
            dma((6,)),
            dma((n_rs,)),
            dma((n_rs,)),
            dma((40 * SUBS,)),
            dma((40 * SUBS,)),
        ],
        compiler_params=pltpu.CompilerParams(collective_id=0, has_side_effects=True, vmem_limit_bytes=VMEM_LIMIT),
        name="layer",
    )(src, page_of, slot_of, rc, lens, table, queries, pool, vu, wo, res, gain, gate, up, down)
    return out


def body(
    page_pool,
    move_source,
    move_page,
    move_slot,
    row_count,
    lengths,
    page_table,
    queries,
    value_up,
    out_proj,
    residual,
    norm_gain,
    gate_proj,
    up_proj,
    down_proj,
):
    return layer(
        move_source.reshape(1, -1), move_page, move_slot, row_count, lengths, page_table, queries, page_pool,
        value_up, out_proj, residual, norm_gain.reshape(1, -1), gate_proj.T, up_proj.T, down_proj,
    )


def solution(mesh):
    in_specs = (
        P(("rep", "dp"), None, None),
        P("rep", None),
        P("rep"),
        P("rep"),
        P(("rep", "dp")),
        P(("rep", "dp")),
        P(("rep", "dp"), None),
        P(("rep", "dp"), None, None),
        P("dp", None, None),
        P("dp", None),
        P(("rep", "dp"), None),
        P(),
        P(None, "dp"),
        P(None, "dp"),
        P("dp", None),
    )
    out_specs = P(("rep", "dp"), None)
    return jax.shard_map(body, mesh=mesh, in_specs=in_specs, out_specs=out_specs, check_vma=False)
```

```python
import functools

import jax
import jax.numpy as jnp
from jax import lax
from jax.experimental import pallas as pl
from jax.experimental.pallas import tpu as pltpu
from jax.sharding import PartitionSpec as P

LATENT = 512
SOFTMAX_SCALE = 192 ** (-0.5)
LOW = -1e30
MESH = pl.DeviceIdType.MESH
F32 = jnp.float32
BF16 = jnp.bfloat16
VMEM_LIMIT = 60 * 2**20
NX = 4
NZ = 4


def vspec():
    return pl.BlockSpec(memory_space=pltpu.VMEM)


def sspec():
    return pl.BlockSpec(memory_space=pltpu.SMEM)


def aspec():
    return pl.BlockSpec(memory_space=pl.ANY)


SUBS = 2


def layer_kernel(
    src, page_of, slot_of, rc, lens, table, q_hbm, pool_hbm, vu, wo, res, gain, gate, up, down,
    out_ref, gate_2, up_2, down_2,
    via, inbox, rl, nrm, vus, wos, packed, entries_v, entries, b1, b2, c1, c2,
    pool_sems, copy_sems, one_ss, one_rs, two_ss, two_rs, w_ls, w_ss, w_rs, lat_ss, lat_rs, in_sems,
    rs_ss, rs_rs, ag_ss, ag_rs,
):
    me = lax.axis_index("dp")
    core = lax.rem(me, 2)
    chip = me // 2
    x = chip // NZ
    z = lax.rem(chip, NZ)
    rows, heads, width = q_hbm.shape
    count, page, _ = pool_hbm.shape
    part = page // 2
    refs = table.shape[1]
    moves = page_of.shape[0] // (NX * NZ * 2)
    mine = me * moves

    def device(a, b, e):
        return (lax.rem(x + a, NX) * NZ + lax.rem(z + b, NZ)) * 2 + lax.rem(core + e, 2)

    def on(a, b, e):
        return {"dp": device(a, b, e)}

    near = [(0, 0, 1)] + [(a, 0, e) for a in (1, 2, 3) for e in (0, 1)] + [(0, b, e) for b in (1, 2, 3) for e in (0, 1)]
    far = [(a, b, 0) for a in (1, 2, 3) for b in (1, 2, 3)]
    barrier = pltpu.get_barrier_semaphore()
    for at in near + far:
        pl.semaphore_signal(barrier, inc=1, device_id=on(*at), device_id_type=MESH)

    sent = []

    def remote(src, dst, ss, rs, to):
        return pltpu.make_async_remote_copy(
            src_ref=src, dst_ref=dst, send_sem=ss, recv_sem=rs, device_id=to, device_id_type=MESH
        )

    def send(src, dst, ss, rs, to):
        copy = remote(src, dst, ss, rs, to)
        copy.start()
        sent.append(copy)
        return copy

    head_groups = (2, 0, 1, 3)

    def weight_copies():
        refs_of = ((vu, vus.at[core]), (wo, wos.at[core]), (gate, gate_2), (up, up_2), (down, down_2))
        return [remote(one, to, w_ss.at[k], w_rs.at[k], on(0, 0, 1)) for k, (one, to) in enumerate(refs_of)]

    def weight_places():
        return [
            pltpu.make_async_copy(one, to, w_ls.at[k])
            for k, (one, to) in enumerate(((vu, vus.at[core]), (wo, wos.at[core])))
        ]

    def latent_copies(n):
        copies = []
        for b in (2, 1, 3, 0):
            one, to = packed.at[n, lax.rem(z + b, NZ)], rl.at[chip]
            if (head_groups[n], b) == (0, 0):
                copies.append(pltpu.make_async_copy(one, to, pool_sems.at[0]))
            else:
                at = n * 4 + b
                copies.append(remote(one, to, lat_ss.at[at], lat_rs.at[at], on(head_groups[n], b, 0)))
        return copies

    def attention(pool, outbox, pages, mult, acc, top, total, q_ref):
        loads = []
        for k in range(8):
            span = pl.ds(k * (count // 8), count // 8)
            loads.append(pltpu.make_async_copy(pool_hbm.at[span], pool.at[span], pool_sems.at[k]))
        for copy in loads:
            copy.start()

        row = lax.broadcasted_iota(jnp.int32, (rows, refs), 0)
        pos = lax.broadcasted_iota(jnp.int32, (rows, refs), 1)
        length = jnp.zeros((rows, refs), jnp.int32)
        for r in range(rows):
            length = jnp.where(row == r, jnp.where(r < rc[0], lens[r], 0), length)
        valid = jnp.clip(length - page * pos, 0, page)
        entry = table[...] * 128 + valid
        for i in range(moves):
            entry = jnp.where(table[...] == slot_of[mine + i], 0, entry)
        entries_v[:, :refs] = entry
        to_scalar = pltpu.make_async_copy(entries_v, entries, pool_sems.at[8])
        to_scalar.start()

        pl.semaphore_wait(barrier, len(near + far))
        for copy in loads:
            copy.wait()

        def pack(i, first):
            d = first + i
            hits = [src[0, d * moves + j] == me for j in range(moves)]
            named = [page_of[d * moves + j] for j in range(moves)]
            early, late = 0, 0
            for j in range(moves):
                late = jnp.where(hits[j], named[j], late)
                early = jnp.where(hits[moves - 1 - j], named[moves - 1 - j], early)
            one, two = pool[early], pool[late]
            rope = jnp.concatenate([one[:, LATENT:], two[:, LATENT:]], axis=1)
            for h in range(2):
                rs = slice(h * part, (h + 1) * part)
                outbox[h, d, :, :LATENT] = one[rs, :LATENT]
                outbox[h, d, :, LATENT : 2 * LATENT] = two[rs, :LATENT]
                outbox[h, d, :, 2 * LATENT :] = rope[rs]
            return first

        one_copies = {}
        final = {}
        local = []

        def deliver(h, a, b, e, src):
            origin = (lax.rem(x + (NX - a if h == 0 else 0), NX) * NZ + lax.rem(z + (0 if h == 0 else NZ - b), NZ)) * 2 + core
            dst = inbox.at[origin, pl.ds(h * part, part), :]
            at = ((a * NZ + b) * 2 + e) * 2 + h
            da, db = (0, b) if h == 0 else (a, 0)
            if (da, db, e) == (0, 0, 0):
                copy = pltpu.make_async_copy(src, dst, copy_sems.at[len(local)])
                copy.start()
                local.append(copy)
            else:
                final[at] = send(src, dst, two_ss.at[at], two_rs.at[at], on(da, db, e))

        for n, a in enumerate((2, 1, 3, 0)):
            xa = lax.rem(x + a, NX)
            lax.fori_loop(0, 8, pack, xa * 8)
            if a:
                one_copies[0, a] = send(
                    outbox.at[0, pl.ds(xa * 8, 8)], via.at[0, a - 1], one_ss.at[a - 1], one_rs.at[a - 1], on(a, 0, 0)
                )
            for b in (2, 1, 3):
                zb = lax.rem(z + b, NZ)
                at = 3 + (b - 1) * 4 + n
                one_copies[1, b, n] = send(
                    outbox.at[1, pl.ds(xa * 8 + zb * 2, 2)],
                    via.at[1, b - 1, pl.ds(xa * 2, 2)],
                    one_ss.at[at],
                    one_rs.at[at],
                    on(0, b, 0),
                )

        def second_hop(k):
            if k:
                one_copies[0, k].wait_recv()
                for n in range(4):
                    one_copies[1, k, n].wait_recv()
            for o in (2, 1, 3, 0):
                for e in range(2):
                    ce = lax.rem(core + e, 2)
                    zo, xo = lax.rem(z + o, NZ), lax.rem(x + o, NX)
                    deliver(0, k, o, e, via.at[0, k - 1, zo * 2 + ce] if k else outbox.at[0, x * 8 + zo * 2 + ce])
                    deliver(1, o, k, e, via.at[1, k - 1, xo * 2 + ce] if k else outbox.at[1, xo * 8 + z * 2 + ce])

        def attend_row(r, carry):
            q = q_ref[r]
            group = 8
            col = lax.broadcasted_iota(jnp.int32, (1, page * group), 1)
            keys, scores = [], []
            for g in range(refs // group):
                es = [entries[r, g * group + i] for i in range(group)]
                k = jnp.concatenate([pool[e >> 7] for e in es], axis=0)
                limit = jnp.zeros((1, page * group), jnp.int32)
                for i, e in enumerate(es):
                    limit = jnp.where((col >> 6) == i, e & 127, limit)
                s = lax.dot_general(q, k, (((1,), (1,)), ((), ())), preferred_element_type=F32) * SOFTMAX_SCALE
                scores.append(jnp.where((col & 63) < limit, s, LOW))
                keys.append(k)
            m = functools.reduce(jnp.maximum, [jnp.max(s, axis=1, keepdims=True) for s in scores])
            t = jnp.zeros((heads, 1), F32)
            o = jnp.zeros((heads, LATENT), F32)
            for s, k in zip(scores, keys):
                p = jnp.exp(s - m)
                t = t + jnp.sum(p, axis=1, keepdims=True)
                o = o + jnp.dot(p.astype(BF16), k[:, :LATENT], preferred_element_type=F32)
            some = m > 0.5 * LOW
            acc[r] = jnp.where(some, o, 0.0)
            top[r] = jnp.broadcast_to(m, (heads, 128))
            total[r] = jnp.broadcast_to(jnp.where(some, t, 0.0), (heads, 128))
            return carry

        for copy in weight_copies() + weight_places():
            copy.start()
        load_q = pltpu.make_async_copy(q_hbm, q_ref, pool_sems.at[9])
        load_q.start()
        second_hop(0)
        to_scalar.wait()
        load_q.wait()
        lax.fori_loop(0, 5, attend_row, 0)
        second_hop(1)
        second_hop(3)
        lax.fori_loop(5, 9, attend_row, 0)
        second_hop(2)
        lax.fori_loop(9, rows, attend_row, 0)

        block = 16
        whole = (valid == page).astype(F32)
        some = ((valid > 0) & (valid < page)).astype(F32)
        last = jnp.sum(some * valid.astype(F32), axis=1, keepdims=True)
        off = lax.broadcasted_iota(jnp.int32, (rows, page), 1).astype(F32)
        inside = (off < last).astype(F32)
        for i in range(0, moves, 2):
            pair = []
            for j in (i, i + 1):
                hit = (table[...] == slot_of[mine + j]).astype(F32)
                pair.append(
                    jnp.sum(hit * whole, axis=1, keepdims=True) + jnp.sum(hit * some, axis=1, keepdims=True) * inside
                )
            pair = jnp.concatenate(pair, axis=1)
            for r in range(rows):
                mult[r * block : (r + 1) * block, i * page : (i + 2) * page] = jnp.broadcast_to(
                    pair[r : r + 1], (block, 2 * page)
                )

        places = []
        for i in range(moves):
            again = 0
            for j in range(i):
                again = again + (src[0, mine + i] == src[0, mine + j]).astype(jnp.int32)
            places.append((src[0, mine + i], again))

        for copy in local:
            copy.wait()
        for copy in final.values():
            copy.wait_recv()
        while sent:
            sent.pop().wait_send()

        rope = width - LATENT
        for i, (rank, again) in enumerate(places):
            pair = inbox[rank]
            first = again == 0
            here = slice(i * page, (i + 1) * page)
            pages[here, :LATENT] = jnp.where(first, pair[:, :LATENT], pair[:, LATENT : 2 * LATENT])
            pages[here, LATENT:] = jnp.where(
                first, pair[:, 2 * LATENT : 2 * LATENT + rope], pair[:, 2 * LATENT + rope :]
            )

        size = rows * block
        to = lax.broadcasted_iota(jnp.int32, (size, size), 0)
        frm = lax.broadcasted_iota(jnp.int32, (size, size), 1)
        turn = (frm == (to % rows) * block + to // rows).astype(BF16)
        for n, a in enumerate(head_groups):
            xa = lax.rem(x + a, NX)
            hs = pl.ds(pl.multiple_of(xa * block, block), block)
            q = q_ref[:, hs, :].reshape(size, width)
            s = lax.dot_general(q, pages[...], (((1,), (1,)), ((), ())), preferred_element_type=F32) * SOFTMAX_SCALE
            times = mult[...]
            s = jnp.where(times > 0.0, s, LOW)
            old = top[:, hs, :].reshape(size, 128)[:, :1]
            m = jnp.maximum(old, jnp.max(s, axis=1, keepdims=True))
            shrink = jnp.exp(old - m)
            p = jnp.exp(s - m) * times
            t = total[:, hs, :].reshape(size, 128)[:, :1] * shrink + jnp.sum(p, axis=1, keepdims=True)
            o = acc[:, hs, :].reshape(size, LATENT) * shrink
            o = o + jnp.dot(p.astype(BF16), pages[:, :LATENT], preferred_element_type=F32)
            o = (o / jnp.where(t == 0.0, 1.0, t)).astype(BF16)
            o = jnp.dot(turn, o, preferred_element_type=F32).astype(BF16)
            packed[n] = o.reshape(NZ, -1, LATENT)
            for copy in latent_copies(n):
                copy.start()

    def rest(gus, ds, ho, part, mid, acc, hid):
        cols_all = part.shape[3]
        half = cols_all // 2
        ff = gate.shape[0]

        def step_to(dx, dz):
            return on(dx % NX, dz % NZ, 0)

        width = half // SUBS
        wing = width // 2
        order = [(h, s) for s in range(SUBS) for h in range(2)]

        row0 = pl.multiple_of(core * ff, 16)
        row1 = pl.multiple_of(2 * ff - row0 - ff, 16)
        loads = []
        w_copies = weight_copies()
        for k, copy in enumerate(w_copies[2:]):
            copy.wait_recv()
            own, other = ((gate, gate_2), (up, up_2), (down, down_2))[k]
            base = 640 if k == 1 else 0
            into = ds if k == 2 else gus
            loads.append(pltpu.make_async_copy(own, into.at[pl.ds(base + row0, ff), :], in_sems.at[2 * k]))
            loads.append(pltpu.make_async_copy(other, into.at[pl.ds(base + row1, ff), :], in_sems.at[2 * k + 1]))
        def weights_ready(*ks):
            for k in ks:
                loads[2 * k].wait()
                loads[2 * k + 1].wait()

        for copy in weight_places():
            copy.wait()
        for copy in w_copies[:2]:
            copy.wait_recv()
        sent.extend(w_copies)
        for n in range(4):
            for b, copy in zip((2, 1, 3, 0), latent_copies(n)):
                if (head_groups[n], b) == (0, 0):
                    copy.wait()
                else:
                    copy.wait_recv()
                    sent.append(copy)
        for h in range(4):
            l = rl[:, h * 16 : (h + 1) * 16, :].reshape(256, LATENT)
            ho[:, h * 128 : (h + 1) * 128] = jnp.dot(l, vus[h // 2, h % 2], preferred_element_type=F32).astype(BF16)

        def reduce_scatter(turn, fill, bufs, finish, after=None):
            r1, r2, t1, t2 = bufs

            def chunk(h, phase, i, base, size):
                cs = pl.ds(base, size)
                xi, zi = lax.rem(x + i + NX, NX), lax.rem(z + i + NZ, NZ)
                along_x = (h == 0) == (phase == 0)
                if phase == 0:
                    return part.at[xi, :, :, cs] if along_x else part.at[:, zi, :, cs]
                return part.at[xi, z, :, cs] if along_x else part.at[x, zi, :, cs]

            def to(h, phase, i):
                return step_to(i, 0) if (h == 0) == (phase == 0) else step_to(0, i)

            def sems(h, s, phase, k):
                at = (((turn * 2 + h) * SUBS + s) * 2 + phase) * 6 + k
                return rs_ss.at[at], rs_rs.at[at]

            def bufs_of(h, s, phase):
                first, second = (r1, r2) if phase == 0 else (t1, t2)
                return first.at[h, s], second.at[h, s]

            state = {}

            def start(h, s, phase, side):
                base = h * half + s * width + side * wing
                first, second = bufs_of(h, s, phase)
                step = 1 - 2 * side
                copies = state.setdefault((h, s, phase), {})
                copies[side] = send(
                    chunk(h, phase, 2, base, wing), first.at[side], *sems(h, s, phase, side), to(h, phase, step)
                )
                copies[3 - side] = send(
                    chunk(h, phase, -step, base, wing),
                    second.at[1 - side, ..., pl.ds(side * wing, wing)],
                    *sems(h, s, phase, 3 - side),
                    to(h, phase, -step),
                )

            def middle(h, s, phase):
                base = h * half + s * width
                first, second = bufs_of(h, s, phase)
                copies = state[h, s, phase]
                for side, (i, at) in enumerate(((1, 0), (-1, wing))):
                    copies[side].wait_recv()
                    mine = chunk(h, phase, i, base + at, wing)
                    mine[...] = (mine[...].astype(F32) + first[side].astype(F32)).astype(BF16)
                    copies[4 + side] = send(
                        mine, second.at[side, ..., pl.ds(at, wing)], *sems(h, s, phase, 4 + side), to(h, phase, i)
                    )

            def total(h, s, phase):
                base = h * half + s * width
                _, second = bufs_of(h, s, phase)
                for k in range(2, 6):
                    state[h, s, phase][k].wait_recv()
                mine = chunk(h, phase, 0, base, width)
                value = mine[...].astype(F32) + second[0].astype(F32) + second[1].astype(F32)
                if phase == 0:
                    mine[...] = value.astype(BF16)
                else:
                    finish(base, width, value)

            for s in range(SUBS):
                for side in range(2):
                    for h in range(2):
                        fill(h * half + s * width + side * wing, wing)
                        start(h, s, 0, side)
            if turn == 0:
                gus[pl.ds(2 * ff, 640 - 2 * ff), :] = jnp.zeros((640 - 2 * ff, cols_all), BF16)
                gus[pl.ds(640 + 2 * ff, 640 - 2 * ff), :] = jnp.zeros((640 - 2 * ff, cols_all), BF16)
            for h, s in order:
                middle(h, s, 0)
            if turn == 0:
                for copy in loads[:4]:
                    copy.start()
            for h, s in order:
                total(h, s, 0)
                start(h, s, 1, 0)
                start(h, s, 1, 1)
            for h, s in order:
                middle(h, s, 1)
            for h, s in order:
                total(h, s, 1)
                if after is not None and h == 1:
                    after(s)


        def fill_out(base, size):
            cs = pl.ds(base, size)
            v = jnp.dot(ho[:, :256], wos[0, :, cs], preferred_element_type=F32)
            v = v + jnp.dot(ho[:, 256:], wos[1, :, cs], preferred_element_type=F32)
            part[:, :, :, cs] = v.astype(BF16).reshape(NX, NZ, 16, size)

        squares = []

        def finish_out(base, size, value):
            cs = pl.ds(base, size)
            m = res[:, cs].astype(F32) + value
            mid[:, cs] = m
            squares.append(jnp.sum(m * m, axis=1, keepdims=True))
            nrm[x, z, :, cs] = (m * gain[:, cs]).astype(BF16)

        def block(h, s, i, j, piece):
            base = h * half + s * width
            rest = wing + (128 if (h, s) == (1, SUBS - 1) else 0)
            lo, size = {"all": (0, wing + rest), "low": (0, wing), "high": (wing, rest)}[piece]
            dx, dz = (j, i) if h == 0 else (i, j)
            return nrm.at[lax.rem(x + dx + NX, NX), lax.rem(z + dz + NZ, NZ), :, pl.ds(base + lo, size)]

        one, two = {}, {}

        def pass_on(h, s, i, j, piece, k, first, step):
            ref = block(h, s, i, j, piece)
            at = (h * SUBS + s) * 20 + k
            to = step_to(0, step) if (h == 0) == first else step_to(step, 0)
            return send(ref, ref, ag_ss.at[at], ag_rs.at[at], to)

        def spread(h, s, n, i):
            two[h, s, n] = [pass_on(h, s, i, 0, "all", 4 + 4 * n, False, 1), pass_on(h, s, i, 0, "all", 5 + 4 * n, False, -1)]

        def forward(s, n, i):
            for h in range(2):
                got = two[h, s, n]
                got[0].wait_recv()
                got.append(pass_on(h, s, i, -1, "low", 6 + 4 * n, False, 1))
                got[1].wait_recv()
                got.append(pass_on(h, s, i, 1, "high", 7 + 4 * n, False, -1))

        def gather_start(s):
            if s == SUBS - 1:
                scale = lax.rsqrt(sum(squares) / cols_all + 1e-06)
                rough = scale.astype(BF16).astype(F32)
                lane = lax.broadcasted_iota(jnp.int32, (16, 128), 1)
                nrm[x, z, :, cols_all:] = jnp.where(lane < 64, rough, scale - rough).astype(BF16)
            for h in range(2):
                one[h, s] = [pass_on(h, s, 0, 0, "all", 0, True, 1), pass_on(h, s, 0, 0, "all", 1, True, -1)]
            for h in range(2):
                spread(h, s, 0, 0)

        def gather_next(s):
            for h in range(2):
                got = one[h, s]
                got[0].wait_recv()
                got.append(pass_on(h, s, -1, 0, "low", 2, True, 1))
                got[1].wait_recv()
                got.append(pass_on(h, s, 1, 0, "high", 3, True, -1))
                spread(h, s, 1, -1)
                spread(h, s, 2, 1)

        def gather_last(s):
            for h in range(2):
                one[h, s][2].wait_recv()
                one[h, s][3].wait_recv()
                spread(h, s, 3, 2)

        def gathered(h, s):
            for n in range(4):
                two[h, s, n][2].wait_recv()
                two[h, s, n][3].wait_recv()

        def up_step(h, s):
            cs = pl.ds(h * half + s * width, width)
            v = lax.dot_general(
                nrm[:, :, :, cs].reshape(256, width), gus[:, cs], (((1,), (1,)), ((), ())), preferred_element_type=F32
            )
            if (h, s) == (0, 0):
                acc[...] = v
            else:
                acc[...] += v

        reduce_scatter(0, fill_out, (b1, b2, c1, c2), finish_out, gather_start)
        gather_next(0)
        gather_next(1)
        forward(0, 0, 0)
        gather_last(0)
        forward(1, 0, 0)
        gather_last(1)
        for copy in loads[4:]:
            copy.start()
        forward(0, 1, -1)
        forward(0, 2, 1)
        forward(1, 1, -1)
        forward(0, 3, 2)
        forward(1, 2, 1)
        forward(1, 3, 2)
        weights_ready(0, 1)
        for s in range(SUBS):
            for h in range(2):
                gathered(h, s)
                up_step(h, s)
        scales = nrm[:, :, :, cols_all:].reshape(256, 128).astype(F32)
        scale = scales[:, :1] + scales[:, 64:65]
        g = acc[:, :640] * scale
        hid[...] = (g / (1.0 + jnp.exp(-g)) * (acc[:, 640:] * scale)).astype(BF16)
        while sent:
            sent.pop().wait_send()
        weights_ready(2)

        def fill_down(base, size):
            cs = pl.ds(base, size)
            v = jnp.dot(hid[:, : 2 * ff], ds[:, cs], preferred_element_type=F32)
            part[:, :, :, cs] = v.astype(BF16).reshape(NX, NZ, 16, size)

        def finish_down(base, size, value):
            cs = pl.ds(base, size)
            out_ref[:, cs] = (mid[:, cs] + value).astype(BF16)

        reduce_scatter(1, fill_down, (b1, b2, c1, c2), finish_down)
        while sent:
            sent.pop().wait_send()


    vmem = pltpu.VMEM
    cols, ff = res.shape[1], gate.shape[0]
    pl.run_scoped(
        attention,
        vmem(pool_hbm.shape, BF16),
        vmem((2, NX * NZ * 2, page // 2, 2 * width), BF16),
        vmem((moves * page, width), BF16),
        vmem((rows * 16, moves * page), F32),
        vmem((rows, heads, LATENT), F32),
        vmem((rows, heads, 128), F32),
        vmem((rows, heads, 128), F32),
        vmem(q_hbm.shape, BF16),
    )
    pl.run_scoped(
        rest,
        vmem((1280, cols), BF16),
        vmem((2 * ff, cols), BF16),
        vmem((256, 512), BF16),
        vmem((NX, NZ, 16, cols), BF16),
        vmem((16, cols), F32),
        vmem((256, 1280), F32),
        vmem((256, 640), BF16),
    )


def layer(src, page_of, slot_of, rc, lens, table, queries, pool, vu, wo, res, gain, gate, up, down):
    rows, heads, width = queries.shape
    page = pool.shape[1]
    ranks = NX * NZ * 2
    cols = res.shape[1]
    block = cols // 2 // SUBS
    n_rs = 2 * 2 * SUBS * 2 * 6
    dma, vmem = pltpu.SemaphoreType.DMA, pltpu.VMEM
    out, _, _, _ = pl.pallas_call(
        layer_kernel,
        out_shape=tuple(jax.ShapeDtypeStruct(a.shape, BF16) for a in (res, gate, up, down)),
        in_specs=[sspec()] * 5 + [vspec()] + [aspec()] * 4 + [vspec()] * 2 + [aspec()] * 3,
        out_specs=(vspec(), aspec(), aspec(), aspec()),
        scratch_shapes=[
            vmem((2, 3, 8, page // 2, 2 * width), BF16),
            vmem((ranks, page, 2 * width), BF16),
            vmem((NX * NZ, rows * heads // (NX * NZ), LATENT), BF16),
            vmem((NX, NZ, 16, cols + 128), BF16),
            vmem((2,) + vu.shape, BF16),
            vmem((2,) + wo.shape, BF16),
            vmem((4, NZ, rows * heads // (NX * NZ), LATENT), BF16),
            vmem((rows, 128), jnp.int32),
            pltpu.SMEM((rows, 128), jnp.int32),
            vmem((2, SUBS, 2, 4, 16, block // 2), BF16),
            vmem((2, SUBS, 2, 4, 16, block), BF16),
            vmem((2, SUBS, 2, 16, block // 2), BF16),
            vmem((2, SUBS, 2, 16, block), BF16),
            dma((10,)),
            dma((8,)),
            dma((15,)),
            dma((15,)),
            dma((64,)),
            dma((64,)),
            dma((2,)),
            dma((5,)),
            dma((5,)),
            dma((16,)),
            dma((16,)),
            dma((6,)),
            dma((n_rs,)),
            dma((n_rs,)),
            dma((40 * SUBS,)),
            dma((40 * SUBS,)),
        ],
        compiler_params=pltpu.CompilerParams(collective_id=0, has_side_effects=True, vmem_limit_bytes=VMEM_LIMIT),
        name="layer",
    )(src, page_of, slot_of, rc, lens, table, queries, pool, vu, wo, res, gain, gate, up, down)
    return out


def body(
    page_pool,
    move_source,
    move_page,
    move_slot,
    row_count,
    lengths,
    page_table,
    queries,
    value_up,
    out_proj,
    residual,
    norm_gain,
    gate_proj,
    up_proj,
    down_proj,
):
    return layer(
        move_source.reshape(1, -1), move_page, move_slot, row_count, lengths, page_table, queries, page_pool,
        value_up, out_proj, residual, norm_gain.reshape(1, -1), gate_proj.T, up_proj.T, down_proj,
    )


def solution(mesh):
    in_specs = (
        P(("rep", "dp"), None, None),
        P("rep", None),
        P("rep"),
        P("rep"),
        P(("rep", "dp")),
        P(("rep", "dp")),
        P(("rep", "dp"), None),
        P(("rep", "dp"), None, None),
        P("dp", None, None),
        P("dp", None),
        P(("rep", "dp"), None),
        P(),
        P(None, "dp"),
        P(None, "dp"),
        P("dp", None),
    )
    out_specs = P(("rep", "dp"), None)
    return jax.shard_map(body, mesh=mesh, in_specs=in_specs, out_specs=out_specs, check_vma=False)
```
